32 devices in a mesh: tensor: 2 (over core), req: 4 (over z), seq: 4 (over y, x).
Axes of the slice: x: 2, y: 2, z: 4, core: 2. Of those that a mesh axis runs over, the one named last changes fastest.
Arguments:
- incoming_activations: bfloat16 [8, 1024, 4096], P('req', 'seq'), may hold values from -6 to 6
- standardize_scaling: float32 [4096], replicated, may hold values from 0.1 to 1.9
- lagged_blending_weights: float32 [4, 4096], replicated, may hold values from 0 to 1
- learner_line_permutation: int32 [4096], replicated, may hold values from 0 to 4095, each once
- learner_acceptor_lookup_slices: float32 [3, 4096, 2048], P(None, ('req', 'seq'), 'tensor'), may hold values from -0.09375 to 0.09375
- learner_projection_slices: float32 [2048, 4096], P('tensor', ('req', 'seq')), may hold values from -0.125 to 0.125
- fading_left_matrix: bfloat16 [4096, 128], replicated, may hold values from -0.09375 to 0.09375
- fading_right_matrix: bfloat16 [128, 2048], P(None, 'tensor'), may hold values from -0.5 to 0.5
- feature_fading_speed: float32 [2048], P('tensor'), may hold values from 0.0002 to 0.08
- self_reward: float32 [2048], P('tensor'), may hold values from -3 to 3
- cluster_scaling_vector: float32 [2048], P('tensor'), may hold values from 0.1 to 1.9
- prompt_extents: int32 [8], P('req'), may hold values from 128 to 1024, as said below
Outputs:
- hidden_out: bfloat16 [8, 1024, 4096], P('req', 'seq', 'tensor')
- stretch_states: float32 [8, 4, 32, 4096], P('req', 'seq', 'tensor')
The draws below stay inside these ranges and needn't reach their ends.
Inputs may be any that keep to these rules, and one draw needn't show every extreme that they name: `prompt_extents`: it counts the valid tokens of each prompt from its start; prompt 0 is always full. learner_line_permutation names each of the 4096 input rows once.
All inputs are finite; a program needn't handle non-finite values.
Results may differ from the reference program's by a relative error of at most 0.013.
Values may be sent and summed in bfloat16 or wider, within the bound.
No kernel may reach another device: no remote copies, remote signals or barrier semaphores. Data moves between devices by JAX's collectives and lax.ppermute only.
A program may use at most 192 MiB of HBM per device.

```python
import math
import jax
import jax.numpy as jnp
from jax import lax

MODEL_WIDTH = 4096
ATTEND_DIM = 64
MIDDLE_COUNT = 32
DECAY_INNER = 128
CH = 256
LEN = 1024
REQS = 8
STRETCHES = 4
ATTEND_FEATURES = 2048
N_TENSOR = 2


def draw_prompt_extents(key, part):
    drawn = jax.random.randint(key, (REQS,), LEN // 8, LEN + 1)
    return drawn.at[0].set(LEN).astype(jnp.int32)


def block_scale(stream_key, dims, split, low, largest):
    level, own = 1.0, jax.random.fold_in(stream_key, 6)
    for position, parts in split:
        draws = jnp.exp(jax.random.uniform(jax.random.fold_in(own, position), (parts,), jnp.float32, low / len(split), largest / len(split)))
        level = level * jnp.repeat(draws, dims[position] // parts).reshape([-1 if axis == position else 1 for axis in range(len(dims))])
    return level


def bell_draw(rng, shape, deviation, most, cuts=(), kind=jnp.bfloat16):
    entries = jax.random.normal(rng, shape, jnp.float32) * deviation
    if len(cuts) > 0:
        entries = block_scale(rng, shape, cuts, -0.22, 0.18) * entries
    return jnp.clip(entries, min=-most, max=most).astype(kind)


def setup_inputs(seed: int = 0) -> dict:
    key_list = jax.random.split(jax.random.key(seed), 13)
    return {
        "incoming_activations": bell_draw(key_list[0], (REQS, LEN, MODEL_WIDTH), 1.0, 6.0, ((0, 4), (1, 4))),
        "standardize_scaling": jnp.clip(1.0 + 0.18 * jax.random.normal(key_list[1], (MODEL_WIDTH,), jnp.float32), 0.1, 1.9),
        "lagged_blending_weights": jnp.clip(jax.random.uniform(key_list[2], (4, MODEL_WIDTH), jnp.float32, 0.0, 1.0), 0.0, 1.0),
        "learner_line_permutation": jax.random.permutation(key_list[3], MODEL_WIDTH).astype(jnp.int32),
        "learner_acceptor_lookup_slices": bell_draw(key_list[4], (3, MODEL_WIDTH, ATTEND_FEATURES), MODEL_WIDTH ** -0.5, 0.09375, ((1, 16), (2, 2)), jnp.float32),
        "learner_projection_slices": bell_draw(key_list[5], (ATTEND_FEATURES, MODEL_WIDTH), ATTEND_FEATURES ** -0.5, 0.125, ((0, 2), (1, 16)), jnp.float32),
        "fading_left_matrix": bell_draw(key_list[6], (MODEL_WIDTH, DECAY_INNER), MODEL_WIDTH ** -0.5, 0.09375),
        "fading_right_matrix": bell_draw(key_list[7], (DECAY_INNER, ATTEND_FEATURES), DECAY_INNER ** -0.5, 0.5, ((1, 2),)),
        "feature_fading_speed": jnp.clip(jnp.exp(math.log(0.08) - 5.9914646 * jax.random.uniform(key_list[8], (ATTEND_FEATURES,), jnp.float32) ** block_scale(key_list[8], (ATTEND_FEATURES,), ((0, 2),), -0.2, 0.2)), 0.0002, 0.08),
        "self_reward": bell_draw(key_list[9], (ATTEND_FEATURES,), 1.0, 3.0, ((0, 2),), jnp.float32),
        "cluster_scaling_vector": jnp.clip(1.0 + 0.18 * jax.random.normal(key_list[10], (ATTEND_FEATURES,), jnp.float32), 0.1, 1.9),
        "prompt_extents": draw_prompt_extents(jax.random.fold_in(key_list[12], 71), 0),
    }


eps = 1e-05

def layer_norm(values, gain):
    mean = lax.optimization_barrier(jnp.mean(values, axis=-1, keepdims=True))
    centred = values - mean
    spread = lax.optimization_barrier(jnp.mean(centred * centred, axis=-1, keepdims=True))
    return centred * lax.rsqrt(spread + eps) * gain

def reference(incoming_activations, standardize_scaling, lagged_blending_weights, learner_line_permutation, learner_acceptor_lookup_slices, learner_projection_slices, fading_left_matrix, fading_right_matrix, feature_fading_speed, self_reward, cluster_scaling_vector, prompt_extents):
    current = layer_norm(incoming_activations.astype(jnp.float32), standardize_scaling)
    previous = jnp.concatenate([jnp.zeros_like(current[:, :1]), current[:, :-1]], axis=1)
    delta = previous - current
    shift_mixed = [(current + delta * lagged_blending_weights[j]).astype(jnp.bfloat16) for j in range(4)]
    valid_mask = (jnp.arange(LEN, dtype=jnp.int32)[None, :] < prompt_extents[:, None]).astype(jnp.float32)[..., None]
    stored = []
    for j in range(3):
        weight = learner_acceptor_lookup_slices[j].astype(jnp.bfloat16)
        product = jnp.dot(shift_mixed[j][..., learner_line_permutation], weight, preferred_element_type=jnp.float32)
        stored.append(lax.optimization_barrier(product.astype(jnp.bfloat16)).astype(jnp.float32))
    receptance = stored[0]
    keys = stored[1] * valid_mask
    values = stored[2]
    decay_lowrank = jnp.tanh(jnp.dot(shift_mixed[3], fading_left_matrix, preferred_element_type=jnp.float32)).astype(jnp.bfloat16)
    decay_logarithm = -feature_fading_speed * jnp.exp(jnp.dot(decay_lowrank, fading_right_matrix, preferred_element_type=jnp.float32)) * valid_mask

    def heads_first(array):
        return jnp.transpose(array.reshape(REQS, LEN, MIDDLE_COUNT, ATTEND_DIM), (1, 0, 2, 3))
    seq_r = heads_first(receptance)
    seq_k = heads_first(keys)
    seq_v = heads_first(values)
    seq_w = heads_first(decay_logarithm)
    attender_reward = self_reward.reshape(MIDDLE_COUNT, ATTEND_DIM)

    def advance(carried_memory, items):
        acceptor_moment, k_t, v_t, w_t = items
        tensor_dyad = k_t[..., :, None] * v_t[..., None, :]
        sublevel_result = jnp.einsum('zhb,zhbs->zhs', acceptor_moment, carried_memory + attender_reward[None, :, :, None] * tensor_dyad, precision=lax.Precision.HIGHEST)
        carried_memory = jnp.exp(w_t)[..., None] * carried_memory + tensor_dyad
        return (carried_memory, sublevel_result)
    carried_memory = jnp.zeros((REQS, MIDDLE_COUNT, ATTEND_DIM, ATTEND_DIM), jnp.float32)
    pieces = []
    saved = []
    for block in range(STRETCHES):
        lo = block * CH
        carried_memory, sublevel_result = lax.scan(advance, carried_memory, (seq_r[lo:lo + CH], seq_k[lo:lo + CH], seq_v[lo:lo + CH], seq_w[lo:lo + CH]))
        pieces.append(sublevel_result)
        saved.append(carried_memory.reshape(REQS, MIDDLE_COUNT, ATTEND_DIM * ATTEND_DIM))
    y_all = jnp.transpose(jnp.concatenate(pieces, axis=0), (1, 0, 2, 3))
    stretch_states = jnp.stack(saved, axis=1)
    mean = lax.optimization_barrier(jnp.mean(y_all, axis=-1, keepdims=True))
    centred = y_all - mean
    spread = lax.optimization_barrier(jnp.mean(centred * centred, axis=-1, keepdims=True))
    normed = centred * lax.rsqrt(spread + eps) * cluster_scaling_vector.reshape(MIDDLE_COUNT, ATTEND_DIM)
    normed = (normed.reshape(REQS, LEN, ATTEND_FEATURES) * valid_mask).astype(jnp.bfloat16)
    out_weight = learner_projection_slices.astype(jnp.bfloat16)
    group = ATTEND_FEATURES // N_TENSOR
    total = jnp.zeros((REQS, LEN, MODEL_WIDTH), jnp.float32)
    for g in range(N_TENSOR):
        part = jnp.dot(normed[..., g * group:(g + 1) * group], out_weight[g * group:(g + 1) * group], preferred_element_type=jnp.float32)
        total = total + lax.optimization_barrier(part.astype(jnp.bfloat16)).astype(jnp.float32)
    hidden_out = (incoming_activations.astype(jnp.float32) + total).astype(jnp.bfloat16)
    return (hidden_out, stretch_states)
```

```python
import functools

import jax
import jax.numpy as jnp
import numpy as np
from jax import lax
from jax.experimental import pallas as pl
from jax.experimental.pallas import tpu as pltpu
from jax.sharding import PartitionSpec as P

ATTEND_DIM = 64
CHUNK = 64
LEVELS = 6
PREFIX = 8

eps = 1e-05
bf16 = jnp.bfloat16
f32 = jnp.float32


def dot(a, b):
    return jnp.dot(a, b, preferred_element_type=f32)


def dot_nt(a, b):
    return lax.dot_general(a, b, (((1,), (1,)), ((), ())), preferred_element_type=f32)


def dot_tn(a, b):
    return lax.dot_general(a, b, (((0,), (0,)), ((), ())), preferred_element_type=f32)


def swapped(value, axis, by):
    peers = lax.axis_size(axis)
    return lax.ppermute(value, axis, [(i, i ^ by) for i in range(peers)])


def vmem(mib):
    return pltpu.CompilerParams(vmem_limit_bytes=mib * 2**20)


def order_kernel(x_ref, gain_ref, coeff_ref, perm_ref, out_ref, coeff_out_ref, cur_ref):
    rows, width = x_ref.shape
    block = out_ref.shape[1]
    depth = 256

    @pl.when(pl.program_id(0) == 0)
    def _():
        x = x_ref[...].astype(f32)
        mean = jnp.mean(x, axis=-1, keepdims=True)
        centred = x - mean
        spread = jnp.mean(centred * centred, axis=-1, keepdims=True)
        cur_ref[:rows, :] = (centred * lax.rsqrt(spread + eps) * gain_ref[...]).astype(bf16)
        c = coeff_ref[...]
        high = c.astype(bf16)
        cur_ref[rows:, :] = jnp.concatenate([high, (c - high.astype(f32)).astype(bf16)], axis=0)

    perm = perm_ref[...]
    total = jnp.zeros((rows + 2 * PREFIX, block), f32)
    for k in range(width // depth):
        lines = lax.broadcasted_iota(jnp.int32, (depth, block), 0) + k * depth
        chosen = jnp.where(lines == perm, 1.0, 0.0).astype(bf16)
        total += dot(cur_ref[:, k * depth : (k + 1) * depth], chosen)
    out_ref[...] = total[:rows].astype(bf16)
    coeff_out_ref[...] = total[rows : rows + PREFIX] + total[rows + PREFIX :]


def ordered(x, gain, coeffs, perm):
    rows, width = x.shape
    block = 512
    return pl.pallas_call(
        order_kernel,
        grid=(width // block,),
        in_specs=[
            pl.BlockSpec((rows, width), lambda n: (0, 0)),
            pl.BlockSpec((1, width), lambda n: (0, 0)),
            pl.BlockSpec((PREFIX, width), lambda n: (0, 0)),
            pl.BlockSpec((1, block), lambda n: (0, n)),
        ],
        out_specs=[
            pl.BlockSpec((rows, block), lambda n: (0, n)),
            pl.BlockSpec((PREFIX, block), lambda n: (0, n)),
        ],
        out_shape=[
            jax.ShapeDtypeStruct((rows, width), bf16),
            jax.ShapeDtypeStruct((PREFIX, width), f32),
        ],
        scratch_shapes=[pltpu.VMEM((rows + 2 * PREFIX, width), bf16)],
        compiler_params=vmem(40),
        cost_estimate=pl.CostEstimate(
            flops=2 * rows * width * width, bytes_accessed=4 * rows * width, transcendentals=0
        ),
    )(x, gain, coeffs, perm)


def mix_kernel(where_ref, act_ref, before_ref, coeff_ref, left_ref, mixed_ref, lora_ref):
    rows, width = act_ref.shape[2:]
    block = 512
    first = (pl.program_id(1) == 0) & (pl.program_id(2) == 0)
    inner = jnp.zeros((rows, left_ref.shape[1]), f32)
    top = lax.broadcasted_iota(jnp.int32, (rows, block), 0) == 0
    for n in range(width // block):
        cols = slice(n * block, (n + 1) * block)
        cur = act_ref[0, 0, :, cols].astype(f32)
        last = before_ref[0, 0, :, cols].astype(f32)[15:16]
        last = jnp.where(first, jnp.zeros_like(last), last)
        delta = jnp.where(top, last, pltpu.roll(cur, 1, 0)) - cur
        for j in range(3):
            mixed_ref[j, 0, 0, :, cols] = (cur + delta * coeff_ref[j : j + 1, cols]).astype(bf16)
        inner += dot((cur + delta * coeff_ref[3:4, cols]).astype(bf16), left_ref[cols, :])
    lora_ref[0, 0] = jnp.tanh(inner).astype(bf16)


def shifted(where, act, coeffs, left):
    stretches, prompts, span, width = act.shape
    inner = left.shape[1]
    rows = 128
    tiles = span // rows
    groups = rows // 16

    def before(p, b, i, where):
        block = jnp.where(i == 0, jnp.maximum(b - 1, 0), b)
        return (block ^ where[0], p, jnp.where(i == 0, tiles, i) * groups - 1, 0)

    return pl.pallas_call(
        mix_kernel,
        grid_spec=pltpu.PrefetchScalarGridSpec(
            num_scalar_prefetch=1,
            grid=(prompts, stretches, tiles),
            in_specs=[
                pl.BlockSpec((1, 1, rows, width), lambda p, b, i, w: (b ^ w[0], p, i, 0)),
                pl.BlockSpec((1, 1, 16, width), before),
                pl.BlockSpec((PREFIX, width), lambda p, b, i, w: (0, 0)),
                pl.BlockSpec((width, inner), lambda p, b, i, w: (0, 0)),
            ],
            out_specs=[
                pl.BlockSpec((3, 1, 1, rows, width), lambda p, b, i, w: (0, p, b, i, 0)),
                pl.BlockSpec((1, 1, rows, inner), lambda p, b, i, w: (p, b, i, 0)),
            ],
        ),
        out_shape=[
            jax.ShapeDtypeStruct((3, prompts, stretches, span, width), bf16),
            jax.ShapeDtypeStruct((prompts, stretches, span, inner), bf16),
        ],
        compiler_params=vmem(40),
        cost_estimate=pl.CostEstimate(
            flops=24 * act.size, bytes_accessed=8 * act.size, transcendentals=0
        ),
    )(where, act, act, coeffs, left)


def project_kernel(where_ref, act_ref, *refs):
    *weights, out_ref, total_ref = refs
    depth = weights[0].shape[2]
    r = pl.program_id(1)

    @pl.when(r == 0)
    def _():
        total_ref[...] = jnp.zeros_like(total_ref)

    for d, w_ref in enumerate(weights):
        cols = pl.ds(pl.multiple_of((where_ref[0] ^ d) * depth, depth), depth)
        total_ref[...] += dot(act_ref[0, :, cols], w_ref[0, 0])

    @pl.when(r == pl.num_programs(1) - 1)
    def _():
        out_ref[0] = total_ref[...].astype(bf16)


def projected(where, mixed, weights):
    reqs, kinds, depth, cols = weights[0].shape
    tokens, width = mixed.shape[1:]
    stretches = len(weights)
    if depth % 128:
        order = jnp.arange(stretches) ^ where[0]
        lines = jnp.stack(weights)[order]
        lines = jnp.transpose(lines, (2, 1, 0, 3, 4)).reshape(kinds, width, cols)
        return jnp.einsum("jtk,jkc->jtc", mixed, lines, preferred_element_type=f32).astype(bf16)
    share = stretches * depth
    return pl.pallas_call(
        project_kernel,
        grid_spec=pltpu.PrefetchScalarGridSpec(
            num_scalar_prefetch=1,
            grid=(kinds, reqs),
            in_specs=[pl.BlockSpec((1, tokens, share), lambda j, r, w: (j, 0, r))]
            + [pl.BlockSpec((1, 1, depth, cols), lambda j, r, w: (r, j, 0, 0))] * stretches,
            out_specs=pl.BlockSpec((1, tokens, cols), lambda j, r, w: (j, 0, 0)),
            scratch_shapes=[pltpu.VMEM((tokens, cols), f32)],
        ),
        out_shape=jax.ShapeDtypeStruct((kinds, tokens, cols), bf16),
        compiler_params=vmem(40),
        cost_estimate=pl.CostEstimate(
            flops=2 * kinds * tokens * width * cols,
            bytes_accessed=2 * (mixed.size + kinds * width * cols),
            transcendentals=0,
        ),
    )(where, mixed, *weights)


def decay_sums():
    place = np.arange(CHUNK)
    of, by = place[:, None], place[None, :]
    parts = []
    for level in range(LEVELS):
        half = 1 << level
        middle = (of // (2 * half)) * 2 * half + half - 1
        later = (of % (2 * half)) >= half
        parts.append(np.where(later, (by > middle) & (by < of), (by > of) & (by <= middle)))
    parts += [by < of, by > of, np.ones((8, CHUNK), bool)]
    sums = np.concatenate(parts).astype(np.float32)
    return np.concatenate([sums, sums], axis=1)


def pair_levels(heads):
    of, by = np.arange(CHUNK)[:, None], np.arange(CHUNK)[None, :]
    level = np.full((CHUNK, CHUNK), -1.0, np.float32)
    for bit in range(LEVELS):
        level[((of ^ by) >> bit) == 1] = bit
    return np.tile(np.where(of > by, level, -1.0).astype(np.float32), (1, heads))


def wkv_kernel(
    extent_ref, where_ref, own_ref, own_lora_ref, far_ref, far_lora_ref, right_ref, speed_ref, reward_ref,
    scale_ref, sums_ref, level_ref, same_ref, normed_ref, state_ref, memory_ref,
):
    chunk = pl.program_id(0)
    prompts = own_ref.shape[1]
    cols = own_ref.shape[3]
    heads = cols // ATTEND_DIM
    per_block = pl.num_programs(0) // lax.axis_size("seq")
    same = same_ref[...]
    same_f32 = same.astype(f32)
    level = level_ref[...]
    at = chunk * CHUNK + lax.broadcasted_iota(jnp.int32, (CHUNK, cols), 0)

    @pl.when(chunk == 0)
    def _():
        memory_ref[...] = jnp.zeros_like(memory_ref)

    for side, (proj_ref, lora_ref) in enumerate(((own_ref, own_lora_ref), (far_ref, far_lora_ref))):
        for p in range(prompts):
            prompt = (where_ref[1] ^ side) * prompts + p
            valid = jnp.where(at < extent_ref[prompt], 1.0, 0.0)
            r = proj_ref[0, p].astype(f32)
            k = proj_ref[1, p].astype(f32) * valid
            v = proj_ref[2, p]
            decay = -speed_ref[...] * jnp.exp(dot(lora_ref[p], right_ref[...])) * valid
            high = decay.astype(bf16)
            low = (decay - high.astype(f32)).astype(bf16)
            kept = jnp.exp(dot(sums_ref[...], jnp.concatenate([high, low], axis=0)))
            scores = jnp.zeros((CHUNK, heads * CHUNK), f32)
            for bit in range(LEVELS):
                part = kept[bit * CHUNK : (bit + 1) * CHUNK]
                lookup = (k * part).astype(bf16)
                lookup = jnp.concatenate([lookup] * heads, axis=0) * same
                found = dot_nt((r * part).astype(bf16), lookup)
                scores = jnp.where(level == bit, found, scores)
            v_heads = jnp.concatenate([v] * heads, axis=0) * same
            memory = memory_ref[side * prompts + p]
            from_start = (r * kept[LEVELS * CHUNK : (LEVELS + 1) * CHUNK]).astype(bf16)
            to_end = (k * kept[(LEVELS + 1) * CHUNK : (LEVELS + 2) * CHUNK]).astype(bf16)
            own = dot((r * reward_ref[...] * k).astype(bf16), same)
            y = dot_nt(from_start, memory.astype(bf16)) + dot(scores.astype(bf16), v_heads)
            y += own * v.astype(f32)
            whole = kept[(LEVELS + 2) * CHUNK : (LEVELS + 2) * CHUNK + 1]
            memory = memory * whole + same_f32 * dot_tn(v, to_end)
            memory_ref[side * prompts + p] = memory

            y_high = y.astype(bf16)
            y_low = (y - y_high.astype(f32)).astype(bf16)
            centred = y - (dot(y_high, same) + dot(y_low, same)) * (1.0 / ATTEND_DIM)
            spread = dot((centred * centred).astype(bf16), same) * (1.0 / ATTEND_DIM)
            normed = centred * lax.rsqrt(spread + eps) * scale_ref[...] * valid
            normed_ref[0, pl.ds(prompt, 1)] = normed.astype(bf16)[None]

            @pl.when(chunk % per_block == per_block - 1)
            def _():
                folded = memory[:ATTEND_DIM]
                for h in range(1, heads):
                    folded += memory[h * ATTEND_DIM : (h + 1) * ATTEND_DIM]
                state_ref[0, pl.ds(prompt, 1)] = folded[None]


def recurrence(extents, where, own, own_lora, far, far_lora, right, speed, reward, scale, stretches, span):
    _, prompts, length, cols = own.shape
    inner = own_lora.shape[-1]
    heads = cols // ATTEND_DIM
    reqs = 2 * prompts
    per_block = span // CHUNK
    sums = jnp.asarray(decay_sums(), bf16)
    level = jnp.asarray(pair_levels(heads), f32)
    head = np.arange(cols) // ATTEND_DIM
    same = jnp.asarray(head[:, None] == head[None, :], bf16)

    def fixed(array):
        return pl.BlockSpec(array.shape, lambda c, e, w: (0,) * array.ndim)

    proj_spec = pl.BlockSpec((3, prompts, CHUNK, cols), lambda c, e, w: (0, 0, c, 0))
    lora_spec = pl.BlockSpec((prompts, CHUNK, inner), lambda c, e, w: (0, c, 0))
    tables = (right, speed, reward, scale, sums, level, same)
    return pl.pallas_call(
        wkv_kernel,
        grid_spec=pltpu.PrefetchScalarGridSpec(
            num_scalar_prefetch=2,
            grid=(length // CHUNK,),
            in_specs=[proj_spec, lora_spec, proj_spec, lora_spec] + [fixed(a) for a in tables],
            out_specs=[
                pl.BlockSpec(
                    (1, reqs, CHUNK, cols), lambda c, e, w: (c // per_block, 0, c % per_block, 0)
                ),
                pl.BlockSpec(
                    (1, reqs, ATTEND_DIM, cols), lambda c, e, w: (c // per_block, 0, 0, 0)
                ),
            ],
            scratch_shapes=[pltpu.VMEM((reqs, cols, cols), f32)],
        ),
        out_shape=[
            jax.ShapeDtypeStruct((stretches, reqs, span, cols), bf16),
            jax.ShapeDtypeStruct((stretches, reqs, ATTEND_DIM, cols), f32),
        ],
        compiler_params=vmem(40),
        cost_estimate=pl.CostEstimate(
            flops=reqs * length * cols * 8000, bytes_accessed=20 * length * cols, transcendentals=0
        ),
    )(extents, where, own, own_lora, far, far_lora, *tables)


def finish_kernel(where_ref, x_ref, own_ref, far_ref, *refs):
    *weights, out_ref = refs
    stretches, rows, cols = own_ref.shape
    chunk = weights[0].shape[-1]
    for e in range(stretches):
        total = x_ref[:, pl.ds(pl.multiple_of((where_ref[0] ^ e) * chunk, chunk), chunk)].astype(f32)
        for side, lines_ref in enumerate((own_ref, far_ref)):
            w_ref = weights[2 * e + side]
            for d in range(stretches):
                at = pl.ds(pl.multiple_of((where_ref[0] ^ d) * cols, cols), cols)
                total += dot(lines_ref[d], w_ref[0, at, :])
        out_ref[:, pl.ds(pl.multiple_of((where_ref[0] ^ e) * chunk, chunk), chunk)] = total.astype(bf16)


def finished(where, x, own, far, weights):
    stretches, rows, cols = own.shape
    width = x.shape[1]
    groups, depth, chunk = weights[0].shape
    share = groups * stretches * chunk
    if chunk % 128:
        order = jnp.arange(stretches) ^ where[0]
        total = lax.dynamic_slice_in_dim(x, where[1] * share, share, 1).astype(f32)
        for side, lines in enumerate((own, far)):
            w = jnp.transpose(jnp.stack(weights[side::2])[order], (2, 1, 0, 3)).reshape(depth, share)
            lines = jnp.transpose(lines[order], (1, 0, 2)).reshape(rows, depth)
            total += dot(lines, w)
        return total.astype(bf16)
    block = stretches * chunk
    whole = pl.BlockSpec((stretches, rows, cols), lambda g, w: (0, 0, 0))
    return pl.pallas_call(
        finish_kernel,
        grid_spec=pltpu.PrefetchScalarGridSpec(
            num_scalar_prefetch=1,
            grid=(groups,),
            in_specs=[pl.BlockSpec((rows, block), lambda g, w: (0, w[1] * groups + g)), whole, whole]
            + [pl.BlockSpec((1, depth, chunk), lambda g, w: (g, 0, 0))] * len(weights),
            out_specs=pl.BlockSpec((rows, block), lambda g, w: (0, g)),
        ),
        out_shape=jax.ShapeDtypeStruct((rows, share), bf16),
        compiler_params=vmem(48),
        cost_estimate=pl.CostEstimate(
            flops=4 * rows * depth * share, bytes_accessed=4 * depth * share, transcendentals=0
        ),
    )(where, x, own, far, *weights)


def over_plane(value):
    peers = lax.axis_size("seq")
    if peers != 4:
        got = [value] + [swapped(value, "seq", d) for d in range(1, peers)]
        half = got[-1].shape[0] // 2
        return got[:-1] + [(got[-1][:half], got[-1][half:])]
    near, other = swapped(value, "seq", 1), swapped(value, "seq", 2)
    half = value.shape[0] // 2
    return [value, near, other, (swapped(near[:half], "seq", 2), swapped(other[half:], "seq", 1))]


def local(
    incoming_activations,
    standardize_scaling,
    lagged_blending_weights,
    learner_line_permutation,
    learner_acceptor_lookup_slices,
    learner_projection_slices,
    fading_left_matrix,
    fading_right_matrix,
    feature_fading_speed,
    self_reward,
    cluster_scaling_vector,
    prompt_extents,
):
    reqs, span, width = incoming_activations.shape
    rows = reqs * span
    stretches = lax.axis_size("seq")
    cores = lax.axis_size("tensor")
    prompts = reqs // cores
    local_width = feature_fading_speed.shape[0]
    cols = local_width // stretches
    t, s = lax.axis_index("tensor"), lax.axis_index("seq")
    where = jnp.stack([s, t]).astype(jnp.int32)

    out_half = learner_projection_slices.astype(bf16)
    out_lines = lax.all_gather(out_half, "req", axis=0, tiled=False)

    pieces = []
    for d in range(stretches):
        piece = lax.dynamic_slice_in_dim(learner_acceptor_lookup_slices, (s ^ d) * cols, cols, 2).astype(bf16)
        pieces.append(swapped(piece, "seq", d) if d else piece)
    weights = [lax.all_gather(piece, "req", axis=0, tiled=False) for piece in pieces]

    x = incoming_activations.reshape(rows, width)
    part = prompts * span
    own_x = lax.dynamic_slice_in_dim(x, t * part, part, 0)
    coeffs = jnp.pad(lagged_blending_weights, ((0, PREFIX - 4), (0, 0)))
    act, coeffs = ordered(own_x, standardize_scaling.reshape(1, width), coeffs, learner_line_permutation.reshape(1, width))
    perm, act = lax.optimization_barrier((learner_line_permutation, act))
    left = fading_left_matrix[perm]
    arrived = over_plane(act)
    acts = jnp.concatenate([*arrived[:-1], *arrived[-1]], axis=0).reshape(stretches, prompts, span, width)
    far_acts = swapped(acts, "tensor", 1)

    groups = out_lines.shape[0] // cores
    kept = lax.dynamic_slice_in_dim(out_lines, t * groups, groups, 0)
    given = lax.dynamic_slice_in_dim(out_lines, (1 - t) * groups, groups, 0)
    out_lines = jnp.stack([kept, swapped(given, "tensor", 1)])
    arrived = over_plane(out_lines)
    out_weights = []
    for pair in arrived[:-1]:
        out_weights += [pair[0], pair[1]]
    out_weights += [half[0] for half in arrived[-1]]

    sides = []
    for values in (acts, far_acts):
        mixed, lora = shifted(where, values, coeffs, left)
        proj = projected(where, mixed.reshape(3, part * stretches, width), weights)
        sides += [proj.reshape(3, prompts, stretches * span, cols), lora.reshape(prompts, stretches * span, -1)]

    def mine(array):
        return lax.dynamic_slice_in_dim(array, s * cols, cols, array.ndim - 1).reshape(-1, cols)

    normed, states = recurrence(
        prompt_extents, where, *sides, mine(fading_right_matrix), mine(feature_fading_speed), mine(self_reward),
        mine(cluster_scaling_vector), stretches, span,
    )

    sent = jnp.concatenate(
        [normed.reshape(stretches, rows, cols), states.reshape(stretches, -1, cols).astype(bf16)], axis=1
    )
    blocks = []
    for d in range(stretches):
        block = lax.dynamic_index_in_dim(sent, s ^ d, 0, keepdims=False)
        blocks.append(swapped(block, "seq", d) if d else block)
    blocks = jnp.stack(blocks)
    own_lines = blocks[:, :rows]
    far_lines = swapped(own_lines, "tensor", 1)
    hidden_out = finished(where, x, own_lines, far_lines, out_weights).reshape(reqs, span, width // cores)

    heads = cols // ATTEND_DIM
    states = blocks[jnp.arange(stretches) ^ s, rows:].reshape(stretches, reqs, ATTEND_DIM, heads, ATTEND_DIM)
    states = jnp.transpose(states, (1, 0, 3, 4, 2)).astype(f32)
    stretch_states = states.reshape(reqs, 1, stretches * heads, ATTEND_DIM * ATTEND_DIM)
    return (hidden_out, stretch_states)


def solution(mesh):
    in_specs = (
        P("req", "seq", None),
        P(),
        P(),
        P(),
        P(None, ("req", "seq"), "tensor"),
        P("tensor", ("req", "seq")),
        P(),
        P(None, "tensor"),
        P("tensor"),
        P("tensor"),
        P("tensor"),
        P("req"),
    )
    out_specs = (P("req", "seq", "tensor"), P("req", "seq", "tensor", None))
    return jax.shard_map(local, mesh=mesh, in_specs=in_specs, out_specs=out_specs, check_vma=False)
```

```python
import functools

import jax
import jax.numpy as jnp
import numpy as np
from jax import lax
from jax.experimental import pallas as pl
from jax.experimental.pallas import tpu as pltpu
from jax.sharding import PartitionSpec as P

ATTEND_DIM = 64
CHUNK = 64
LEVELS = 6
PREFIX = 8
PAST = 16

eps = 1e-05
bf16 = jnp.bfloat16
f32 = jnp.float32


def dot(a, b):
    return jnp.dot(a, b, preferred_element_type=f32)


def dot_nt(a, b):
    return lax.dot_general(a, b, (((1,), (1,)), ((), ())), preferred_element_type=f32)


def dot_tn(a, b):
    return lax.dot_general(a, b, (((0,), (0,)), ((), ())), preferred_element_type=f32)


def swapped(value, axis, by):
    peers = lax.axis_size(axis)
    return lax.ppermute(value, axis, [(i, i ^ by) for i in range(peers)])


def vmem(mib):
    return pltpu.CompilerParams(vmem_limit_bytes=mib * 2**20)


def order_kernel(x_ref, gain_ref, coeff_ref, perm_ref, out_ref, coeff_out_ref, cur_ref):
    rows, width = x_ref.shape
    block = out_ref.shape[1]
    depth = 256

    @pl.when(pl.program_id(0) == 0)
    def _():
        x = x_ref[...].astype(f32)
        mean = jnp.mean(x, axis=-1, keepdims=True)
        centred = x - mean
        spread = jnp.mean(centred * centred, axis=-1, keepdims=True)
        cur_ref[:rows, :] = (centred * lax.rsqrt(spread + eps) * gain_ref[...]).astype(bf16)
        c = coeff_ref[...]
        high = c.astype(bf16)
        cur_ref[rows:, :] = jnp.concatenate([high, (c - high.astype(f32)).astype(bf16)], axis=0)

    perm = perm_ref[...]
    total = jnp.zeros((rows + 2 * PREFIX, block), f32)
    for k in range(width // depth):
        lines = lax.broadcasted_iota(jnp.int32, (depth, block), 0) + k * depth
        chosen = jnp.where(lines == perm, 1.0, 0.0).astype(bf16)
        total += dot(cur_ref[:, k * depth : (k + 1) * depth], chosen)
    out_ref[...] = total[:rows].astype(bf16)
    coeff_out_ref[...] = total[rows : rows + PREFIX] + total[rows + PREFIX :]


def ordered(x, gain, coeffs, perm):
    rows, width = x.shape
    block = 512
    return pl.pallas_call(
        order_kernel,
        grid=(width // block,),
        in_specs=[
            pl.BlockSpec((rows, width), lambda n: (0, 0)),
            pl.BlockSpec((1, width), lambda n: (0, 0)),
            pl.BlockSpec((PREFIX, width), lambda n: (0, 0)),
            pl.BlockSpec((1, block), lambda n: (0, n)),
        ],
        out_specs=[
            pl.BlockSpec((rows, block), lambda n: (0, n)),
            pl.BlockSpec((PREFIX, block), lambda n: (0, n)),
        ],
        out_shape=[
            jax.ShapeDtypeStruct((rows, width), bf16),
            jax.ShapeDtypeStruct((PREFIX, width), f32),
        ],
        scratch_shapes=[pltpu.VMEM((rows + 2 * PREFIX, width), bf16)],
        compiler_params=vmem(40),
        cost_estimate=pl.CostEstimate(
            flops=2 * rows * width * width, bytes_accessed=4 * rows * width, transcendentals=0
        ),
    )(x, gain, coeffs, perm)


def mix_kernel(where_ref, act_ref, coeff_ref, left_ref, *refs):
    mixed_ref, lora_ref, inner_ref = refs[-3:]
    rows, block = mixed_ref.shape[-2:]
    width = 512
    n = pl.program_id(0)
    inner = jnp.zeros(inner_ref.shape, f32)
    for c in range(block // width):
        cols = slice(c * width, (c + 1) * width)
        act = act_ref[:, cols].astype(f32)
        cur = act[PAST:]
        delta = pltpu.roll(act, 1, 0)[PAST:] - cur
        for j in range(3):
            mixed_ref[j, 0, 0, :, cols] = (cur + delta * coeff_ref[j : j + 1, cols]).astype(bf16)
        inner += dot((cur + delta * coeff_ref[3:4, cols]).astype(bf16), left_ref[cols, :])

    @pl.when(n == 0)
    def _():
        inner_ref[...] = inner

    @pl.when(n > 0)
    def _():
        inner_ref[...] += inner

    @pl.when(n == pl.num_programs(0) - 1)
    def _():
        lora_ref[0, 0] = jnp.tanh(inner_ref[...]).astype(bf16)


def shifted(where, act, coeffs, left, side, apart, stretches, earlier):
    span, width = act.shape[0] - PAST, act.shape[1]
    inner = left.shape[1]
    block = 1024
    kept = pl.BlockSpec(memory_space=pl.ANY)
    return pl.pallas_call(
        mix_kernel,
        grid_spec=pltpu.PrefetchScalarGridSpec(
            num_scalar_prefetch=1,
            grid=(width // block,),
            in_specs=[
                pl.BlockSpec((span + PAST, block), lambda n, w: (0, n)),
                pl.BlockSpec((PREFIX, block), lambda n, w: (0, n)),
                pl.BlockSpec((block, inner), lambda n, w: (n, 0)),
            ]
            + [kept] * len(earlier),
            out_specs=[
                pl.BlockSpec((3, 1, 1, span, block), lambda n, w: (0, side, w[0] ^ apart, 0, n)),
                pl.BlockSpec((1, 1, span, inner), lambda n, w: (side, w[0] ^ apart, 0, 0)),
            ],
            scratch_shapes=[pltpu.VMEM((span, inner), f32)],
        ),
        out_shape=[
            jax.ShapeDtypeStruct((3, 2, stretches, span, width), bf16),
            jax.ShapeDtypeStruct((2, stretches, span, inner), bf16),
        ],
        input_output_aliases={4: 0, 5: 1} if earlier else {},
        compiler_params=vmem(32),
        cost_estimate=pl.CostEstimate(
            flops=24 * act.size, bytes_accessed=8 * act.size, transcendentals=0
        ),
    )(where, act, coeffs, left, *earlier)


def project_kernel(where_ref, act_ref, gathered_ref, *refs):
    *pieces, out_ref, lines_ref = refs
    reqs, depth = gathered_ref.shape[0], gathered_ref.shape[2]
    stretches = 1 + len(pieces) // reqs

    @pl.when(pl.program_id(1) == 0)
    def _():
        for r in range(reqs):
            at = (r * stretches + where_ref[0]) * depth
            lines_ref[pl.ds(pl.multiple_of(at, depth), depth), :] = gathered_ref[r, 0]
        for i, piece_ref in enumerate(pieces):
            d, k = 1 + i // reqs, i % reqs
            at = (lax.rem(where_ref[2] + k, reqs) * stretches + (where_ref[0] ^ d)) * depth
            lines_ref[pl.ds(pl.multiple_of(at, depth), depth), :] = piece_ref[0]

    out_ref[0, 0, 0] = dot(act_ref[0, 0, 0], lines_ref[...]).astype(bf16)


def projected(where, mixed, gathered, pieces):
    reqs, kinds, depth, cols = gathered.shape
    _, sides, stretches, span, width = mixed.shape
    if depth % 128:
        order = jnp.arange(stretches) ^ where[0]
        lines = jnp.stack([gathered, *pieces])[order]
        lines = jnp.transpose(lines, (2, 1, 0, 3, 4)).reshape(kinds, width, cols)
        return jnp.einsum("jxbtk,jkc->jxbtc", mixed, lines, preferred_element_type=f32).astype(bf16)
    return pl.pallas_call(
        project_kernel,
        grid_spec=pltpu.PrefetchScalarGridSpec(
            num_scalar_prefetch=1,
            grid=(kinds, sides * stretches),
            in_specs=[
                pl.BlockSpec((1, 1, 1, span, width), lambda j, m, w: (j, m // stretches, m % stretches, 0, 0)),
                pl.BlockSpec((reqs, 1, depth, cols), lambda j, m, w: (0, j, 0, 0)),
            ]
            + [pl.BlockSpec((1, depth, cols), lambda j, m, w: (j, 0, 0))] * len(pieces),
            out_specs=pl.BlockSpec((1, 1, 1, span, cols), lambda j, m, w: (j, m // stretches, m % stretches, 0, 0)),
            scratch_shapes=[pltpu.VMEM((width, cols), bf16)],
        ),
        out_shape=jax.ShapeDtypeStruct((kinds, sides, stretches, span, cols), bf16),
        compiler_params=vmem(40),
        cost_estimate=pl.CostEstimate(
            flops=2 * mixed.size * cols,
            bytes_accessed=2 * (mixed.size + kinds * width * cols),
            transcendentals=0,
        ),
    )(where, mixed, gathered, *pieces)


def decay_sums():
    place = np.arange(CHUNK)
    of, by = place[:, None], place[None, :]
    parts = []
    for level in range(LEVELS):
        half = 1 << level
        middle = (of // (2 * half)) * 2 * half + half - 1
        later = (of % (2 * half)) >= half
        parts.append(np.where(later, (by > middle) & (by < of), (by > of) & (by <= middle)))
    parts += [by < of, by > of, np.ones((8, CHUNK), bool)]
    sums = np.concatenate(parts).astype(np.float32)
    return np.concatenate([sums, sums], axis=1)


def pair_levels(heads):
    of, by = np.arange(CHUNK)[:, None], np.arange(CHUNK)[None, :]
    level = np.full((CHUNK, CHUNK), -1.0, np.float32)
    for bit in range(LEVELS):
        level[((of ^ by) >> bit) == 1] = bit
    return np.tile(np.where(of > by, level, -1.0).astype(np.float32), (1, heads))


def wkv_kernel(
    extent_ref, where_ref, proj_ref, lora_ref, right_ref, speed_ref, reward_ref, scale_ref, sums_ref, level_ref,
    same_ref, normed_ref, state_ref, memory_ref,
):
    step = pl.program_id(0)
    tokens, cols = proj_ref.shape[3:]
    heads = cols // ATTEND_DIM
    per_block = pl.num_programs(0) // lax.axis_size("seq")
    same = same_ref[...]
    same_f32 = same.astype(f32)
    level = level_ref[...]

    @pl.when(step == 0)
    def _():
        memory_ref[...] = jnp.zeros_like(memory_ref)

    memories = [memory_ref[0], memory_ref[1]]
    for sub in range(tokens // CHUNK):
        lines = slice(sub * CHUNK, (sub + 1) * CHUNK)
        at = step * tokens + sub * CHUNK + lax.broadcasted_iota(jnp.int32, (CHUNK, cols), 0)
        for side in range(2):
            prompt = where_ref[1] ^ side
            valid = jnp.where(at < extent_ref[prompt], 1.0, 0.0)
            r = proj_ref[0, side, 0, lines].astype(f32)
            k = proj_ref[1, side, 0, lines].astype(f32) * valid
            v = proj_ref[2, side, 0, lines]
            decay = -speed_ref[...] * jnp.exp(dot(lora_ref[side, 0, lines], right_ref[...])) * valid
            high = decay.astype(bf16)
            low = (decay - high.astype(f32)).astype(bf16)
            kept = jnp.exp(dot(sums_ref[...], jnp.concatenate([high, low], axis=0)))
            scores = jnp.zeros((CHUNK, heads * CHUNK), f32)
            for bit in range(LEVELS):
                part = kept[bit * CHUNK : (bit + 1) * CHUNK]
                lookup = (k * part).astype(bf16)
                lookup = jnp.concatenate([lookup] * heads, axis=0) * same
                found = dot_nt((r * part).astype(bf16), lookup)
                scores = jnp.where(level == bit, found, scores)
            v_heads = jnp.concatenate([v] * heads, axis=0) * same
            memory = memories[side]
            from_start = (r * kept[LEVELS * CHUNK : (LEVELS + 1) * CHUNK]).astype(bf16)
            to_end = (k * kept[(LEVELS + 1) * CHUNK : (LEVELS + 2) * CHUNK]).astype(bf16)
            own = dot((r * reward_ref[...] * k).astype(bf16), same)
            y = dot_nt(from_start, memory.astype(bf16)) + dot(scores.astype(bf16), v_heads)
            y += own * v.astype(f32)
            whole = kept[(LEVELS + 2) * CHUNK : (LEVELS + 2) * CHUNK + 1]
            memories[side] = memory * whole + same_f32 * dot_tn(v, to_end)

            y_high = y.astype(bf16)
            y_low = (y - y_high.astype(f32)).astype(bf16)
            centred = y - (dot(y_high, same) + dot(y_low, same)) * (1.0 / ATTEND_DIM)
            spread = dot((centred * centred).astype(bf16), same) * (1.0 / ATTEND_DIM)
            normed = centred * lax.rsqrt(spread + eps) * scale_ref[...] * valid
            normed_ref[0, pl.ds(prompt, 1), lines] = normed.astype(bf16)[None]
    for side in range(2):
        memory_ref[side] = memories[side]

    @pl.when(step % per_block == per_block - 1)
    def _():
        for side in range(2):
            folded = memory_ref[side, :ATTEND_DIM]
            for h in range(1, heads):
                folded += memory_ref[side, h * ATTEND_DIM : (h + 1) * ATTEND_DIM]
            state_ref[0, pl.ds(where_ref[1] ^ side, 1)] = folded[None]


def recurrence(extents, where, proj, lora, right, speed, reward, scale):
    _, reqs, stretches, span, cols = proj.shape
    inner = lora.shape[-1]
    heads = cols // ATTEND_DIM
    tokens = 2 * CHUNK
    per_block = span // tokens
    sums = jnp.asarray(decay_sums(), bf16)
    level = jnp.asarray(pair_levels(heads), f32)
    head = np.arange(cols) // ATTEND_DIM
    same = jnp.asarray(head[:, None] == head[None, :], bf16)

    def fixed(array):
        return pl.BlockSpec(array.shape, lambda c, e, w: (0,) * array.ndim)

    tables = (right, speed, reward, scale, sums, level, same)
    return pl.pallas_call(
        wkv_kernel,
        grid_spec=pltpu.PrefetchScalarGridSpec(
            num_scalar_prefetch=2,
            grid=(stretches * per_block,),
            in_specs=[
                pl.BlockSpec((3, reqs, 1, tokens, cols), lambda c, e, w: (0, 0, c // per_block, c % per_block, 0)),
                pl.BlockSpec((reqs, 1, tokens, inner), lambda c, e, w: (0, c // per_block, c % per_block, 0)),
            ]
            + [fixed(a) for a in tables],
            out_specs=[
                pl.BlockSpec((1, reqs, tokens, cols), lambda c, e, w: (c // per_block, 0, c % per_block, 0)),
                pl.BlockSpec((1, reqs, ATTEND_DIM, cols), lambda c, e, w: (c // per_block, 0, 0, 0)),
            ],
            scratch_shapes=[pltpu.VMEM((reqs, cols, cols), f32)],
        ),
        out_shape=[
            jax.ShapeDtypeStruct((stretches, reqs, span, cols), bf16),
            jax.ShapeDtypeStruct((stretches, reqs, ATTEND_DIM, cols), f32),
        ],
        compiler_params=vmem(40),
        cost_estimate=pl.CostEstimate(
            flops=proj.size * 3000, bytes_accessed=4 * proj.size, transcendentals=0
        ),
    )(extents, where, proj, lora, *tables)


def finish_kernel(where_ref, x_ref, own_ref, far_ref, *refs):
    *weights, out_ref = refs
    stretches, rows, cols = own_ref.shape
    chunk = weights[0].shape[-1]
    for e in range(stretches):
        total = x_ref[:, pl.ds(pl.multiple_of((where_ref[0] ^ e) * chunk, chunk), chunk)].astype(f32)
        for side, lines_ref in enumerate((own_ref, far_ref)):
            w_ref = weights[e]
            for d in range(stretches):
                at = pl.ds(pl.multiple_of((where_ref[0] ^ d) * cols, cols), cols)
                total += dot(lines_ref[d], w_ref[side, 0, at, :])
        out_ref[:, pl.ds(pl.multiple_of((where_ref[0] ^ e) * chunk, chunk), chunk)] = total.astype(bf16)


def finished(where, x, own, far, weights):
    stretches, rows, cols = own.shape
    width = x.shape[1]
    _, groups, depth, chunk = weights[0].shape
    share = groups * stretches * chunk
    if chunk % 128:
        order = jnp.arange(stretches) ^ where[0]
        total = lax.dynamic_slice_in_dim(x, where[1] * share, share, 1).astype(f32)
        for side, lines in enumerate((own, far)):
            w = jnp.transpose(jnp.stack([w[side] for w in weights])[order], (2, 1, 0, 3)).reshape(depth, share)
            lines = jnp.transpose(lines[order], (1, 0, 2)).reshape(rows, depth)
            total += dot(lines, w)
        return total.astype(bf16)
    block = stretches * chunk
    whole = pl.BlockSpec((stretches, rows, cols), lambda g, w: (0, 0, 0))
    return pl.pallas_call(
        finish_kernel,
        grid_spec=pltpu.PrefetchScalarGridSpec(
            num_scalar_prefetch=1,
            grid=(groups,),
            in_specs=[pl.BlockSpec((rows, block), lambda g, w: (0, w[1] * groups + g)), whole, whole]
            + [pl.BlockSpec((2, 1, depth, chunk), lambda g, w: (0, g, 0, 0))] * len(weights),
            out_specs=pl.BlockSpec((rows, block), lambda g, w: (0, g)),
        ),
        out_shape=jax.ShapeDtypeStruct((rows, share), bf16),
        compiler_params=vmem(48),
        cost_estimate=pl.CostEstimate(
            flops=4 * rows * depth * share, bytes_accessed=4 * depth * share, transcendentals=0
        ),
    )(where, x, own, far, *weights)


def over_plane(value, cut):
    peers = lax.axis_size("seq")
    if peers != 4 or not cut:
        return [value] + [swapped(value, "seq", d) for d in range(1, peers)]
    near, other = swapped(value, "seq", 1), swapped(value, "seq", 2)
    across = [swapped(near[:cut], "seq", 2), swapped(other[cut:], "seq", 1)]
    return [value, near, other, jnp.concatenate(across, axis=0)]


def ahead(value, axis, by):
    peers = lax.axis_size(axis)
    return lax.ppermute(value, axis, [((i + by) % peers, i) for i in range(peers)])


def local(
    incoming_activations,
    standardize_scaling,
    lagged_blending_weights,
    learner_line_permutation,
    learner_acceptor_lookup_slices,
    learner_projection_slices,
    fading_left_matrix,
    fading_right_matrix,
    feature_fading_speed,
    self_reward,
    cluster_scaling_vector,
    prompt_extents,
):
    reqs, span, width = incoming_activations.shape
    rows = reqs * span
    stretches = lax.axis_size("seq")
    cores = lax.axis_size("tensor")
    groups = lax.axis_size("req")
    assert reqs == cores == 2
    local_width = feature_fading_speed.shape[0]
    cols = local_width // stretches
    t, s = lax.axis_index("tensor"), lax.axis_index("seq")
    where = jnp.stack([s, t, lax.axis_index("req")]).astype(jnp.int32)

    x = incoming_activations.reshape(rows, width)
    own_x = lax.dynamic_slice_in_dim(x, t * span, span, 0)
    past = lax.ppermute(own_x[span - PAST :], "seq", [(i, i + 1) for i in range(stretches - 1)])
    pieces = [
        lax.dynamic_slice_in_dim(learner_acceptor_lookup_slices, (s ^ d) * cols, cols, 2).astype(bf16)
        for d in range(stretches)
    ]
    out_half = learner_projection_slices.astype(bf16)
    out_lines = lax.all_gather(out_half, "req", axis=0, tiled=False)
    gathered = lax.all_gather(pieces[0], "req", axis=0, tiled=False)
    got = [swapped(pieces[d], "seq", d) for d in range(1, stretches)]

    own_x, past, *_ = lax.optimization_barrier((own_x, past, *pieces))
    coeffs = jnp.pad(lagged_blending_weights, ((0, PREFIX - 4), (0, 0)))
    act, coeffs = ordered(
        jnp.concatenate([past, own_x], axis=0),
        standardize_scaling.reshape(1, width),
        coeffs,
        learner_line_permutation.reshape(1, width),
    )
    act, perm, *got = lax.optimization_barrier((act, learner_line_permutation, *got))
    if pieces[0].shape[1] % 128:
        weights = [lax.all_gather(piece, "req", axis=0, tiled=False) for piece in got]
    else:
        weights = [ahead(piece, "req", k) if k else piece for piece in got for k in range(groups)]
    left = fading_left_matrix[perm]

    acts = over_plane(act, (span + PAST) // 32 * 16)
    results = ()
    for d, block in enumerate(acts):
        for side, values in enumerate((block, swapped(block, "tensor", 1))):
            results = shifted(where, values, coeffs, left, side, d, stretches, results)
    mixed, lora = results

    share = groups // cores
    kept = lax.dynamic_slice_in_dim(out_lines, t * share, share, 0)
    given = lax.dynamic_slice_in_dim(out_lines, (1 - t) * share, share, 0)
    out_lines = jnp.stack([kept, swapped(given, "tensor", 1)])
    out_lines, _ = lax.optimization_barrier((out_lines, acts[-1]))
    out_weights = over_plane(out_lines, 0)

    proj = projected(where, mixed, gathered, weights)

    def mine(array):
        return lax.dynamic_slice_in_dim(array, s * cols, cols, array.ndim - 1).reshape(-1, cols)

    normed, states = recurrence(
        prompt_extents, where, proj, lora, mine(fading_right_matrix), mine(feature_fading_speed), mine(self_reward),
        mine(cluster_scaling_vector),
    )

    sent = jnp.concatenate(
        [normed.reshape(stretches, rows, cols), states.reshape(stretches, -1, cols).astype(bf16)], axis=1
    )
    blocks = []
    for d in range(stretches):
        block = lax.dynamic_index_in_dim(sent, s ^ d, 0, keepdims=False)
        blocks.append(swapped(block, "seq", d) if d else block)
    blocks = jnp.stack(blocks)
    own_lines = blocks[:, :rows]
    far_lines = swapped(own_lines, "tensor", 1)
    hidden_out = finished(where, x, own_lines, far_lines, out_weights).reshape(reqs, span, width // cores)

    heads = cols // ATTEND_DIM
    states = blocks[jnp.arange(stretches) ^ s, rows:].reshape(stretches, reqs, ATTEND_DIM, heads, ATTEND_DIM)
    states = jnp.transpose(states, (1, 0, 3, 4, 2)).astype(f32)
    stretch_states = states.reshape(reqs, 1, stretches * heads, ATTEND_DIM * ATTEND_DIM)
    return (hidden_out, stretch_states)


def solution(mesh):
    in_specs = (
        P("req", "seq", None),
        P(),
        P(),
        P(),
        P(None, ("req", "seq"), "tensor"),
        P("tensor", ("req", "seq")),
        P(),
        P(None, "tensor"),
        P("tensor"),
        P("tensor"),
        P("tensor"),
        P("req"),
    )
    out_specs = (P("req", "seq", "tensor"), P("req", "seq", "tensor", None))
    return jax.shard_map(local, mesh=mesh, in_specs=in_specs, out_specs=out_specs, check_vma=False)
```

```python
import functools

import jax
import jax.numpy as jnp
import numpy as np
from jax import lax
from jax.experimental import pallas as pl
from jax.experimental.pallas import tpu as pltpu
from jax.sharding import PartitionSpec as P

ATTEND_DIM = 64
CHUNK = 64
LEVELS = 6
PREFIX = 8
PAST = 16

SMALL = pl.CostEstimate(flops=1024, bytes_accessed=1024, transcendentals=0)

eps = 1e-05
bf16 = jnp.bfloat16
f32 = jnp.float32


def dot(a, b):
    return jnp.dot(a, b, preferred_element_type=f32)


def dot_nt(a, b):
    return lax.dot_general(a, b, (((1,), (1,)), ((), ())), preferred_element_type=f32)


def dot_tn(a, b):
    return lax.dot_general(a, b, (((0,), (0,)), ((), ())), preferred_element_type=f32)


def swapped(value, axis, by):
    peers = lax.axis_size(axis)
    return lax.ppermute(value, axis, [(i, i ^ by) for i in range(peers)])


def vmem(mib):
    return pltpu.CompilerParams(vmem_limit_bytes=mib * 2**20)


def order_kernel(x_ref, gain_ref, coeff_ref, perm_ref, out_ref, coeff_out_ref, cur_ref):
    rows, width = x_ref.shape
    block = out_ref.shape[1]
    depth = 256

    @pl.when(pl.program_id(0) == 0)
    def _():
        x = x_ref[...].astype(f32)
        mean = jnp.mean(x, axis=-1, keepdims=True)
        centred = x - mean
        spread = jnp.mean(centred * centred, axis=-1, keepdims=True)
        cur_ref[:rows, :] = (centred * lax.rsqrt(spread + eps) * gain_ref[...]).astype(bf16)
        c = coeff_ref[...]
        high = c.astype(bf16)
        cur_ref[rows:, :] = jnp.concatenate([high, (c - high.astype(f32)).astype(bf16)], axis=0)

    perm = perm_ref[...]
    total = jnp.zeros((rows + 2 * PREFIX, block), f32)
    for k in range(width // depth):
        lines = lax.broadcasted_iota(jnp.int32, (depth, block), 0) + k * depth
        chosen = jnp.where(lines == perm, 1.0, 0.0).astype(bf16)
        total += dot(cur_ref[:, k * depth : (k + 1) * depth], chosen)
    out_ref[...] = total[:rows].astype(bf16)
    coeff_out_ref[...] = total[rows : rows + PREFIX] + total[rows + PREFIX :]


def ordered(x, gain, coeffs, perm):
    rows, width = x.shape
    block = 512
    return pl.pallas_call(
        order_kernel,
        grid=(width // block,),
        in_specs=[
            pl.BlockSpec((rows, width), lambda n: (0, 0)),
            pl.BlockSpec((1, width), lambda n: (0, 0)),
            pl.BlockSpec((PREFIX, width), lambda n: (0, 0)),
            pl.BlockSpec((1, block), lambda n: (0, n)),
        ],
        out_specs=[
            pl.BlockSpec((rows, block), lambda n: (0, n)),
            pl.BlockSpec((PREFIX, block), lambda n: (0, n)),
        ],
        out_shape=[
            jax.ShapeDtypeStruct((rows, width), bf16),
            jax.ShapeDtypeStruct((PREFIX, width), f32),
        ],
        scratch_shapes=[pltpu.VMEM((rows + 2 * PREFIX, width), bf16)],
        compiler_params=vmem(40),
        cost_estimate=SMALL,
    )(x, gain, coeffs, perm)


def mix_kernel(where_ref, act_ref, coeff_ref, left_ref, *refs):
    mixed_ref, lora_ref, inner_ref = refs[-3:]
    rows, block = mixed_ref.shape[-2:]
    width = 512
    n = pl.program_id(0)
    inner = jnp.zeros(inner_ref.shape, f32)
    for c in range(block // width):
        cols = slice(c * width, (c + 1) * width)
        cur = act_ref[PAST:, cols]
        delta = pltpu.roll(act_ref[:, cols].astype(f32), 1, 0)[PAST:].astype(bf16) - cur
        for j in range(3):
            mixed_ref[j, 0, 0, :, cols] = cur + delta * coeff_ref[j : j + 1, cols].astype(bf16)
        inner += dot(cur + delta * coeff_ref[3:4, cols].astype(bf16), left_ref[cols, :])

    @pl.when(n == 0)
    def _():
        inner_ref[...] = inner

    @pl.when(n > 0)
    def _():
        inner_ref[...] += inner

    @pl.when(n == pl.num_programs(0) - 1)
    def _():
        lora_ref[0, 0] = jnp.tanh(inner_ref[...]).astype(bf16)


def shifted(where, act, coeffs, left, side, apart, stretches, earlier):
    span, width = act.shape[0] - PAST, act.shape[1]
    inner = left.shape[1]
    block = 1024
    kept = pl.BlockSpec(memory_space=pl.ANY)
    return pl.pallas_call(
        mix_kernel,
        grid_spec=pltpu.PrefetchScalarGridSpec(
            num_scalar_prefetch=1,
            grid=(width // block,),
            in_specs=[
                pl.BlockSpec((span + PAST, block), lambda n, w: (0, n)),
                pl.BlockSpec((PREFIX, block), lambda n, w: (0, n)),
                pl.BlockSpec((block, inner), lambda n, w: (n, 0)),
            ]
            + [kept] * len(earlier),
            out_specs=[
                pl.BlockSpec((3, 1, 1, span, block), lambda n, w: (0, side, w[0] ^ apart, 0, n)),
                pl.BlockSpec((1, 1, span, inner), lambda n, w: (side, w[0] ^ apart, 0, 0)),
            ],
            scratch_shapes=[pltpu.VMEM((span, inner), f32)],
        ),
        out_shape=[
            jax.ShapeDtypeStruct((3, 2, stretches, span, width), bf16),
            jax.ShapeDtypeStruct((2, stretches, span, inner), bf16),
        ],
        input_output_aliases={4: 0, 5: 1} if earlier else {},
        compiler_params=vmem(32),
        cost_estimate=SMALL,
    )(where, act, coeffs, left, *earlier)


def project_kernel(where_ref, act_ref, gathered_ref, *refs):
    *pieces, out_ref, lines_ref = refs
    reqs, depth = gathered_ref.shape[0], gathered_ref.shape[2]
    stretches = 1 + len(pieces) // reqs

    @pl.when(pl.program_id(1) == 0)
    def _():
        for r in range(reqs):
            at = (r * stretches + where_ref[0]) * depth
            lines_ref[pl.ds(pl.multiple_of(at, depth), depth), :] = gathered_ref[r, 0]
        for i, piece_ref in enumerate(pieces):
            d, k = 1 + i // reqs, i % reqs
            at = (lax.rem(where_ref[2] + k, reqs) * stretches + (where_ref[0] ^ d)) * depth
            lines_ref[pl.ds(pl.multiple_of(at, depth), depth), :] = piece_ref[0]

    act = act_ref[0, 0].reshape(-1, act_ref.shape[-1])
    out_ref[0, 0] = dot(act, lines_ref[...]).astype(bf16).reshape(out_ref.shape[2:])


def projected(where, mixed, gathered, pieces):
    reqs, kinds, depth, cols = gathered.shape
    _, sides, stretches, span, width = mixed.shape
    if depth % 128:
        order = jnp.arange(stretches) ^ where[0]
        lines = jnp.stack([gathered, *pieces])[order]
        lines = jnp.transpose(lines, (2, 1, 0, 3, 4)).reshape(kinds, width, cols)
        return jnp.einsum("jxbtk,jkc->jxbtc", mixed, lines, preferred_element_type=f32).astype(bf16)
    return pl.pallas_call(
        project_kernel,
        grid_spec=pltpu.PrefetchScalarGridSpec(
            num_scalar_prefetch=1,
            grid=(kinds, sides),
            in_specs=[
                pl.BlockSpec((1, 1, stretches, span, width), lambda j, m, w: (j, m, 0, 0, 0)),
                pl.BlockSpec((reqs, 1, depth, cols), lambda j, m, w: (0, j, 0, 0)),
            ]
            + [pl.BlockSpec((1, depth, cols), lambda j, m, w: (j, 0, 0))] * len(pieces),
            out_specs=pl.BlockSpec((1, 1, stretches, span, cols), lambda j, m, w: (j, m, 0, 0, 0)),
            scratch_shapes=[pltpu.VMEM((width, cols), bf16)],
        ),
        out_shape=jax.ShapeDtypeStruct((kinds, sides, stretches, span, cols), bf16),
        compiler_params=vmem(40),
        cost_estimate=SMALL,
    )(where, mixed, gathered, *pieces)


def decay_sums():
    place = np.arange(CHUNK)
    of, by = place[:, None], place[None, :]
    parts = []
    for level in range(LEVELS):
        half = 1 << level
        middle = (of // (2 * half)) * 2 * half + half - 1
        later = (of % (2 * half)) >= half
        parts.append(np.where(later, (by > middle) & (by < of), (by > of) & (by <= middle)))
    parts += [by < of, by > of, np.ones((8, CHUNK), bool)]
    sums = np.concatenate(parts).astype(np.float32)
    return np.concatenate([sums, sums], axis=1)


def pair_levels(heads):
    of, by = np.arange(CHUNK)[:, None], np.arange(CHUNK)[None, :]
    level = np.full((CHUNK, CHUNK), -1.0, np.float32)
    for bit in range(LEVELS):
        level[((of ^ by) >> bit) == 1] = bit
    return np.tile(np.where(of > by, level, -1.0).astype(np.float32), (1, heads))


def wkv_kernel(
    extent_ref, where_ref, proj_ref, lora_ref, right_ref, speed_ref, reward_ref, scale_ref, sums_ref, level_ref,
    same_ref, normed_ref, state_ref, memory_ref,
):
    step = pl.program_id(0)
    tokens, cols = proj_ref.shape[3:]
    heads = cols // ATTEND_DIM
    per_block = pl.num_programs(0) // lax.axis_size("seq")
    same = same_ref[...]
    same_f32 = same.astype(f32)
    level = level_ref[...]

    @pl.when(step == 0)
    def _():
        memory_ref[...] = jnp.zeros_like(memory_ref)

    memories = [memory_ref[0], memory_ref[1]]
    for sub in range(tokens // CHUNK):
        lines = slice(sub * CHUNK, (sub + 1) * CHUNK)
        at = step * tokens + sub * CHUNK + lax.broadcasted_iota(jnp.int32, (CHUNK, cols), 0)
        for side in range(2):
            prompt = where_ref[1] ^ side
            valid = jnp.where(at < extent_ref[prompt], 1.0, 0.0)
            r = proj_ref[0, side, 0, lines].astype(f32)
            k = proj_ref[1, side, 0, lines].astype(f32) * valid
            v = proj_ref[2, side, 0, lines]
            decay = -speed_ref[...] * jnp.exp(dot(lora_ref[side, 0, lines], right_ref[...])) * valid
            high = decay.astype(bf16)
            low = (decay - high.astype(f32)).astype(bf16)
            kept = jnp.exp(dot(sums_ref[...], jnp.concatenate([high, low], axis=0)))
            scores = jnp.zeros((CHUNK, heads * CHUNK), f32)
            for bit in range(LEVELS):
                part = kept[bit * CHUNK : (bit + 1) * CHUNK]
                lookup = (k * part).astype(bf16)
                lookup = jnp.concatenate([lookup] * heads, axis=0) * same
                found = dot_nt((r * part).astype(bf16), lookup)
                scores = jnp.where(level == bit, found, scores)
            v_heads = jnp.concatenate([v] * heads, axis=0) * same
            memory = memories[side]
            from_start = (r * kept[LEVELS * CHUNK : (LEVELS + 1) * CHUNK]).astype(bf16)
            to_end = (k * kept[(LEVELS + 1) * CHUNK : (LEVELS + 2) * CHUNK]).astype(bf16)
            own = dot((r * reward_ref[...] * k).astype(bf16), same)
            y = dot_nt(from_start, memory.astype(bf16)) + dot(scores.astype(bf16), v_heads)
            y += own * v.astype(f32)
            whole = kept[(LEVELS + 2) * CHUNK : (LEVELS + 2) * CHUNK + 1]
            memories[side] = memory * whole + same_f32 * dot_tn(v, to_end)

            y_high = y.astype(bf16)
            y_low = (y - y_high.astype(f32)).astype(bf16)
            centred = y - (dot(y_high, same) + dot(y_low, same)) * (1.0 / ATTEND_DIM)
            spread = dot((centred * centred).astype(bf16), same) * (1.0 / ATTEND_DIM)
            normed = centred * lax.rsqrt(spread + eps) * scale_ref[...] * valid
            normed_ref[0, pl.ds(prompt, 1), lines] = normed.astype(bf16)[None]
    for side in range(2):
        memory_ref[side] = memories[side]

    @pl.when(step % per_block == per_block - 1)
    def _():
        for side in range(2):
            folded = memory_ref[side, :ATTEND_DIM]
            for h in range(1, heads):
                folded += memory_ref[side, h * ATTEND_DIM : (h + 1) * ATTEND_DIM]
            state_ref[0, pl.ds(where_ref[1] ^ side, 1)] = folded[None]


def recurrence(extents, where, proj, lora, right, speed, reward, scale):
    _, reqs, stretches, span, cols = proj.shape
    inner = lora.shape[-1]
    heads = cols // ATTEND_DIM
    tokens = 2 * CHUNK
    per_block = span // tokens
    sums = jnp.asarray(decay_sums(), bf16)
    level = jnp.asarray(pair_levels(heads), f32)
    head = np.arange(cols) // ATTEND_DIM
    same = jnp.asarray(head[:, None] == head[None, :], bf16)

    def fixed(array):
        return pl.BlockSpec(array.shape, lambda c, e, w: (0,) * array.ndim)

    tables = (right, speed, reward, scale, sums, level, same)
    return pl.pallas_call(
        wkv_kernel,
        grid_spec=pltpu.PrefetchScalarGridSpec(
            num_scalar_prefetch=2,
            grid=(stretches * per_block,),
            in_specs=[
                pl.BlockSpec((3, reqs, 1, tokens, cols), lambda c, e, w: (0, 0, c // per_block, c % per_block, 0)),
                pl.BlockSpec((reqs, 1, tokens, inner), lambda c, e, w: (0, c // per_block, c % per_block, 0)),
            ]
            + [fixed(a) for a in tables],
            out_specs=[
                pl.BlockSpec((1, reqs, tokens, cols), lambda c, e, w: (c // per_block, 0, c % per_block, 0)),
                pl.BlockSpec((1, reqs, ATTEND_DIM, cols), lambda c, e, w: (c // per_block, 0, 0, 0)),
            ],
            scratch_shapes=[pltpu.VMEM((reqs, cols, cols), f32)],
        ),
        out_shape=[
            jax.ShapeDtypeStruct((stretches, reqs, span, cols), bf16),
            jax.ShapeDtypeStruct((stretches, reqs, ATTEND_DIM, cols), f32),
        ],
        compiler_params=vmem(40),
        cost_estimate=SMALL,
    )(extents, where, proj, lora, *tables)


def finish_kernel(where_ref, x_ref, own_ref, far_ref, *refs):
    *weights, out_ref = refs
    stretches, rows, cols = own_ref.shape
    chunk = weights[0].shape[-1]
    for e in range(stretches):
        total = x_ref[:, pl.ds(pl.multiple_of((where_ref[0] ^ e) * chunk, chunk), chunk)].astype(f32)
        for side, lines_ref in enumerate((own_ref, far_ref)):
            w_ref = weights[e]
            for d in range(stretches):
                at = pl.ds(pl.multiple_of((where_ref[0] ^ d) * cols, cols), cols)
                total += dot(lines_ref[d], w_ref[side, 0, at, :])
        out_ref[:, pl.ds(pl.multiple_of((where_ref[0] ^ e) * chunk, chunk), chunk)] = total.astype(bf16)


def finished(where, x, own, far, weights):
    stretches, rows, cols = own.shape
    width = x.shape[1]
    _, groups, depth, chunk = weights[0].shape
    share = groups * stretches * chunk
    if chunk % 128:
        order = jnp.arange(stretches) ^ where[0]
        total = lax.dynamic_slice_in_dim(x, where[1] * share, share, 1).astype(f32)
        for side, lines in enumerate((own, far)):
            w = jnp.transpose(jnp.stack([w[side] for w in weights])[order], (2, 1, 0, 3)).reshape(depth, share)
            lines = jnp.transpose(lines[order], (1, 0, 2)).reshape(rows, depth)
            total += dot(lines, w)
        return total.astype(bf16)
    block = stretches * chunk
    whole = pl.BlockSpec((stretches, rows, cols), lambda g, w: (0, 0, 0))
    return pl.pallas_call(
        finish_kernel,
        grid_spec=pltpu.PrefetchScalarGridSpec(
            num_scalar_prefetch=1,
            grid=(groups,),
            in_specs=[pl.BlockSpec((rows, block), lambda g, w: (0, w[1] * groups + g)), whole, whole]
            + [pl.BlockSpec((2, 1, depth, chunk), lambda g, w: (0, g, 0, 0))] * len(weights),
            out_specs=pl.BlockSpec((rows, block), lambda g, w: (0, g)),
        ),
        out_shape=jax.ShapeDtypeStruct((rows, share), bf16),
        compiler_params=vmem(48),
        cost_estimate=SMALL,
    )(where, x, own, far, *weights)


def ahead(value, axis, by):
    peers = lax.axis_size(axis)
    return lax.ppermute(value, axis, [((i + by) % peers, i) for i in range(peers)])


def local(
    incoming_activations,
    standardize_scaling,
    lagged_blending_weights,
    learner_line_permutation,
    learner_acceptor_lookup_slices,
    learner_projection_slices,
    fading_left_matrix,
    fading_right_matrix,
    feature_fading_speed,
    self_reward,
    cluster_scaling_vector,
    prompt_extents,
):
    reqs, span, width = incoming_activations.shape
    rows = reqs * span
    stretches = lax.axis_size("seq")
    cores = lax.axis_size("tensor")
    groups = lax.axis_size("req")
    assert reqs == cores == 2 and stretches == 4
    local_width = feature_fading_speed.shape[0]
    cols = local_width // stretches
    t, s = lax.axis_index("tensor"), lax.axis_index("seq")
    where = jnp.stack([s, t, lax.axis_index("req")]).astype(jnp.int32)

    x = incoming_activations.reshape(rows, width)
    own_x = lax.dynamic_slice_in_dim(x, t * span, span, 0)
    past = lax.ppermute(own_x[span - PAST :], "seq", [(i, i + 1) for i in range(stretches - 1)])
    pieces = [
        lax.dynamic_slice_in_dim(learner_acceptor_lookup_slices, (s ^ d) * cols, cols, 2).astype(bf16)
        for d in range(stretches)
    ]
    out_half = learner_projection_slices.astype(bf16)
    out_lines = lax.all_gather(out_half, "req", axis=0, tiled=False)
    gathered = lax.all_gather(pieces[0], "req", axis=0, tiled=False)
    got = [swapped(pieces[d], "seq", d) for d in range(1, stretches)]

    def tied(*values):
        return lax.optimization_barrier(values)

    own_x, past, *_ = tied(own_x, past, out_half, *pieces)
    coeffs = jnp.pad(lagged_blending_weights, ((0, PREFIX - 4), (0, 0)))
    act, coeffs = ordered(
        jnp.concatenate([past, own_x], axis=0),
        standardize_scaling.reshape(1, width),
        coeffs,
        learner_line_permutation.reshape(1, width),
    )
    act, perm, *got = tied(act, learner_line_permutation, *got)
    direct = pieces[0].shape[1] % 128 == 0

    def along_z(piece):
        if not direct:
            return [lax.all_gather(piece, "req", axis=0, tiled=False)]
        return [ahead(piece, "req", k) if k else piece for k in range(groups)]

    def mixed_in(values, side, apart, earlier):
        return shifted(where, values, coeffs, left, side, apart, stretches, earlier)

    left = fading_left_matrix[perm]
    cut = (span + PAST) // 32 * 16
    near, other = swapped(act, "seq", 1), swapped(act, "seq", 2)
    lines = along_z(got[0])
    results = mixed_in(act, 0, 0, ())
    results = mixed_in(swapped(act, "tensor", 1), 1, 0, results)
    near, other, *rest = tied(near, other, *results, *lines, *got[1:])
    results, lines, got = tuple(rest[:2]), rest[2:-2], rest[-2:]

    across = [swapped(near[:cut], "seq", 2), swapped(other[cut:], "seq", 1)]
    more = along_z(got[0])
    results = mixed_in(near, 0, 1, results)
    results = mixed_in(other, 0, 2, results)
    far = swapped(jnp.stack([near, other]), "tensor", 1)
    share = groups // cores
    kept = lax.dynamic_slice_in_dim(out_lines, t * share, share, 0)
    given = lax.dynamic_slice_in_dim(out_lines, (1 - t) * share, share, 0)
    out_lines = jnp.stack([kept, swapped(given, "tensor", 1)])
    across = jnp.concatenate(across, axis=0)
    across, out_lines, far, *rest = tied(across, out_lines, far, *results, *more, got[1])
    results, got = tuple(rest[:2]), rest[-1]
    lines += rest[2:-1]

    lines += along_z(got)
    out_weights = [out_lines] + [swapped(out_lines, "seq", d) for d in range(1, stretches)]
    last = swapped(across, "tensor", 1)
    results = mixed_in(across, 0, 3, results)
    results = mixed_in(far[0], 1, 1, results)
    results = mixed_in(far[1], 1, 2, results)
    mixed, lora = mixed_in(last, 1, 3, results)

    proj = projected(where, mixed, gathered, lines)

    def mine(array):
        return lax.dynamic_slice_in_dim(array, s * cols, cols, array.ndim - 1).reshape(-1, cols)

    normed, states = recurrence(
        prompt_extents, where, proj, lora, mine(fading_right_matrix), mine(feature_fading_speed), mine(self_reward),
        mine(cluster_scaling_vector),
    )

    sent = jnp.concatenate(
        [normed.reshape(stretches, rows, cols), states.reshape(stretches, -1, cols).astype(bf16)], axis=1
    )
    blocks = []
    for d in range(stretches):
        block = lax.dynamic_index_in_dim(sent, s ^ d, 0, keepdims=False)
        blocks.append(swapped(block, "seq", d) if d else block)
    blocks = jnp.stack(blocks)
    own_lines = blocks[:, :rows]
    far_lines = swapped(own_lines, "tensor", 1)
    hidden_out = finished(where, x, own_lines, far_lines, out_weights).reshape(reqs, span, width // cores)

    heads = cols // ATTEND_DIM
    states = blocks[jnp.arange(stretches) ^ s, rows:].reshape(stretches, reqs, ATTEND_DIM, heads, ATTEND_DIM)
    states = jnp.transpose(states, (1, 0, 3, 4, 2)).astype(f32)
    stretch_states = states.reshape(reqs, 1, stretches * heads, ATTEND_DIM * ATTEND_DIM)
    return (hidden_out, stretch_states)


def solution(mesh):
    in_specs = (
        P("req", "seq", None),
        P(),
        P(),
        P(),
        P(None, ("req", "seq"), "tensor"),
        P("tensor", ("req", "seq")),
        P(),
        P(None, "tensor"),
        P("tensor"),
        P("tensor"),
        P("tensor"),
        P("req"),
    )
    out_specs = (P("req", "seq", "tensor"), P("req", "seq", "tensor", None))
    return jax.shard_map(local, mesh=mesh, in_specs=in_specs, out_specs=out_specs, check_vma=False)
```

```python
import functools

import jax
import jax.numpy as jnp
import numpy as np
from jax import lax
from jax.experimental import pallas as pl
from jax.experimental.pallas import tpu as pltpu
from jax.sharding import PartitionSpec as P

ATTEND_DIM = 64
CHUNK = 64
LEVELS = 6
PREFIX = 8
PAST = 16

SMALL = pl.CostEstimate(flops=1024, bytes_accessed=1024, transcendentals=0)

eps = 1e-05
bf16 = jnp.bfloat16
f32 = jnp.float32


def dot(a, b):
    return jnp.dot(a, b, preferred_element_type=f32)


def dot_nt(a, b):
    return lax.dot_general(a, b, (((1,), (1,)), ((), ())), preferred_element_type=f32)


def dot_tn(a, b):
    return lax.dot_general(a, b, (((0,), (0,)), ((), ())), preferred_element_type=f32)


def swapped(value, axis, by):
    peers = lax.axis_size(axis)
    return lax.ppermute(value, axis, [(i, i ^ by) for i in range(peers)])


def vmem(mib):
    return pltpu.CompilerParams(vmem_limit_bytes=mib * 2**20)


def order_kernel(x_ref, gain_ref, coeff_ref, perm_ref, out_ref, coeff_out_ref, cur_ref):
    rows, width = x_ref.shape
    block = out_ref.shape[1]
    depth = 256

    @pl.when(pl.program_id(0) == 0)
    def _():
        x = x_ref[...].astype(f32)
        mean = jnp.mean(x, axis=-1, keepdims=True)
        centred = x - mean
        spread = jnp.mean(centred * centred, axis=-1, keepdims=True)
        cur_ref[:rows, :] = (centred * lax.rsqrt(spread + eps) * gain_ref[...]).astype(bf16)
        c = coeff_ref[...]
        high = c.astype(bf16)
        cur_ref[rows:, :] = jnp.concatenate([high, (c - high.astype(f32)).astype(bf16)], axis=0)

    perm = perm_ref[...]
    total = jnp.zeros((rows + 2 * PREFIX, block), f32)
    for k in range(width // depth):
        lines = lax.broadcasted_iota(jnp.int32, (depth, block), 0) + k * depth
        chosen = jnp.where(lines == perm, 1.0, 0.0).astype(bf16)
        total += dot(cur_ref[:, k * depth : (k + 1) * depth], chosen)
    out_ref[...] = total[:rows].astype(bf16)
    coeff_out_ref[...] = total[rows : rows + PREFIX] + total[rows + PREFIX :]


def ordered(x, gain, coeffs, perm):
    rows, width = x.shape
    block = 512
    return pl.pallas_call(
        order_kernel,
        grid=(width // block,),
        in_specs=[
            pl.BlockSpec((rows, width), lambda n: (0, 0)),
            pl.BlockSpec((1, width), lambda n: (0, 0)),
            pl.BlockSpec((PREFIX, width), lambda n: (0, 0)),
            pl.BlockSpec((1, block), lambda n: (0, n)),
        ],
        out_specs=[
            pl.BlockSpec((rows, block), lambda n: (0, n)),
            pl.BlockSpec((PREFIX, block), lambda n: (0, n)),
        ],
        out_shape=[
            jax.ShapeDtypeStruct((rows, width), bf16),
            jax.ShapeDtypeStruct((PREFIX, width), f32),
        ],
        scratch_shapes=[pltpu.VMEM((rows + 2 * PREFIX, width), bf16)],
        compiler_params=vmem(40),
        cost_estimate=SMALL,
    )(x, gain, coeffs, perm)


def mix_kernel(where_ref, act_ref, coeff_ref, left_ref, *refs):
    mixed_ref, lora_ref, inner_ref = refs[-3:]
    rows, block = mixed_ref.shape[-2:]
    width = 512
    n = pl.program_id(0)
    inner = jnp.zeros(inner_ref.shape, f32)
    for c in range(block // width):
        cols = slice(c * width, (c + 1) * width)
        cur = act_ref[PAST:, cols]
        delta = pltpu.roll(act_ref[:, cols].astype(f32), 1, 0)[PAST:].astype(bf16) - cur
        for j in range(3):
            mixed_ref[j, 0, 0, :, cols] = cur + delta * coeff_ref[j : j + 1, cols].astype(bf16)
        inner += dot(cur + delta * coeff_ref[3:4, cols].astype(bf16), left_ref[cols, :])

    @pl.when(n == 0)
    def _():
        inner_ref[...] = inner

    @pl.when(n > 0)
    def _():
        inner_ref[...] += inner

    @pl.when(n == pl.num_programs(0) - 1)
    def _():
        lora_ref[0, 0] = jnp.tanh(inner_ref[...]).astype(bf16)


def shifted(where, act, coeffs, left, side, apart, stretches, earlier):
    span, width = act.shape[0] - PAST, act.shape[1]
    inner = left.shape[1]
    block = 1024
    kept = pl.BlockSpec(memory_space=pl.ANY)
    return pl.pallas_call(
        mix_kernel,
        grid_spec=pltpu.PrefetchScalarGridSpec(
            num_scalar_prefetch=1,
            grid=(width // block,),
            in_specs=[
                pl.BlockSpec((span + PAST, block), lambda n, w: (0, n)),
                pl.BlockSpec((PREFIX, block), lambda n, w: (0, n)),
                pl.BlockSpec((block, inner), lambda n, w: (n, 0)),
            ]
            + [kept] * len(earlier),
            out_specs=[
                pl.BlockSpec((3, 1, 1, span, block), lambda n, w: (0, side, w[0] ^ apart, 0, n)),
                pl.BlockSpec((1, 1, span, inner), lambda n, w: (side, w[0] ^ apart, 0, 0)),
            ],
            scratch_shapes=[pltpu.VMEM((span, inner), f32)],
        ),
        out_shape=[
            jax.ShapeDtypeStruct((3, 2, stretches, span, width), bf16),
            jax.ShapeDtypeStruct((2, stretches, span, inner), bf16),
        ],
        input_output_aliases={4: 0, 5: 1} if earlier else {},
        compiler_params=vmem(32),
        cost_estimate=SMALL,
    )(where, act, coeffs, left, *earlier)


def project_kernel(where_ref, act_ref, *refs):
    *hops, out_ref, lines_ref = refs
    stretches, _, depth, _ = hops[0].shape
    reqs = (len(hops) + 1) // 2

    def place(hop_ref, r):
        for d in range(stretches):
            at = (r * stretches + (where_ref[0] ^ d)) * depth
            lines_ref[pl.ds(pl.multiple_of(at, depth), depth), :] = hop_ref[d, 0]

    @pl.when(pl.program_id(1) == 0)
    def _():
        me = where_ref[2]
        place(hops[0], me)
        for hop in range(1, reqs):

            @pl.when(me >= hop)
            def _():
                place(hops[2 * hop - 1], me - hop)

            @pl.when(me + hop < reqs)
            def _():
                place(hops[2 * hop], me + hop)

    act = act_ref[0, 0].reshape(-1, act_ref.shape[-1])
    out_ref[0, 0] = dot(act, lines_ref[...]).astype(bf16).reshape(out_ref.shape[2:])


def projected(where, mixed, hops):
    stretches, kinds, depth, cols = hops[0].shape
    _, sides, _, span, width = mixed.shape
    if depth % 128:
        (lines,) = hops[1:]
        lines = lines[:, jnp.arange(stretches) ^ where[0]]
        lines = jnp.transpose(lines, (2, 0, 1, 3, 4)).reshape(kinds, width, cols)
        return jnp.einsum("jxbtk,jkc->jxbtc", mixed, lines, preferred_element_type=f32).astype(bf16)
    return pl.pallas_call(
        project_kernel,
        grid_spec=pltpu.PrefetchScalarGridSpec(
            num_scalar_prefetch=1,
            grid=(kinds, sides),
            in_specs=[pl.BlockSpec((1, 1, stretches, span, width), lambda j, m, w: (j, m, 0, 0, 0))]
            + [pl.BlockSpec((stretches, 1, depth, cols), lambda j, m, w: (0, j, 0, 0))] * len(hops),
            out_specs=pl.BlockSpec((1, 1, stretches, span, cols), lambda j, m, w: (j, m, 0, 0, 0)),
            scratch_shapes=[pltpu.VMEM((width, cols), bf16)],
        ),
        out_shape=jax.ShapeDtypeStruct((kinds, sides, stretches, span, cols), bf16),
        compiler_params=vmem(60),
        cost_estimate=SMALL,
    )(where, mixed, *hops)


def decay_sums():
    place = np.arange(CHUNK)
    of, by = place[:, None], place[None, :]
    parts = []
    for level in range(LEVELS):
        half = 1 << level
        middle = (of // (2 * half)) * 2 * half + half - 1
        later = (of % (2 * half)) >= half
        parts.append(np.where(later, (by > middle) & (by < of), (by > of) & (by <= middle)))
    parts += [by < of, by > of, np.ones((8, CHUNK), bool)]
    sums = np.concatenate(parts).astype(np.float32)
    return np.concatenate([sums, sums], axis=1)


def pair_levels(heads):
    of, by = np.arange(CHUNK)[:, None], np.arange(CHUNK)[None, :]
    level = np.full((CHUNK, CHUNK), -1.0, np.float32)
    for bit in range(LEVELS):
        level[((of ^ by) >> bit) == 1] = bit
    return np.tile(np.where(of > by, level, -1.0).astype(np.float32), (1, heads))


def wkv_kernel(
    extent_ref, where_ref, proj_ref, lora_ref, right_ref, speed_ref, reward_ref, scale_ref, sums_ref, level_ref,
    same_ref, normed_ref, state_ref, memory_ref,
):
    step = pl.program_id(0)
    tokens, cols = proj_ref.shape[3:]
    heads = cols // ATTEND_DIM
    per_block = pl.num_programs(0) // lax.axis_size("seq")
    same = same_ref[...]
    same_f32 = same.astype(f32)
    level = level_ref[...]

    @pl.when(step == 0)
    def _():
        memory_ref[...] = jnp.zeros_like(memory_ref)

    memories = [memory_ref[0], memory_ref[1]]
    for sub in range(tokens // CHUNK):
        lines = slice(sub * CHUNK, (sub + 1) * CHUNK)
        at = step * tokens + sub * CHUNK + lax.broadcasted_iota(jnp.int32, (CHUNK, cols), 0)
        for side in range(2):
            prompt = where_ref[1] ^ side
            valid = jnp.where(at < extent_ref[prompt], 1.0, 0.0)
            r = proj_ref[0, side, 0, lines].astype(f32)
            k = proj_ref[1, side, 0, lines].astype(f32) * valid
            v = proj_ref[2, side, 0, lines]
            decay = -speed_ref[...] * jnp.exp(dot(lora_ref[side, 0, lines], right_ref[...])) * valid
            high = decay.astype(bf16)
            low = (decay - high.astype(f32)).astype(bf16)
            kept = jnp.exp(dot(sums_ref[...], jnp.concatenate([high, low], axis=0)))
            scores = jnp.zeros((CHUNK, heads * CHUNK), f32)
            for bit in range(LEVELS):
                part = kept[bit * CHUNK : (bit + 1) * CHUNK]
                lookup = (k * part).astype(bf16)
                lookup = jnp.concatenate([lookup] * heads, axis=0) * same
                found = dot_nt((r * part).astype(bf16), lookup)
                scores = jnp.where(level == bit, found, scores)
            v_heads = jnp.concatenate([v] * heads, axis=0) * same
            memory = memories[side]
            from_start = (r * kept[LEVELS * CHUNK : (LEVELS + 1) * CHUNK]).astype(bf16)
            to_end = (k * kept[(LEVELS + 1) * CHUNK : (LEVELS + 2) * CHUNK]).astype(bf16)
            own = dot((r * reward_ref[...] * k).astype(bf16), same)
            y = dot_nt(from_start, memory.astype(bf16)) + dot(scores.astype(bf16), v_heads)
            y += own * v.astype(f32)
            whole = kept[(LEVELS + 2) * CHUNK : (LEVELS + 2) * CHUNK + 1]
            memories[side] = memory * whole + same_f32 * dot_tn(v, to_end)

            y_high = y.astype(bf16)
            y_low = (y - y_high.astype(f32)).astype(bf16)
            centred = y - (dot(y_high, same) + dot(y_low, same)) * (1.0 / ATTEND_DIM)
            spread = dot((centred * centred).astype(bf16), same) * (1.0 / ATTEND_DIM)
            normed = centred * lax.rsqrt(spread + eps) * scale_ref[...] * valid
            normed_ref[0, pl.ds(prompt, 1), lines] = normed.astype(bf16)[None]
    for side in range(2):
        memory_ref[side] = memories[side]

    @pl.when(step % per_block == per_block - 1)
    def _():
        for side in range(2):
            folded = memory_ref[side, :ATTEND_DIM]
            for h in range(1, heads):
                folded += memory_ref[side, h * ATTEND_DIM : (h + 1) * ATTEND_DIM]
            state_ref[0, pl.ds(where_ref[1] ^ side, 1)] = folded[None]


def recurrence(extents, where, proj, lora, right, speed, reward, scale):
    _, reqs, stretches, span, cols = proj.shape
    inner = lora.shape[-1]
    heads = cols // ATTEND_DIM
    tokens = 2 * CHUNK
    per_block = span // tokens
    sums = jnp.asarray(decay_sums(), bf16)
    level = jnp.asarray(pair_levels(heads), f32)
    head = np.arange(cols) // ATTEND_DIM
    same = jnp.asarray(head[:, None] == head[None, :], bf16)

    def fixed(array):
        return pl.BlockSpec(array.shape, lambda c, e, w: (0,) * array.ndim)

    tables = (right, speed, reward, scale, sums, level, same)
    return pl.pallas_call(
        wkv_kernel,
        grid_spec=pltpu.PrefetchScalarGridSpec(
            num_scalar_prefetch=2,
            grid=(stretches * per_block,),
            in_specs=[
                pl.BlockSpec((3, reqs, 1, tokens, cols), lambda c, e, w: (0, 0, c // per_block, c % per_block, 0)),
                pl.BlockSpec((reqs, 1, tokens, inner), lambda c, e, w: (0, c // per_block, c % per_block, 0)),
            ]
            + [fixed(a) for a in tables],
            out_specs=[
                pl.BlockSpec((1, reqs, tokens, cols), lambda c, e, w: (c // per_block, 0, c % per_block, 0)),
                pl.BlockSpec((1, reqs, ATTEND_DIM, cols), lambda c, e, w: (c // per_block, 0, 0, 0)),
            ],
            scratch_shapes=[pltpu.VMEM((reqs, cols, cols), f32)],
        ),
        out_shape=[
            jax.ShapeDtypeStruct((stretches, reqs, span, cols), bf16),
            jax.ShapeDtypeStruct((stretches, reqs, ATTEND_DIM, cols), f32),
        ],
        compiler_params=vmem(40),
        cost_estimate=SMALL,
    )(extents, where, proj, lora, *tables)


def finish_kernel(where_ref, x_ref, own_ref, far_ref, *refs):
    *weights, out_ref = refs
    stretches, rows, cols = own_ref.shape
    chunk = weights[0].shape[-1]
    for e in range(stretches):
        total = x_ref[:, pl.ds(pl.multiple_of((where_ref[0] ^ e) * chunk, chunk), chunk)].astype(f32)
        for side, lines_ref in enumerate((own_ref, far_ref)):
            w_ref = weights[e]
            for d in range(stretches):
                at = pl.ds(pl.multiple_of((where_ref[0] ^ d) * cols, cols), cols)
                total += dot(lines_ref[d], w_ref[side, 0, at, :])
        out_ref[:, pl.ds(pl.multiple_of((where_ref[0] ^ e) * chunk, chunk), chunk)] = total.astype(bf16)


def finished(where, x, own, far, weights):
    stretches, rows, cols = own.shape
    width = x.shape[1]
    _, groups, depth, chunk = weights[0].shape
    share = groups * stretches * chunk
    if chunk % 128:
        order = jnp.arange(stretches) ^ where[0]
        total = lax.dynamic_slice_in_dim(x, where[1] * share, share, 1).astype(f32)
        for side, lines in enumerate((own, far)):
            w = jnp.transpose(jnp.stack([w[side] for w in weights])[order], (2, 1, 0, 3)).reshape(depth, share)
            lines = jnp.transpose(lines[order], (1, 0, 2)).reshape(rows, depth)
            total += dot(lines, w)
        return total.astype(bf16)
    block = stretches * chunk
    whole = pl.BlockSpec((stretches, rows, cols), lambda g, w: (0, 0, 0))
    return pl.pallas_call(
        finish_kernel,
        grid_spec=pltpu.PrefetchScalarGridSpec(
            num_scalar_prefetch=1,
            grid=(groups,),
            in_specs=[pl.BlockSpec((rows, block), lambda g, w: (0, w[1] * groups + g)), whole, whole]
            + [pl.BlockSpec((2, 1, depth, chunk), lambda g, w: (0, g, 0, 0))] * len(weights),
            out_specs=pl.BlockSpec((rows, block), lambda g, w: (0, g)),
        ),
        out_shape=jax.ShapeDtypeStruct((rows, share), bf16),
        compiler_params=vmem(48),
        cost_estimate=SMALL,
    )(where, x, own, far, *weights)


def moved(value, axis, by):
    peers = lax.axis_size(axis)
    return lax.ppermute(value, axis, [(i, i + by) for i in range(peers) if 0 <= i + by < peers])


def local(
    incoming_activations,
    standardize_scaling,
    lagged_blending_weights,
    learner_line_permutation,
    learner_acceptor_lookup_slices,
    learner_projection_slices,
    fading_left_matrix,
    fading_right_matrix,
    feature_fading_speed,
    self_reward,
    cluster_scaling_vector,
    prompt_extents,
):
    reqs, span, width = incoming_activations.shape
    rows = reqs * span
    stretches = lax.axis_size("seq")
    cores = lax.axis_size("tensor")
    groups = lax.axis_size("req")
    assert reqs == cores == 2 and stretches == 4
    local_width = feature_fading_speed.shape[0]
    cols = local_width // stretches
    t, s = lax.axis_index("tensor"), lax.axis_index("seq")
    where = jnp.stack([s, t, lax.axis_index("req")]).astype(jnp.int32)

    x = incoming_activations.reshape(rows, width)
    own_x = lax.dynamic_slice_in_dim(x, t * span, span, 0)
    past = moved(own_x[span - PAST :], "seq", 1)
    pieces = [
        lax.dynamic_slice_in_dim(learner_acceptor_lookup_slices, (s ^ d) * cols, cols, 2).astype(bf16)
        for d in range(stretches)
    ]
    out_half = learner_projection_slices.astype(bf16)
    out_lines = lax.all_gather(out_half, "req", axis=0, tiled=False)
    got = [swapped(pieces[d], "seq", d) for d in range(1, stretches)]

    def tied(*values):
        return lax.optimization_barrier(values)

    own_x, past, *_ = tied(own_x, past, out_half, *pieces)
    coeffs = jnp.pad(lagged_blending_weights, ((0, PREFIX - 4), (0, 0)))
    act, coeffs = ordered(
        jnp.concatenate([past, own_x], axis=0),
        standardize_scaling.reshape(1, width),
        coeffs,
        learner_line_permutation.reshape(1, width),
    )
    act, perm, *got = tied(act, learner_line_permutation, *got)
    lines = jnp.stack([pieces[0], *got])
    chained = groups == 4

    def mixed_in(values, side, apart, earlier):
        return shifted(where, values, coeffs, left, side, apart, stretches, earlier)

    left = fading_left_matrix[perm]
    near, other = swapped(act, "seq", 1), swapped(act, "seq", 2)
    hops = [moved(lines, "req", 1), moved(lines, "req", -1)] if chained else [lax.all_gather(lines, "req", axis=0)]
    results = mixed_in(act, 0, 0, ())
    results = mixed_in(swapped(act, "tensor", 1), 1, 0, results)
    near, other, out_lines, act, *rest = tied(near, other, out_lines, act, *results, *hops)
    results, hops = tuple(rest[:2]), rest[2:]

    across = swapped(act, "seq", 3)
    if chained:
        hops += [moved(hops[0], "req", 1), moved(hops[1], "req", -1)]
    far = swapped(jnp.stack([near, other]), "tensor", 1)
    results = mixed_in(near, 0, 1, results)
    results = mixed_in(other, 0, 2, results)
    share = groups // cores
    kept = lax.dynamic_slice_in_dim(out_lines, t * share, share, 0)
    given = lax.dynamic_slice_in_dim(out_lines, (1 - t) * share, share, 0)
    out_lines = jnp.stack([kept, swapped(given, "tensor", 1)])
    across, out_lines, far, *rest = tied(across, out_lines, far, *results, *hops)
    results, hops = tuple(rest[:2]), rest[2:]

    if chained:
        hops += [moved(hops[2], "req", 1), moved(hops[3], "req", -1)]
    near, other = swapped(out_lines, "seq", 1), swapped(out_lines, "seq", 2)
    last = swapped(across, "tensor", 1)
    results = mixed_in(across, 0, 3, results)
    results = mixed_in(far[0], 1, 1, results)
    results = mixed_in(far[1], 1, 2, results)
    results = mixed_in(last, 1, 3, results)
    mixed, lora, out_lines, *hops = tied(*results, out_lines, *hops)
    across = swapped(out_lines, "seq", 3)

    proj = projected(where, mixed, [lines, *hops])

    def mine(array):
        return lax.dynamic_slice_in_dim(array, s * cols, cols, array.ndim - 1).reshape(-1, cols)

    normed, states = recurrence(
        prompt_extents, where, proj, lora, mine(fading_right_matrix), mine(feature_fading_speed), mine(self_reward),
        mine(cluster_scaling_vector),
    )

    normed, states, near, other, across = tied(normed, states, near, other, across)
    sent = jnp.concatenate(
        [normed.reshape(stretches, rows, cols), states.reshape(stretches, -1, cols).astype(bf16)], axis=1
    )
    blocks = []
    for d in range(stretches):
        block = lax.dynamic_index_in_dim(sent, s ^ d, 0, keepdims=False)
        blocks.append(swapped(block, "seq", d) if d else block)
    own_lines = jnp.stack([block[:rows] for block in blocks])
    far_lines = swapped(own_lines, "tensor", 1)
    out_weights = [out_lines, near, other, across]
    hidden_out = finished(where, x, own_lines, far_lines, out_weights).reshape(reqs, span, width // cores)

    heads = cols // ATTEND_DIM
    states = jnp.stack([block[rows:] for block in blocks]).reshape(2, 2, reqs, ATTEND_DIM, heads, ATTEND_DIM)
    states = jnp.where(s % 2 == 1, states[:, ::-1], states)
    states = jnp.where(s // 2 == 1, states[::-1], states)
    states = jnp.transpose(states, (2, 0, 1, 4, 5, 3)).astype(f32)
    stretch_states = states.reshape(reqs, 1, stretches * heads, ATTEND_DIM * ATTEND_DIM)
    return (hidden_out, stretch_states)


def solution(mesh):
    in_specs = (
        P("req", "seq", None),
        P(),
        P(),
        P(),
        P(None, ("req", "seq"), "tensor"),
        P("tensor", ("req", "seq")),
        P(),
        P(None, "tensor"),
        P("tensor"),
        P("tensor"),
        P("tensor"),
        P("req"),
    )
    out_specs = (P("req", "seq", "tensor"), P("req", "seq", "tensor", None))
    return jax.shard_map(local, mesh=mesh, in_specs=in_specs, out_specs=out_specs, check_vma=False)
```

```python
import functools

import jax
import jax.numpy as jnp
import numpy as np
from jax import lax
from jax.experimental import pallas as pl
from jax.experimental.pallas import tpu as pltpu
from jax.sharding import PartitionSpec as P

ATTEND_DIM = 64
CHUNK = 64
LEVELS = 6
PREFIX = 8
PAST = 16

SMALL = pl.CostEstimate(flops=1024, bytes_accessed=1024, transcendentals=0)

eps = 1e-05
bf16 = jnp.bfloat16
f32 = jnp.float32


def dot(a, b):
    return jnp.dot(a, b, preferred_element_type=f32)


def dot_nt(a, b):
    return lax.dot_general(a, b, (((1,), (1,)), ((), ())), preferred_element_type=f32)


def dot_tn(a, b):
    return lax.dot_general(a, b, (((0,), (0,)), ((), ())), preferred_element_type=f32)


def swapped(value, axis, by):
    peers = lax.axis_size(axis)
    return lax.ppermute(value, axis, [(i, i ^ by) for i in range(peers)])


def vmem(mib):
    return pltpu.CompilerParams(vmem_limit_bytes=mib * 2**20)


def order_kernel(x_ref, gain_ref, coeff_ref, perm_ref, out_ref, coeff_out_ref, cur_ref):
    rows, width = x_ref.shape
    block = out_ref.shape[1]
    depth = 256

    @pl.when(pl.program_id(0) == 0)
    def _():
        x = x_ref[...].astype(f32)
        mean = jnp.mean(x, axis=-1, keepdims=True)
        centred = x - mean
        spread = jnp.mean(centred * centred, axis=-1, keepdims=True)
        cur_ref[:rows, :] = (centred * lax.rsqrt(spread + eps) * gain_ref[...]).astype(bf16)
        c = coeff_ref[...]
        high = c.astype(bf16)
        cur_ref[rows:, :] = jnp.concatenate([high, (c - high.astype(f32)).astype(bf16)], axis=0)

    perm = perm_ref[...]
    high, low = perm // depth, (perm % depth).astype(bf16)
    lines = lax.broadcasted_iota(jnp.int32, (depth, block), 0).astype(bf16)
    one, none = jnp.ones((depth, block), bf16), jnp.zeros((depth, block), bf16)
    total = jnp.zeros((rows + 2 * PREFIX, block), f32)
    for k in range(width // depth):
        mine = jnp.where(high == k, low, jnp.full_like(low, -1.0))
        total += dot(cur_ref[:, k * depth : (k + 1) * depth], jnp.where(lines == mine, one, none))
    out_ref[...] = total[:rows].astype(bf16)
    coeff_out_ref[...] = total[rows : rows + PREFIX] + total[rows + PREFIX :]


def ordered(x, gain, coeffs, perm):
    rows, width = x.shape
    block = 512
    return pl.pallas_call(
        order_kernel,
        grid=(width // block,),
        in_specs=[
            pl.BlockSpec((rows, width), lambda n: (0, 0)),
            pl.BlockSpec((1, width), lambda n: (0, 0)),
            pl.BlockSpec((PREFIX, width), lambda n: (0, 0)),
            pl.BlockSpec((1, block), lambda n: (0, n)),
        ],
        out_specs=[
            pl.BlockSpec((rows, block), lambda n: (0, n)),
            pl.BlockSpec((PREFIX, block), lambda n: (0, n)),
        ],
        out_shape=[
            jax.ShapeDtypeStruct((rows, width), bf16),
            jax.ShapeDtypeStruct((PREFIX, width), f32),
        ],
        scratch_shapes=[pltpu.VMEM((rows + 2 * PREFIX, width), bf16)],
        compiler_params=vmem(40),
        cost_estimate=SMALL,
    )(x, gain, coeffs, perm)


def mix_kernel(where_ref, act_ref, coeff_ref, left_ref, *refs):
    mixed_ref, lora_ref, inner_ref = refs[-3:]
    rows, block = mixed_ref.shape[-2:]
    width = 512
    n = pl.program_id(0)
    inner = jnp.zeros(inner_ref.shape, f32)
    for c in range(block // width):
        cols = slice(c * width, (c + 1) * width)
        cur = act_ref[PAST:, cols]
        delta = pltpu.roll(act_ref[:, cols].astype(f32), 1, 0)[PAST:].astype(bf16) - cur
        for j in range(3):
            mixed_ref[j, 0, 0, :, cols] = cur + delta * coeff_ref[j : j + 1, cols].astype(bf16)
        inner += dot(cur + delta * coeff_ref[3:4, cols].astype(bf16), left_ref[cols, :])

    @pl.when(n == 0)
    def _():
        inner_ref[...] = inner

    @pl.when(n > 0)
    def _():
        inner_ref[...] += inner

    @pl.when(n == pl.num_programs(0) - 1)
    def _():
        lora_ref[0, 0] = jnp.tanh(inner_ref[...]).astype(bf16)


def shifted(where, act, coeffs, left, side, apart, stretches, earlier):
    span, width = act.shape[0] - PAST, act.shape[1]
    inner = left.shape[1]
    block = 1024
    kept = pl.BlockSpec(memory_space=pl.ANY)
    return pl.pallas_call(
        mix_kernel,
        grid_spec=pltpu.PrefetchScalarGridSpec(
            num_scalar_prefetch=1,
            grid=(width // block,),
            in_specs=[
                pl.BlockSpec((span + PAST, block), lambda n, w: (0, n)),
                pl.BlockSpec((PREFIX, block), lambda n, w: (0, n)),
                pl.BlockSpec((block, inner), lambda n, w: (n, 0)),
            ]
            + [kept] * len(earlier),
            out_specs=[
                pl.BlockSpec((3, 1, 1, span, block), lambda n, w: (0, side, w[0] ^ apart, 0, n)),
                pl.BlockSpec((1, 1, span, inner), lambda n, w: (side, w[0] ^ apart, 0, 0)),
            ],
            scratch_shapes=[pltpu.VMEM((span, inner), f32)],
        ),
        out_shape=[
            jax.ShapeDtypeStruct((3, 2, stretches, span, width), bf16),
            jax.ShapeDtypeStruct((2, stretches, span, inner), bf16),
        ],
        input_output_aliases={4: 0, 5: 1} if earlier else {},
        compiler_params=vmem(32),
        cost_estimate=SMALL,
    )(where, act, coeffs, left, *earlier)


def project_kernel(where_ref, act_ref, *refs):
    *hops, out_ref, lines_ref = refs
    stretches, _, depth, _ = hops[0].shape
    reqs = lines_ref.shape[0] // (stretches * depth)
    reach = len(hops) // 2

    def place(r, values):
        for d in range(stretches):
            at = (r * stretches + (where_ref[0] ^ d)) * depth
            lines_ref[pl.ds(pl.multiple_of(at, depth), depth), :] = values(d)

    @pl.when(pl.program_id(1) == 0)
    def _():
        me = where_ref[2]
        place(me, lambda d: hops[0][d, 0])
        for hop in range(1, reqs):
            for r, ref in ((me - hop, 2 * hop - 1), (me + hop, 2 * hop)):

                @pl.when((r >= 0) & (r < reqs))
                def _():
                    if hop > reach:
                        place(r, lambda d: jnp.zeros_like(hops[0][d, 0]))
                    else:
                        place(r, lambda d: hops[ref][d, 0])

    act = act_ref[0, 0].reshape(-1, act_ref.shape[-1])
    out_ref[0, 0] = dot(act, lines_ref[...]).reshape(out_ref.shape[2:])


def last_kernel(where_ref, act_ref, part_ref, below_ref, above_ref, out_ref, lines_ref):
    stretches, _, depth, _ = below_ref.shape

    @pl.when(pl.program_id(1) == 0)
    def _():
        for d in range(stretches):
            at = (where_ref[0] ^ d) * depth
            lines_ref[pl.ds(pl.multiple_of(at, depth), depth), :] = below_ref[d, 0] + above_ref[d, 0]

    act = act_ref[0, 0].reshape(-1, act_ref.shape[-1])
    out_ref[0, 0] = (part_ref[0, 0] + dot(act, lines_ref[...]).reshape(out_ref.shape[2:])).astype(bf16)


def projected(where, mixed, hops):
    stretches, kinds, depth, cols = hops[0].shape
    _, sides, _, span, width = mixed.shape
    return pl.pallas_call(
        project_kernel,
        grid_spec=pltpu.PrefetchScalarGridSpec(
            num_scalar_prefetch=1,
            grid=(kinds, sides),
            in_specs=[pl.BlockSpec((1, 1, stretches, span, width), lambda j, m, w: (j, m, 0, 0, 0))]
            + [pl.BlockSpec((stretches, 1, depth, cols), lambda j, m, w: (0, j, 0, 0))] * len(hops),
            out_specs=pl.BlockSpec((1, 1, stretches, span, cols), lambda j, m, w: (j, m, 0, 0, 0)),
            scratch_shapes=[pltpu.VMEM((width, cols), bf16)],
        ),
        out_shape=jax.ShapeDtypeStruct((kinds, sides, stretches, span, cols), f32),
        compiler_params=vmem(60),
        cost_estimate=SMALL,
    )(where, mixed, *hops)


def completed(where, mixed, part, below, above):
    stretches, kinds, depth, cols = below.shape
    _, sides, _, span, width = mixed.shape
    share = stretches * depth
    last = width // share - 1

    def act_block(j, m, w):
        return (j, m, 0, 0, jnp.where(w[2] == last, 0, last))

    block = pl.BlockSpec((1, 1, stretches, span, cols), lambda j, m, w: (j, m, 0, 0, 0))
    line_block = pl.BlockSpec((stretches, 1, depth, cols), lambda j, m, w: (0, j, 0, 0))
    return pl.pallas_call(
        last_kernel,
        grid_spec=pltpu.PrefetchScalarGridSpec(
            num_scalar_prefetch=1,
            grid=(kinds, sides),
            in_specs=[pl.BlockSpec((1, 1, stretches, span, share), act_block), block, line_block, line_block],
            out_specs=block,
            scratch_shapes=[pltpu.VMEM((share, cols), bf16)],
        ),
        out_shape=jax.ShapeDtypeStruct((kinds, sides, stretches, span, cols), bf16),
        compiler_params=vmem(60),
        cost_estimate=SMALL,
    )(where, mixed, part, below, above)


def projected_whole(where, mixed, lines):
    _, stretches, kinds, depth, cols = lines.shape
    lines = lines[:, jnp.arange(stretches) ^ where[0]]
    lines = jnp.transpose(lines, (2, 0, 1, 3, 4)).reshape(kinds, mixed.shape[-1], cols)
    return jnp.einsum("jxbtk,jkc->jxbtc", mixed, lines, preferred_element_type=f32).astype(bf16)


def decay_sums():
    place = np.arange(CHUNK)
    of, by = place[:, None], place[None, :]
    parts = []
    for level in range(LEVELS):
        half = 1 << level
        middle = (of // (2 * half)) * 2 * half + half - 1
        later = (of % (2 * half)) >= half
        parts.append(np.where(later, (by > middle) & (by < of), (by > of) & (by <= middle)))
    parts += [by < of, by > of, np.ones((8, CHUNK), bool)]
    sums = np.concatenate(parts).astype(np.float32)
    return np.concatenate([sums, sums], axis=1)


def pair_levels(heads):
    of, by = np.arange(CHUNK)[:, None], np.arange(CHUNK)[None, :]
    level = np.full((CHUNK, CHUNK), -1.0, np.float32)
    for bit in range(LEVELS):
        level[((of ^ by) >> bit) == 1] = bit
    return np.tile(np.where(of > by, level, -1.0).astype(np.float32), (1, heads))


def wkv_kernel(
    extent_ref, where_ref, proj_ref, lora_ref, right_ref, speed_ref, reward_ref, scale_ref, sums_ref, level_ref,
    same_ref, normed_ref, state_ref, memory_ref, *, prompt,
):
    step = pl.program_id(0)
    tokens, cols = proj_ref.shape[3:]
    heads = cols // ATTEND_DIM
    same = same_ref[...]
    same_f32 = same.astype(f32)
    level = level_ref[...]

    @pl.when(step == 0)
    def _():
        memory_ref[...] = jnp.zeros_like(memory_ref)

    at = step * tokens + lax.broadcasted_iota(jnp.int32, (tokens, cols), 0)
    valid = jnp.where(at < extent_ref[prompt], 1.0, 0.0)
    r = proj_ref[0, 0, 0]
    k = proj_ref[1, 0, 0] * valid.astype(bf16)
    v = proj_ref[2, 0, 0]
    decay = -speed_ref[...] * jnp.exp(dot(lora_ref[0, 0], right_ref[...])) * valid
    high = decay.astype(bf16)
    low = (decay - high.astype(f32)).astype(bf16)
    own = dot((r.astype(f32) * reward_ref[...] * k.astype(f32)).astype(bf16), same) * v.astype(f32)

    memory = memory_ref[...]
    rows = []
    for sub in range(tokens // CHUNK):
        lines = slice(sub * CHUNK, (sub + 1) * CHUNK)
        r_sub, k_sub, v_sub = r[lines], k[lines], v[lines]
        kept = jnp.exp(dot(sums_ref[...], jnp.concatenate([high[lines], low[lines]], axis=0)))
        scores = jnp.zeros((CHUNK, heads * CHUNK), f32)
        for bit in range(LEVELS):
            part = kept[bit * CHUNK : (bit + 1) * CHUNK].astype(bf16)
            lookup = jnp.concatenate([k_sub * part] * heads, axis=0) * same
            scores = jnp.where(level == bit, dot_nt(r_sub * part, lookup), scores)
        v_heads = jnp.concatenate([v_sub] * heads, axis=0) * same
        from_start = r_sub * kept[LEVELS * CHUNK : (LEVELS + 1) * CHUNK].astype(bf16)
        to_end = k_sub * kept[(LEVELS + 1) * CHUNK : (LEVELS + 2) * CHUNK].astype(bf16)
        whole = kept[(LEVELS + 2) * CHUNK : (LEVELS + 2) * CHUNK + 1]
        rows.append(dot_nt(from_start, memory.astype(bf16)) + dot(scores.astype(bf16), v_heads))
        memory = memory * whole + same_f32 * dot_tn(v_sub, to_end)
    memory_ref[...] = memory
    folded = memory[:ATTEND_DIM]
    for h in range(1, heads):
        folded += memory[h * ATTEND_DIM : (h + 1) * ATTEND_DIM]
    state_ref[0] = folded

    y = jnp.concatenate(rows, axis=0) + own
    y_high = y.astype(bf16)
    y_low = (y - y_high.astype(f32)).astype(bf16)
    centred = y - (dot(y_high, same) + dot(y_low, same)) * (1.0 / ATTEND_DIM)
    spread = dot((centred * centred).astype(bf16), same) * (1.0 / ATTEND_DIM)
    normed_ref[0] = (centred * lax.rsqrt(spread + eps) * scale_ref[...] * valid).astype(bf16)


def recurrence(prompt, extents, where, proj, lora, right, speed, reward, scale):
    _, _, stretches, span, cols = proj.shape
    inner = lora.shape[-1]
    heads = cols // ATTEND_DIM
    sums = jnp.asarray(decay_sums(), bf16)
    level = jnp.asarray(pair_levels(heads), f32)
    head = np.arange(cols) // ATTEND_DIM
    same = jnp.asarray(head[:, None] == head[None, :], bf16)

    def fixed(array):
        return pl.BlockSpec(array.shape, lambda c, e, w: (0,) * array.ndim)

    tables = (right, speed, reward, scale, sums, level, same)
    return pl.pallas_call(
        functools.partial(wkv_kernel, prompt=prompt),
        grid_spec=pltpu.PrefetchScalarGridSpec(
            num_scalar_prefetch=2,
            grid=(stretches,),
            in_specs=[
                pl.BlockSpec((3, 1, 1, span, cols), lambda c, e, w: (0, w[1] ^ prompt, c, 0, 0)),
                pl.BlockSpec((1, 1, span, inner), lambda c, e, w: (w[1] ^ prompt, c, 0, 0)),
            ]
            + [fixed(a) for a in tables],
            out_specs=[
                pl.BlockSpec((1, span, cols), lambda c, e, w: (c, 0, 0)),
                pl.BlockSpec((1, ATTEND_DIM, cols), lambda c, e, w: (c, 0, 0)),
            ],
            scratch_shapes=[pltpu.VMEM((cols, cols), f32)],
        ),
        out_shape=[
            jax.ShapeDtypeStruct((stretches, span, cols), bf16),
            jax.ShapeDtypeStruct((stretches, ATTEND_DIM, cols), f32),
        ],
        compiler_params=vmem(40),
        cost_estimate=SMALL,
    )(extents, where, proj, lora, *tables)


def finish_kernel(where_ref, x_ref, own_ref, far_ref, *refs):
    weights, out_ref = refs[:4], refs[-1]
    stretches, rows, cols = own_ref.shape
    chunk = weights[0].shape[-1]
    for e in range(stretches):
        places = pl.ds(pl.multiple_of((where_ref[0] ^ e) * chunk, chunk), chunk)
        total = x_ref[:, places].astype(f32)
        for side, lines_ref in enumerate((own_ref, far_ref)):
            for d in range(stretches):
                at = pl.ds(pl.multiple_of((where_ref[0] ^ d) * cols, cols), cols)
                total += dot(lines_ref[d], weights[e][side, 0, at, :])
        out_ref[0, :, places] = total.astype(bf16)


def finished(prompt, prompts, where, x, own, far, weights, earlier):
    stretches, rows, cols = own.shape
    _, groups, depth, chunk = weights[0].shape
    share = groups * stretches * chunk
    if chunk % 128:
        order = jnp.arange(stretches) ^ where[0]
        total = lax.dynamic_slice(x, (prompt * rows, where[1] * share), (rows, share)).astype(f32)
        for side, lines in enumerate((own, far)):
            w = jnp.stack([w[side] for w in weights])[order]
            w = jnp.transpose(w, (2, 1, 0, 3)).reshape(depth, share)
            lines = jnp.transpose(lines[order], (1, 0, 2)).reshape(rows, depth)
            total += dot(lines, w)
        return jnp.concatenate([*earlier, total.astype(bf16)[None]], axis=0)
    block = stretches * chunk
    whole = pl.BlockSpec((stretches, rows, cols), lambda g, w: (0, 0, 0))
    return pl.pallas_call(
        finish_kernel,
        grid_spec=pltpu.PrefetchScalarGridSpec(
            num_scalar_prefetch=1,
            grid=(groups,),
            in_specs=[pl.BlockSpec((rows, block), lambda g, w: (prompt, w[1] * groups + g)), whole, whole]
            + [pl.BlockSpec((2, 1, depth, chunk), lambda g, w: (0, g, 0, 0))] * len(weights)
            + [pl.BlockSpec(memory_space=pl.ANY)] * len(earlier),
            out_specs=pl.BlockSpec((1, rows, block), lambda g, w: (prompt, 0, g)),
        ),
        out_shape=jax.ShapeDtypeStruct((prompts, rows, share), bf16),
        input_output_aliases={8: 0} if earlier else {},
        compiler_params=vmem(48),
        cost_estimate=SMALL,
    )(where, x, own, far, *weights, *earlier)


def moved(value, axis, by):
    peers = lax.axis_size(axis)
    return lax.ppermute(value, axis, [(i, i + by) for i in range(peers) if 0 <= i + by < peers])


def local(
    incoming_activations,
    standardize_scaling,
    lagged_blending_weights,
    learner_line_permutation,
    learner_acceptor_lookup_slices,
    learner_projection_slices,
    fading_left_matrix,
    fading_right_matrix,
    feature_fading_speed,
    self_reward,
    cluster_scaling_vector,
    prompt_extents,
):
    reqs, span, width = incoming_activations.shape
    rows = reqs * span
    stretches = lax.axis_size("seq")
    cores = lax.axis_size("tensor")
    groups = lax.axis_size("req")
    assert reqs == cores == 2 and stretches == 4
    local_width = feature_fading_speed.shape[0]
    cols = local_width // stretches
    t, s = lax.axis_index("tensor"), lax.axis_index("seq")
    where = jnp.stack([s, t, lax.axis_index("req")]).astype(jnp.int32)

    x = incoming_activations.reshape(rows, width)
    own_x = lax.dynamic_slice_in_dim(x, t * span, span, 0)
    past = moved(own_x[span - PAST :], "seq", 1)
    pieces = [
        lax.dynamic_slice_in_dim(learner_acceptor_lookup_slices, (s ^ d) * cols, cols, 2).astype(bf16)
        for d in range(stretches)
    ]
    out_half = learner_projection_slices.astype(bf16)
    out_lines = lax.all_gather(out_half, "req", axis=0, tiled=False)
    got = [swapped(pieces[d], "seq", d) for d in range(1, stretches)]

    def tied(*values):
        return lax.optimization_barrier(values)

    own_x, past, *_ = tied(own_x, past, out_half, *pieces)
    coeffs = jnp.pad(lagged_blending_weights, ((0, PREFIX - 4), (0, 0)))
    act, coeffs = ordered(
        jnp.concatenate([past, own_x], axis=0),
        standardize_scaling.reshape(1, width),
        coeffs,
        learner_line_permutation.reshape(1, width),
    )
    act, perm, *got = tied(act, learner_line_permutation, *got)
    lines = jnp.stack([pieces[0], *got])
    chained = groups == 4

    def mixed_in(values, side, apart, earlier):
        return shifted(where, values, coeffs, left, side, apart, stretches, earlier)

    left = fading_left_matrix[perm]
    near, other = swapped(act, "seq", 1), swapped(act, "seq", 2)
    hops = [moved(lines, "req", 1), moved(lines, "req", -1)] if chained else [lax.all_gather(lines, "req", axis=0)]
    results = mixed_in(act, 0, 0, ())
    results = mixed_in(swapped(act, "tensor", 1), 1, 0, results)
    share = groups // cores
    out_lines, *results = tied(out_lines, *results)
    kept = lax.dynamic_slice_in_dim(out_lines, t * share, share, 0)
    given = lax.dynamic_slice_in_dim(out_lines, (1 - t) * share, share, 0)
    out_lines = jnp.stack([kept, swapped(given, "tensor", 1)])
    near, other, out_lines, act, *rest = tied(near, other, out_lines, act, *results, *hops)
    results, hops = tuple(rest[:2]), rest[2:]

    across = swapped(act, "seq", 3)
    if chained:
        hops += [moved(hops[0], "req", 1), moved(hops[1], "req", -1)]
    results = mixed_in(near, 0, 1, results)
    results = mixed_in(other, 0, 2, results)
    results = mixed_in(swapped(near, "tensor", 1), 1, 1, results)
    results = mixed_in(swapped(other, "tensor", 1), 1, 2, results)
    across, out_lines, *rest = tied(across, out_lines, *results, *hops)
    results, hops = tuple(rest[:2]), rest[2:]

    near, other = swapped(out_lines, "seq", 1), swapped(out_lines, "seq", 2)
    ends = [moved(hops[2], "req", 1), moved(hops[3], "req", -1)] if chained else []
    last = swapped(across, "tensor", 1)
    results = mixed_in(across, 0, 3, results)
    mixed, lora = mixed_in(last, 1, 3, results)
    if chained:
        proj = projected(where, mixed, [lines, *hops])
    else:
        proj = projected_whole(where, mixed, *hops)
    mixed, proj, out_lines, *ends = tied(mixed, proj, out_lines, *ends)
    across = swapped(out_lines, "seq", 3)
    if chained:
        proj = completed(where, mixed, proj, *ends)

    def mine(array):
        return lax.dynamic_slice_in_dim(array, s * cols, cols, array.ndim - 1).reshape(-1, cols)

    tables = [mine(a) for a in (fading_right_matrix, feature_fading_speed, self_reward, cluster_scaling_vector)]

    def one_prompt(prompt, proj):
        normed, states = recurrence(prompt, prompt_extents, where, proj, lora, *tables)
        return jnp.concatenate([normed, states.astype(bf16)], axis=1)

    def exchanged(block):
        parts = [lax.dynamic_index_in_dim(block, s ^ d, 0, keepdims=False) for d in range(stretches)]
        return parts[:1] + [swapped(parts[d], "seq", d) for d in range(1, stretches)]

    def output(prompt, blocks, earlier):
        own_lines = jnp.stack([block[:span] for block in blocks])
        far_lines = swapped(own_lines, "tensor", 1)
        return finished(prompt, reqs, where, x, own_lines, far_lines, out_weights, earlier)

    block = one_prompt(0, proj)
    block, near, other, proj = tied(block, near, other, proj)
    first = exchanged(block)
    block, across, *first = tied(one_prompt(1, proj), across, *first)
    out_weights = [out_lines, near, other, across]
    second = exchanged(block)
    hidden_out = output(0, first, ())
    hidden_out, *second = tied(hidden_out, *second)
    hidden_out = output(1, second, (hidden_out,))
    stretch_blocks = [jnp.stack([block[span:] for block in blocks]) for blocks in (first, second)]

    heads = cols // ATTEND_DIM
    states = jnp.stack(stretch_blocks).reshape(reqs, 2, 2, ATTEND_DIM, heads, ATTEND_DIM)
    states = jnp.where(s % 2 == 1, states[:, :, ::-1], states)
    states = jnp.where(s // 2 == 1, states[:, ::-1], states)
    states = jnp.transpose(states, (0, 1, 2, 4, 5, 3)).astype(f32)
    stretch_states = states.reshape(reqs, 1, stretches * heads, ATTEND_DIM * ATTEND_DIM)
    return (hidden_out, stretch_states)


def solution(mesh):
    in_specs = (
        P("req", "seq", None),
        P(),
        P(),
        P(),
        P(None, ("req", "seq"), "tensor"),
        P("tensor", ("req", "seq")),
        P(),
        P(None, "tensor"),
        P("tensor"),
        P("tensor"),
        P("tensor"),
        P("req"),
    )
    out_specs = (P("req", "seq", "tensor"), P("req", "seq", "tensor", None))
    return jax.shard_map(local, mesh=mesh, in_specs=in_specs, out_specs=out_specs, check_vma=False)
```

```python
import functools

import jax
import jax.numpy as jnp
import numpy as np
from jax import lax
from jax.experimental import pallas as pl
from jax.experimental.pallas import tpu as pltpu
from jax.sharding import PartitionSpec as P

ATTEND_DIM = 64
CHUNK = 64
LEVELS = 6
PREFIX = 8
PAST = 16

SMALL = pl.CostEstimate(flops=1024, bytes_accessed=1024, transcendentals=0)

eps = 1e-05
bf16 = jnp.bfloat16
f32 = jnp.float32


def dot(a, b):
    return jnp.dot(a, b, preferred_element_type=f32)


def dot_nt(a, b):
    return lax.dot_general(a, b, (((1,), (1,)), ((), ())), preferred_element_type=f32)


def dot_tn(a, b):
    return lax.dot_general(a, b, (((0,), (0,)), ((), ())), preferred_element_type=f32)


def swapped(value, axis, by):
    peers = lax.axis_size(axis)
    return lax.ppermute(value, axis, [(i, i ^ by) for i in range(peers)])


def vmem(mib):
    return pltpu.CompilerParams(vmem_limit_bytes=mib * 2**20)


def order_kernel(x_ref, gain_ref, coeff_ref, perm_ref, out_ref, coeff_out_ref, cur_ref):
    rows, width = x_ref.shape
    block = out_ref.shape[1]
    depth = 256

    @pl.when(pl.program_id(0) == 0)
    def _():
        x = x_ref[...].astype(f32)
        mean = jnp.mean(x, axis=-1, keepdims=True)
        centred = x - mean
        spread = jnp.mean(centred * centred, axis=-1, keepdims=True)
        cur_ref[:rows, :] = (centred * lax.rsqrt(spread + eps) * gain_ref[...]).astype(bf16)
        c = coeff_ref[...]
        high = c.astype(bf16)
        cur_ref[rows:, :] = jnp.concatenate([high, (c - high.astype(f32)).astype(bf16)], axis=0)

    perm = perm_ref[...]
    high, low = perm // depth, (perm % depth).astype(bf16)
    lines = lax.broadcasted_iota(jnp.int32, (depth, block), 0).astype(bf16)
    one, none = jnp.ones((depth, block), bf16), jnp.zeros((depth, block), bf16)
    total = jnp.zeros((rows + 2 * PREFIX, block), f32)
    for k in range(width // depth):
        mine = jnp.where(high == k, low, jnp.full_like(low, -1.0))
        total += dot(cur_ref[:, k * depth : (k + 1) * depth], jnp.where(lines == mine, one, none))
    out_ref[...] = total[:rows].astype(bf16)
    coeff_out_ref[...] = total[rows : rows + PREFIX] + total[rows + PREFIX :]


def ordered(x, gain, coeffs, perm):
    rows, width = x.shape
    block = 512
    return pl.pallas_call(
        order_kernel,
        grid=(width // block,),
        in_specs=[
            pl.BlockSpec((rows, width), lambda n: (0, 0)),
            pl.BlockSpec((1, width), lambda n: (0, 0)),
            pl.BlockSpec((PREFIX, width), lambda n: (0, 0)),
            pl.BlockSpec((1, block), lambda n: (0, n)),
        ],
        out_specs=[
            pl.BlockSpec((rows, block), lambda n: (0, n)),
            pl.BlockSpec((PREFIX, block), lambda n: (0, n)),
        ],
        out_shape=[
            jax.ShapeDtypeStruct((rows, width), bf16),
            jax.ShapeDtypeStruct((PREFIX, width), f32),
        ],
        scratch_shapes=[pltpu.VMEM((rows + 2 * PREFIX, width), bf16)],
        compiler_params=vmem(40),
        cost_estimate=SMALL,
    )(x, gain, coeffs, perm)


def mix_kernel(where_ref, act_ref, coeff_ref, left_ref, *refs):
    mixed_ref, lora_ref, inner_ref = refs[-3:]
    rows, block = mixed_ref.shape[-2:]
    width = 512
    n = pl.program_id(0)
    inner = jnp.zeros(inner_ref.shape, f32)
    for c in range(block // width):
        cols = slice(c * width, (c + 1) * width)
        cur = act_ref[PAST:, cols]
        delta = pltpu.roll(act_ref[:, cols].astype(f32), 1, 0)[PAST:].astype(bf16) - cur
        for j in range(3):
            mixed_ref[j, 0, 0, :, cols] = cur + delta * coeff_ref[j : j + 1, cols].astype(bf16)
        inner += dot(cur + delta * coeff_ref[3:4, cols].astype(bf16), left_ref[cols, :])

    @pl.when(n == 0)
    def _():
        inner_ref[...] = inner

    @pl.when(n > 0)
    def _():
        inner_ref[...] += inner

    @pl.when(n == pl.num_programs(0) - 1)
    def _():
        lora_ref[0, 0] = jnp.tanh(inner_ref[...]).astype(bf16)


def shifted(where, act, coeffs, left, side, apart, stretches, earlier):
    span, width = act.shape[0] - PAST, act.shape[1]
    inner = left.shape[1]
    block = 1024
    kept = pl.BlockSpec(memory_space=pl.ANY)
    return pl.pallas_call(
        mix_kernel,
        grid_spec=pltpu.PrefetchScalarGridSpec(
            num_scalar_prefetch=1,
            grid=(width // block,),
            in_specs=[
                pl.BlockSpec((span + PAST, block), lambda n, w: (0, n)),
                pl.BlockSpec((PREFIX, block), lambda n, w: (0, n)),
                pl.BlockSpec((block, inner), lambda n, w: (n, 0)),
            ]
            + [kept] * len(earlier),
            out_specs=[
                pl.BlockSpec((3, 1, 1, span, block), lambda n, w: (0, side, w[0] ^ apart, 0, n)),
                pl.BlockSpec((1, 1, span, inner), lambda n, w: (side, w[0] ^ apart, 0, 0)),
            ],
            scratch_shapes=[pltpu.VMEM((span, inner), f32)],
        ),
        out_shape=[
            jax.ShapeDtypeStruct((3, 2, stretches, span, width), bf16),
            jax.ShapeDtypeStruct((2, stretches, span, inner), bf16),
        ],
        input_output_aliases={4: 0, 5: 1} if earlier else {},
        compiler_params=vmem(32),
        cost_estimate=SMALL,
    )(where, act, coeffs, left, *earlier)


def project_kernel(where_ref, act_ref, *refs):
    *hops, out_ref, lines_ref = refs
    stretches, _, depth, _ = hops[0].shape
    reqs = lines_ref.shape[0] // (stretches * depth)
    reach = len(hops) // 2

    def place(r, values):
        for d in range(stretches):
            at = (r * stretches + (where_ref[0] ^ d)) * depth
            lines_ref[pl.ds(pl.multiple_of(at, depth), depth), :] = values(d)

    @pl.when(pl.program_id(1) == 0)
    def _():
        me = where_ref[2]
        place(me, lambda d: hops[0][d, 0])
        for hop in range(1, reqs):
            for r, ref in ((me - hop, 2 * hop - 1), (me + hop, 2 * hop)):

                @pl.when((r >= 0) & (r < reqs))
                def _():
                    if hop > reach:
                        place(r, lambda d: jnp.zeros_like(hops[0][d, 0]))
                    else:
                        place(r, lambda d: hops[ref][d, 0])

    act = act_ref[0, 0].reshape(-1, act_ref.shape[-1])
    out_ref[0, 0] = dot(act, lines_ref[...]).reshape(out_ref.shape[2:])


def projected(where, mixed, hops):
    stretches, kinds, depth, cols = hops[0].shape
    _, sides, _, span, width = mixed.shape
    return pl.pallas_call(
        project_kernel,
        grid_spec=pltpu.PrefetchScalarGridSpec(
            num_scalar_prefetch=1,
            grid=(kinds, sides),
            in_specs=[pl.BlockSpec((1, 1, stretches, span, width), lambda j, m, w: (j, m, 0, 0, 0))]
            + [pl.BlockSpec((stretches, 1, depth, cols), lambda j, m, w: (0, j, 0, 0))] * len(hops),
            out_specs=pl.BlockSpec((1, 1, stretches, span, cols), lambda j, m, w: (j, m, 0, 0, 0)),
            scratch_shapes=[pltpu.VMEM((width, cols), bf16)],
        ),
        out_shape=jax.ShapeDtypeStruct((kinds, sides, stretches, span, cols), f32),
        compiler_params=vmem(60),
        cost_estimate=SMALL,
    )(where, mixed, *hops)


def projected_whole(where, mixed, lines):
    _, stretches, kinds, depth, cols = lines.shape
    lines = lines[:, jnp.arange(stretches) ^ where[0]]
    lines = jnp.transpose(lines, (2, 0, 1, 3, 4)).reshape(kinds, mixed.shape[-1], cols)
    return jnp.einsum("jxbtk,jkc->jxbtc", mixed, lines, preferred_element_type=f32).astype(bf16)


def decay_sums():
    place = np.arange(CHUNK)
    of, by = place[:, None], place[None, :]
    parts = []
    for level in range(LEVELS):
        half = 1 << level
        middle = (of // (2 * half)) * 2 * half + half - 1
        later = (of % (2 * half)) >= half
        parts.append(np.where(later, (by > middle) & (by < of), (by > of) & (by <= middle)))
    parts += [by < of, by > of, np.ones((8, CHUNK), bool)]
    sums = np.concatenate(parts).astype(np.float32)
    return np.concatenate([sums, sums], axis=1)


def pair_levels(heads):
    of, by = np.arange(CHUNK)[:, None], np.arange(CHUNK)[None, :]
    level = np.full((CHUNK, CHUNK), -1.0, np.float32)
    for bit in range(LEVELS):
        level[((of ^ by) >> bit) == 1] = bit
    return np.tile(np.where(of > by, level, -1.0).astype(np.float32), (1, heads))


def wkv_kernel(extent_ref, where_ref, *refs, prompt, parted):
    if parted:
        act_ref, below_ref, above_ref, *refs, lines_ref = refs
    proj_ref, lora_ref, right_ref, speed_ref, reward_ref, scale_ref, sums_ref, level_ref, same_ref, *refs = refs
    normed_ref, state_ref, memory_ref = refs
    step = pl.program_id(0)
    tokens, cols = proj_ref.shape[3:]
    heads = cols // ATTEND_DIM
    same = same_ref[...]
    same_f32 = same.astype(f32)
    level = level_ref[...]

    @pl.when(step == 0)
    def _():
        memory_ref[...] = jnp.zeros_like(memory_ref)
        if parted:
            stretches, kinds, depth, _ = below_ref.shape
            for d in range(stretches):
                at = pl.ds(pl.multiple_of((where_ref[0] ^ d) * depth, depth), depth)
                for j in range(kinds):
                    lines_ref[j, at, :] = below_ref[d, j] + above_ref[d, j]

    def projection(j):
        if not parted:
            return proj_ref[j, 0, 0]
        return (proj_ref[j, 0, 0] + dot(act_ref[j, 0, 0], lines_ref[j])).astype(bf16)

    at = step * tokens + lax.broadcasted_iota(jnp.int32, (tokens, cols), 0)
    valid = jnp.where(at < extent_ref[prompt], 1.0, 0.0)
    r = projection(0)
    k = projection(1) * valid.astype(bf16)
    v = projection(2)
    decay = -speed_ref[...] * jnp.exp(dot(lora_ref[0, 0], right_ref[...])) * valid
    high = decay.astype(bf16)
    low = (decay - high.astype(f32)).astype(bf16)
    own = dot((r.astype(f32) * reward_ref[...] * k.astype(f32)).astype(bf16), same) * v.astype(f32)

    memory = memory_ref[...]
    rows = []
    for sub in range(tokens // CHUNK):
        lines = slice(sub * CHUNK, (sub + 1) * CHUNK)
        r_sub, k_sub, v_sub = r[lines], k[lines], v[lines]
        kept = jnp.exp(dot(sums_ref[...], jnp.concatenate([high[lines], low[lines]], axis=0)))
        scores = jnp.zeros((CHUNK, heads * CHUNK), f32)
        for bit in range(LEVELS):
            part = kept[bit * CHUNK : (bit + 1) * CHUNK].astype(bf16)
            lookup = jnp.concatenate([k_sub * part] * heads, axis=0) * same
            scores = jnp.where(level == bit, dot_nt(r_sub * part, lookup), scores)
        v_heads = jnp.concatenate([v_sub] * heads, axis=0) * same
        from_start = r_sub * kept[LEVELS * CHUNK : (LEVELS + 1) * CHUNK].astype(bf16)
        to_end = k_sub * kept[(LEVELS + 1) * CHUNK : (LEVELS + 2) * CHUNK].astype(bf16)
        whole = kept[(LEVELS + 2) * CHUNK : (LEVELS + 2) * CHUNK + 1]
        rows.append(dot_nt(from_start, memory.astype(bf16)) + dot(scores.astype(bf16), v_heads))
        memory = memory * whole + same_f32 * dot_tn(v_sub, to_end)
    memory_ref[...] = memory
    folded = memory[:ATTEND_DIM]
    for h in range(1, heads):
        folded += memory[h * ATTEND_DIM : (h + 1) * ATTEND_DIM]
    state_ref[0] = folded

    y = jnp.concatenate(rows, axis=0) + own
    y_high = y.astype(bf16)
    y_low = (y - y_high.astype(f32)).astype(bf16)
    centred = y - (dot(y_high, same) + dot(y_low, same)) * (1.0 / ATTEND_DIM)
    spread = dot((centred * centred).astype(bf16), same) * (1.0 / ATTEND_DIM)
    normed_ref[0] = (centred * lax.rsqrt(spread + eps) * scale_ref[...] * valid).astype(bf16)


def recurrence(prompt, extents, where, mixed, proj, ends, lora, right, speed, reward, scale):
    kinds, _, stretches, span, cols = proj.shape
    width = mixed.shape[-1]
    inner = lora.shape[-1]
    heads = cols // ATTEND_DIM
    sums = jnp.asarray(decay_sums(), bf16)
    level = jnp.asarray(pair_levels(heads), f32)
    head = np.arange(cols) // ATTEND_DIM
    same = jnp.asarray(head[:, None] == head[None, :], bf16)

    def fixed(array):
        return pl.BlockSpec(array.shape, lambda c, e, w: (0,) * array.ndim)

    tables = (right, speed, reward, scale, sums, level, same)
    first, first_specs, scratch = (), [], [pltpu.VMEM((cols, cols), f32)]
    if ends:
        share = stretches * ends[0].shape[2]
        last = width // share - 1
        first = (mixed, *ends)
        first_specs = [
            pl.BlockSpec(
                (kinds, 1, 1, span, share),
                lambda c, e, w: (0, w[1] ^ prompt, c, 0, jnp.where(w[2] == last, 0, last)),
            ),
            *map(fixed, ends),
        ]
        scratch.append(pltpu.VMEM((kinds, share, cols), bf16))
    return pl.pallas_call(
        functools.partial(wkv_kernel, prompt=prompt, parted=bool(ends)),
        grid_spec=pltpu.PrefetchScalarGridSpec(
            num_scalar_prefetch=2,
            grid=(stretches,),
            in_specs=first_specs
            + [
                pl.BlockSpec((kinds, 1, 1, span, cols), lambda c, e, w: (0, w[1] ^ prompt, c, 0, 0)),
                pl.BlockSpec((1, 1, span, inner), lambda c, e, w: (w[1] ^ prompt, c, 0, 0)),
            ]
            + [fixed(a) for a in tables],
            out_specs=[
                pl.BlockSpec((1, span, cols), lambda c, e, w: (c, 0, 0)),
                pl.BlockSpec((1, ATTEND_DIM, cols), lambda c, e, w: (c, 0, 0)),
            ],
            scratch_shapes=scratch,
        ),
        out_shape=[
            jax.ShapeDtypeStruct((stretches, span, cols), bf16),
            jax.ShapeDtypeStruct((stretches, ATTEND_DIM, cols), f32),
        ],
        compiler_params=vmem(56),
        cost_estimate=SMALL,
    )(extents, where, *first, proj, lora, *tables)


def finish_kernel(where_ref, x_ref, own_ref, far_ref, *refs):
    weights, out_ref = refs[:5], refs[-1]
    stretches, rows, cols = own_ref.shape
    chunk = weights[0].shape[-1]
    for e in range(stretches):
        places = pl.ds(pl.multiple_of((where_ref[0] ^ e) * chunk, chunk), chunk)
        total = x_ref[:, places].astype(f32)
        for side, lines_ref in enumerate((own_ref, far_ref)):
            w_ref = weights[e].at[side, 0] if e < 3 else weights[e + side].at[0, 0]
            for d in range(stretches):
                at = pl.ds(pl.multiple_of((where_ref[0] ^ d) * cols, cols), cols)
                total += dot(lines_ref[d], w_ref[at, :])
        out_ref[0, :, places] = total.astype(bf16)


def finished(prompt, prompts, where, x, own, far, weights, earlier):
    stretches, _, cols = own.shape
    rows = x.shape[0] // prompts
    _, groups, depth, chunk = weights[0].shape
    share = groups * stretches * chunk
    if chunk % 128:
        order = jnp.arange(stretches) ^ where[0]
        total = lax.dynamic_slice(x, (prompt * rows, where[1] * share), (rows, share)).astype(f32)
        weights = [*weights[:3], jnp.concatenate(weights[3:])]
        for side, lines in enumerate((own, far)):
            w = jnp.stack([w[side] for w in weights])[order]
            w = jnp.transpose(w, (2, 1, 0, 3)).reshape(depth, share)
            lines = jnp.transpose(lines[order, :rows], (1, 0, 2)).reshape(rows, depth)
            total += dot(lines, w)
        return jnp.concatenate([*earlier, total.astype(bf16)[None]], axis=0)
    block = stretches * chunk
    lines_spec = pl.BlockSpec((stretches, rows, cols), lambda g, w: (0, 0, 0))
    return pl.pallas_call(
        finish_kernel,
        grid_spec=pltpu.PrefetchScalarGridSpec(
            num_scalar_prefetch=1,
            grid=(groups,),
            in_specs=[pl.BlockSpec((rows, block), lambda g, w: (prompt, w[1] * groups + g)), lines_spec, lines_spec]
            + [pl.BlockSpec((a.shape[0], 1, depth, chunk), lambda g, w: (0, g, 0, 0)) for a in weights]
            + [pl.BlockSpec(memory_space=pl.ANY)] * len(earlier),
            out_specs=pl.BlockSpec((1, rows, block), lambda g, w: (prompt, 0, g)),
        ),
        out_shape=jax.ShapeDtypeStruct((prompts, rows, share), bf16),
        input_output_aliases={9: 0} if earlier else {},
        compiler_params=vmem(48),
        cost_estimate=SMALL,
    )(where, x, own, far, *weights, *earlier)


def moved(value, axis, by):
    peers = lax.axis_size(axis)
    return lax.ppermute(value, axis, [(i, i + by) for i in range(peers) if 0 <= i + by < peers])


def local(
    incoming_activations,
    standardize_scaling,
    lagged_blending_weights,
    learner_line_permutation,
    learner_acceptor_lookup_slices,
    learner_projection_slices,
    fading_left_matrix,
    fading_right_matrix,
    feature_fading_speed,
    self_reward,
    cluster_scaling_vector,
    prompt_extents,
):
    reqs, span, width = incoming_activations.shape
    rows = reqs * span
    stretches = lax.axis_size("seq")
    cores = lax.axis_size("tensor")
    groups = lax.axis_size("req")
    assert reqs == cores == 2 and stretches == 4
    local_width = feature_fading_speed.shape[0]
    cols = local_width // stretches
    t, s = lax.axis_index("tensor"), lax.axis_index("seq")
    where = jnp.stack([s, t, lax.axis_index("req")]).astype(jnp.int32)

    x = incoming_activations.reshape(rows, width)
    own_x = lax.dynamic_slice_in_dim(x, t * span, span, 0)
    past = moved(own_x[span - PAST :], "seq", 1)
    pieces = [
        lax.dynamic_slice_in_dim(learner_acceptor_lookup_slices, (s ^ d) * cols, cols, 2).astype(bf16)
        for d in range(stretches)
    ]
    out_half = learner_projection_slices.astype(bf16)
    out_lines = lax.all_gather(out_half, "req", axis=0, tiled=False)
    got = [swapped(pieces[d], "seq", d) for d in range(1, stretches)]

    def tied(*values):
        return lax.optimization_barrier(values)

    own_x, past, *_ = tied(own_x, past, out_half, *pieces)
    coeffs = jnp.pad(lagged_blending_weights, ((0, PREFIX - 4), (0, 0)))
    act, coeffs = ordered(
        jnp.concatenate([past, own_x], axis=0),
        standardize_scaling.reshape(1, width),
        coeffs,
        learner_line_permutation.reshape(1, width),
    )
    act, perm, *got = tied(act, learner_line_permutation, *got)
    lines = jnp.stack([pieces[0], *got])
    chained = groups == 4

    def mixed_in(values, side, apart, earlier):
        return shifted(where, values, coeffs, left, side, apart, stretches, earlier)

    left = fading_left_matrix[perm]
    near, other = swapped(act, "seq", 1), swapped(act, "seq", 2)
    hops = [moved(lines, "req", 1), moved(lines, "req", -1)] if chained else [lax.all_gather(lines, "req", axis=0)]
    results = mixed_in(act, 0, 0, ())
    results = mixed_in(swapped(act, "tensor", 1), 1, 0, results)
    share = groups // cores
    out_lines, *results = tied(out_lines, *results)
    kept = lax.dynamic_slice_in_dim(out_lines, t * share, share, 0)
    given = lax.dynamic_slice_in_dim(out_lines, (1 - t) * share, share, 0)
    out_lines = jnp.stack([kept, swapped(given, "tensor", 1)])
    near, other, out_lines, *rest = tied(near, other, out_lines, *results, *hops)
    results, hops = tuple(rest[:2]), rest[2:]

    cut = (span + PAST) // 32 * 16
    across = [swapped(near[:cut], "seq", 2), swapped(other[cut:], "seq", 1)]
    if chained:
        hops += [moved(hops[0], "req", 1), moved(hops[1], "req", -1)]
    results = mixed_in(near, 0, 1, results)
    results = mixed_in(other, 0, 2, results)
    results = mixed_in(swapped(near, "tensor", 1), 1, 1, results)
    results = mixed_in(swapped(other, "tensor", 1), 1, 2, results)
    out_lines, *rest = tied(out_lines, *results, *hops, *across)
    results, hops, across = tuple(rest[:2]), rest[2:-2], jnp.concatenate(rest[-2:], axis=0)

    near, other = swapped(out_lines, "seq", 1), swapped(out_lines, "seq", 2)
    ends = [moved(hops[2], "req", 1), moved(hops[3], "req", -1)] if chained else []
    last = swapped(across, "tensor", 1)
    results = mixed_in(across, 0, 3, results)
    mixed, lora = mixed_in(last, 1, 3, results)
    if chained:
        proj = projected(where, mixed, [lines, *hops])
    else:
        proj = projected_whole(where, mixed, *hops)
    mixed, proj, *ends = tied(mixed, proj, *ends)

    def mine(array):
        return lax.dynamic_slice_in_dim(array, s * cols, cols, array.ndim - 1).reshape(-1, cols)

    tables = [mine(a) for a in (fading_right_matrix, feature_fading_speed, self_reward, cluster_scaling_vector)]

    def one_prompt(prompt, proj):
        normed, states = recurrence(prompt, prompt_extents, where, mixed, proj, ends, lora, *tables)
        return jnp.concatenate([normed, states.astype(bf16)], axis=1)

    def exchanged(block):
        parts = [lax.dynamic_index_in_dim(block, s ^ d, 0, keepdims=False) for d in range(stretches)]
        return parts[:1] + [swapped(parts[d], "seq", d) for d in range(1, stretches)]

    def output(prompt, blocks, earlier):
        far_blocks = swapped(blocks, "tensor", 1)
        return finished(prompt, reqs, where, x, blocks, far_blocks, out_weights, earlier)

    block = one_prompt(0, proj)
    block, near, other, proj = tied(block, near, other, proj)
    first = exchanged(block)
    across = [swapped(near[:1], "seq", 2), swapped(other[1:], "seq", 1)]
    block, *first = tied(one_prompt(1, proj), *first)
    second = exchanged(block)
    first, *across = tied(jnp.stack(first), *across)
    out_weights = [out_lines, near, other, *across]
    hidden_out = output(0, first, ())
    hidden_out, *second = tied(hidden_out, *second)
    second = jnp.stack(second)
    hidden_out = output(1, second, (hidden_out,))
    stretch_blocks = [blocks[:, span:] for blocks in (first, second)]

    heads = cols // ATTEND_DIM
    states = jnp.stack(stretch_blocks).reshape(reqs, 2, 2, ATTEND_DIM, heads, ATTEND_DIM)
    states = jnp.where(s % 2 == 1, states[:, :, ::-1], states)
    states = jnp.where(s // 2 == 1, states[:, ::-1], states)
    states = jnp.transpose(states, (0, 1, 2, 4, 5, 3)).astype(f32)
    stretch_states = states.reshape(reqs, 1, stretches * heads, ATTEND_DIM * ATTEND_DIM)
    return (hidden_out, stretch_states)


def solution(mesh):
    in_specs = (
        P("req", "seq", None),
        P(),
        P(),
        P(),
        P(None, ("req", "seq"), "tensor"),
        P("tensor", ("req", "seq")),
        P(),
        P(None, "tensor"),
        P("tensor"),
        P("tensor"),
        P("tensor"),
        P("req"),
    )
    out_specs = (P("req", "seq", "tensor"), P("req", "seq", "tensor", None))
    return jax.shard_map(local, mesh=mesh, in_specs=in_specs, out_specs=out_specs, check_vma=False)
```

```python
import functools

import jax
import jax.numpy as jnp
import numpy as np
from jax import lax
from jax.experimental import pallas as pl
from jax.experimental.pallas import tpu as pltpu
from jax.sharding import PartitionSpec as P

ATTEND_DIM = 64
CHUNK = 64
LEVELS = 6
PREFIX = 8
PAST = 16

SMALL = pl.CostEstimate(flops=1024, bytes_accessed=1024, transcendentals=0)

eps = 1e-05
bf16 = jnp.bfloat16
f32 = jnp.float32


def dot(a, b):
    return jnp.dot(a, b, preferred_element_type=f32)


def dot_nt(a, b):
    return lax.dot_general(a, b, (((1,), (1,)), ((), ())), preferred_element_type=f32)


def dot_tn(a, b):
    return lax.dot_general(a, b, (((0,), (0,)), ((), ())), preferred_element_type=f32)


def swapped(value, axis, by):
    peers = lax.axis_size(axis)
    return lax.ppermute(value, axis, [(i, i ^ by) for i in range(peers)])


def vmem(mib):
    return pltpu.CompilerParams(vmem_limit_bytes=mib * 2**20)


def order_kernel(x_ref, gain_ref, coeff_ref, perm_ref, out_ref, coeff_out_ref, cur_ref):
    rows, width = x_ref.shape
    block = out_ref.shape[1]
    depth = 256

    @pl.when(pl.program_id(0) == 0)
    def _():
        x = x_ref[...].astype(f32)
        mean = jnp.mean(x, axis=-1, keepdims=True)
        centred = x - mean
        spread = jnp.mean(centred * centred, axis=-1, keepdims=True)
        cur_ref[:rows, :] = (centred * lax.rsqrt(spread + eps) * gain_ref[...]).astype(bf16)
        c = coeff_ref[...]
        high = c.astype(bf16)
        cur_ref[rows:, :] = jnp.concatenate([high, (c - high.astype(f32)).astype(bf16)], axis=0)

    perm = perm_ref[...]
    high, low = perm // depth, (perm % depth).astype(bf16)
    lines = lax.broadcasted_iota(jnp.int32, (depth, block), 0).astype(bf16)
    one, none = jnp.ones((depth, block), bf16), jnp.zeros((depth, block), bf16)
    total = jnp.zeros((rows + 2 * PREFIX, block), f32)
    for k in range(width // depth):
        mine = jnp.where(high == k, low, jnp.full_like(low, -1.0))
        total += dot(cur_ref[:, k * depth : (k + 1) * depth], jnp.where(lines == mine, one, none))
    out_ref[...] = total[:rows].astype(bf16)
    coeff_out_ref[...] = total[rows : rows + PREFIX] + total[rows + PREFIX :]


def ordered(x, gain, coeffs, perm):
    rows, width = x.shape
    block = 512
    return pl.pallas_call(
        order_kernel,
        grid=(width // block,),
        in_specs=[
            pl.BlockSpec((rows, width), lambda n: (0, 0)),
            pl.BlockSpec((1, width), lambda n: (0, 0)),
            pl.BlockSpec((PREFIX, width), lambda n: (0, 0)),
            pl.BlockSpec((1, block), lambda n: (0, n)),
        ],
        out_specs=[
            pl.BlockSpec((rows, block), lambda n: (0, n)),
            pl.BlockSpec((PREFIX, block), lambda n: (0, n)),
        ],
        out_shape=[
            jax.ShapeDtypeStruct((rows, width), bf16),
            jax.ShapeDtypeStruct((PREFIX, width), f32),
        ],
        scratch_shapes=[pltpu.VMEM((rows + 2 * PREFIX, width), bf16)],
        compiler_params=vmem(40),
        cost_estimate=SMALL,
    )(x, gain, coeffs, perm)


def mix_kernel(where_ref, act_ref, coeff_ref, left_ref, *refs):
    mixed_ref, lora_ref, inner_ref = refs[-3:]
    rows, block = mixed_ref.shape[-2:]
    width = 512
    n = pl.program_id(0)
    inner = jnp.zeros(inner_ref.shape, f32)
    for c in range(block // width):
        cols = slice(c * width, (c + 1) * width)
        cur = act_ref[PAST:, cols]
        delta = pltpu.roll(act_ref[:, cols].astype(f32), 1, 0)[PAST:].astype(bf16) - cur
        for j in range(3):
            mixed_ref[j, 0, 0, :, cols] = cur + delta * coeff_ref[j : j + 1, cols].astype(bf16)
        inner += dot(cur + delta * coeff_ref[3:4, cols].astype(bf16), left_ref[cols, :])

    @pl.when(n == 0)
    def _():
        inner_ref[...] = inner

    @pl.when(n > 0)
    def _():
        inner_ref[...] += inner

    @pl.when(n == pl.num_programs(0) - 1)
    def _():
        lora_ref[0, 0] = jnp.tanh(inner_ref[...]).astype(bf16)


def shifted(where, act, coeffs, left, side, apart, stretches, earlier):
    span, width = act.shape[0] - PAST, act.shape[1]
    inner = left.shape[1]
    block = 1024
    kept = pl.BlockSpec(memory_space=pl.ANY)
    return pl.pallas_call(
        mix_kernel,
        grid_spec=pltpu.PrefetchScalarGridSpec(
            num_scalar_prefetch=1,
            grid=(width // block,),
            in_specs=[
                pl.BlockSpec((span + PAST, block), lambda n, w: (0, n)),
                pl.BlockSpec((PREFIX, block), lambda n, w: (0, n)),
                pl.BlockSpec((block, inner), lambda n, w: (n, 0)),
            ]
            + [kept] * len(earlier),
            out_specs=[
                pl.BlockSpec((3, 1, 1, span, block), lambda n, w: (0, side, w[0] ^ apart, 0, n)),
                pl.BlockSpec((1, 1, span, inner), lambda n, w: (side, w[0] ^ apart, 0, 0)),
            ],
            scratch_shapes=[pltpu.VMEM((span, inner), f32)],
        ),
        out_shape=[
            jax.ShapeDtypeStruct((3, 2, stretches, span, width), bf16),
            jax.ShapeDtypeStruct((2, stretches, span, inner), bf16),
        ],
        input_output_aliases={4: 0, 5: 1} if earlier else {},
        compiler_params=vmem(32),
        cost_estimate=SMALL,
    )(where, act, coeffs, left, *earlier)


def project_kernel(where_ref, act_ref, *refs):
    *hops, out_ref, lines_ref = refs
    stretches, _, depth, _ = hops[0].shape
    reqs = lines_ref.shape[0] // (stretches * depth)
    reach = len(hops) // 2

    def place(r, values):
        for d in range(stretches):
            at = (r * stretches + (where_ref[0] ^ d)) * depth
            lines_ref[pl.ds(pl.multiple_of(at, depth), depth), :] = values(d)

    @pl.when(pl.program_id(1) == 0)
    def _():
        me = where_ref[2]
        place(me, lambda d: hops[0][d, 0])
        for hop in range(1, reqs):
            for r, ref in ((me - hop, 2 * hop - 1), (me + hop, 2 * hop)):

                @pl.when((r >= 0) & (r < reqs))
                def _():
                    if hop > reach:
                        place(r, lambda d: jnp.zeros_like(hops[0][d, 0]))
                    else:
                        place(r, lambda d: hops[ref][d, 0])

    act = act_ref[0, 0].reshape(-1, act_ref.shape[-1])
    out_ref[0, 0] = dot(act, lines_ref[...]).reshape(out_ref.shape[2:])


def projected(where, mixed, hops):
    stretches, kinds, depth, cols = hops[0].shape
    _, sides, _, span, width = mixed.shape
    return pl.pallas_call(
        project_kernel,
        grid_spec=pltpu.PrefetchScalarGridSpec(
            num_scalar_prefetch=1,
            grid=(kinds, 2 * sides),
            in_specs=[pl.BlockSpec((1, 1, stretches // 2, span, width), lambda j, m, w: (j, m // 2, m % 2, 0, 0))]
            + [pl.BlockSpec((stretches, 1, depth, cols), lambda j, m, w: (0, j, 0, 0))] * len(hops),
            out_specs=pl.BlockSpec((1, 1, stretches // 2, span, cols), lambda j, m, w: (j, m // 2, m % 2, 0, 0)),
            scratch_shapes=[pltpu.VMEM((width, cols), bf16)],
        ),
        out_shape=jax.ShapeDtypeStruct((kinds, sides, stretches, span, cols), f32),
        compiler_params=vmem(60),
        cost_estimate=SMALL,
    )(where, mixed, *hops)


def projected_whole(where, mixed, lines):
    _, stretches, kinds, depth, cols = lines.shape
    lines = lines[:, jnp.arange(stretches) ^ where[0]]
    lines = jnp.transpose(lines, (2, 0, 1, 3, 4)).reshape(kinds, mixed.shape[-1], cols)
    return jnp.einsum("jxbtk,jkc->jxbtc", mixed, lines, preferred_element_type=f32).astype(bf16)


def decay_sums():
    place = np.arange(CHUNK)
    of, by = place[:, None], place[None, :]
    parts = []
    for level in range(LEVELS):
        half = 1 << level
        middle = (of // (2 * half)) * 2 * half + half - 1
        later = (of % (2 * half)) >= half
        parts.append(np.where(later, (by > middle) & (by < of), (by > of) & (by <= middle)))
    parts += [by < of, by > of, np.ones((8, CHUNK), bool)]
    sums = np.concatenate(parts).astype(np.float32)
    return np.concatenate([sums, sums], axis=1)


def pair_levels(heads):
    of, by = np.arange(CHUNK)[:, None], np.arange(CHUNK)[None, :]
    level = np.full((CHUNK, CHUNK), -1.0, np.float32)
    for bit in range(LEVELS):
        level[((of ^ by) >> bit) == 1] = bit
    return np.tile(np.where(of > by, level, -1.0).astype(np.float32), (1, heads))


def wkv_kernel(extent_ref, where_ref, *refs, prompt, parted):
    if parted:
        act_ref, below_ref, above_ref, *refs, lines_ref = refs
    proj_ref, lora_ref, right_ref, speed_ref, reward_ref, scale_ref, sums_ref, level_ref, same_ref, *refs = refs
    out_ref, memory_ref = refs
    step = pl.program_id(0)
    tokens, cols = proj_ref.shape[3:]
    heads = cols // ATTEND_DIM
    same = same_ref[...]
    same_f32 = same.astype(f32)
    level = level_ref[...]

    @pl.when(step == 0)
    def _():
        memory_ref[...] = jnp.zeros_like(memory_ref)
        if parted:
            stretches, kinds, depth, _ = below_ref.shape
            for d in range(stretches):
                at = pl.ds(pl.multiple_of((where_ref[0] ^ d) * depth, depth), depth)
                for j in range(kinds):
                    lines_ref[j, at, :] = below_ref[d, j] + above_ref[d, j]

    def projection(j):
        if not parted:
            return proj_ref[j, 0, 0]
        return (proj_ref[j, 0, 0] + dot(act_ref[j, 0, 0], lines_ref[j])).astype(bf16)

    at = step * tokens + lax.broadcasted_iota(jnp.int32, (tokens, cols), 0)
    valid = jnp.where(at < extent_ref[prompt], 1.0, 0.0)
    r = projection(0)
    k = projection(1) * valid.astype(bf16)
    v = projection(2)
    decay = -speed_ref[...] * jnp.exp(dot(lora_ref[0, 0], right_ref[...])) * valid
    high = decay.astype(bf16)
    low = (decay - high.astype(f32)).astype(bf16)
    own = dot((r.astype(f32) * reward_ref[...] * k.astype(f32)).astype(bf16), same) * v.astype(f32)

    memory = memory_ref[...]
    rows = []
    for sub in range(tokens // CHUNK):
        lines = slice(sub * CHUNK, (sub + 1) * CHUNK)
        r_sub, k_sub, v_sub = r[lines], k[lines], v[lines]
        kept = jnp.exp(dot(sums_ref[...], jnp.concatenate([high[lines], low[lines]], axis=0)))
        scores = jnp.zeros((CHUNK, heads * CHUNK), f32)
        for bit in range(LEVELS):
            part = kept[bit * CHUNK : (bit + 1) * CHUNK].astype(bf16)
            lookup = jnp.concatenate([k_sub * part] * heads, axis=0) * same
            scores = jnp.where(level == bit, dot_nt(r_sub * part, lookup), scores)
        v_heads = jnp.concatenate([v_sub] * heads, axis=0) * same
        from_start = r_sub * kept[LEVELS * CHUNK : (LEVELS + 1) * CHUNK].astype(bf16)
        to_end = k_sub * kept[(LEVELS + 1) * CHUNK : (LEVELS + 2) * CHUNK].astype(bf16)
        whole = kept[(LEVELS + 2) * CHUNK : (LEVELS + 2) * CHUNK + 1]
        rows.append(dot_nt(from_start, memory.astype(bf16)) + dot(scores.astype(bf16), v_heads))
        memory = memory * whole + same_f32 * dot_tn(v_sub, to_end)
    memory_ref[...] = memory
    folded = memory[:ATTEND_DIM]
    for h in range(1, heads):
        folded += memory[h * ATTEND_DIM : (h + 1) * ATTEND_DIM]
    out_ref[0, tokens:] = folded.astype(bf16)

    y = jnp.concatenate(rows, axis=0) + own
    y_high = y.astype(bf16)
    y_low = (y - y_high.astype(f32)).astype(bf16)
    centred = y - (dot(y_high, same) + dot(y_low, same)) * (1.0 / ATTEND_DIM)
    spread = dot((centred * centred).astype(bf16), same) * (1.0 / ATTEND_DIM)
    out_ref[0, :tokens] = (centred * lax.rsqrt(spread + eps) * scale_ref[...] * valid).astype(bf16)


def recurrence(prompt, extents, where, mixed, proj, ends, lora, right, speed, reward, scale):
    kinds, _, stretches, span, cols = proj.shape
    width = mixed.shape[-1]
    inner = lora.shape[-1]
    heads = cols // ATTEND_DIM
    sums = jnp.asarray(decay_sums(), bf16)
    level = jnp.asarray(pair_levels(heads), f32)
    head = np.arange(cols) // ATTEND_DIM
    same = jnp.asarray(head[:, None] == head[None, :], bf16)

    def fixed(array):
        return pl.BlockSpec(array.shape, lambda c, e, w: (0,) * array.ndim)

    tables = (right, speed, reward, scale, sums, level, same)
    first, first_specs, scratch = (), [], [pltpu.VMEM((cols, cols), f32)]
    if ends:
        share = stretches * ends[0].shape[2]
        last = width // share - 1
        first = (mixed, *ends)
        first_specs = [
            pl.BlockSpec(
                (kinds, 1, 1, span, share),
                lambda c, e, w: (0, w[1] ^ prompt, c, 0, jnp.where(w[2] == last, 0, last)),
            ),
            *map(fixed, ends),
        ]
        scratch.append(pltpu.VMEM((kinds, share, cols), bf16))
    return pl.pallas_call(
        functools.partial(wkv_kernel, prompt=prompt, parted=bool(ends)),
        grid_spec=pltpu.PrefetchScalarGridSpec(
            num_scalar_prefetch=2,
            grid=(stretches,),
            in_specs=first_specs
            + [
                pl.BlockSpec((kinds, 1, 1, span, cols), lambda c, e, w: (0, w[1] ^ prompt, c, 0, 0)),
                pl.BlockSpec((1, 1, span, inner), lambda c, e, w: (w[1] ^ prompt, c, 0, 0)),
            ]
            + [fixed(a) for a in tables],
            out_specs=pl.BlockSpec((1, span + ATTEND_DIM, cols), lambda c, e, w: (c, 0, 0)),
            scratch_shapes=scratch,
        ),
        out_shape=jax.ShapeDtypeStruct((stretches, span + ATTEND_DIM, cols), bf16),
        compiler_params=vmem(56),
        cost_estimate=SMALL,
    )(extents, where, *first, proj, lora, *tables)


def finish_kernel(where_ref, x_ref, own_ref, far_ref, *refs):
    weights, out_ref = refs[:5], refs[-1]
    stretches, rows, cols = own_ref.shape
    chunk = weights[0].shape[-1]
    for e in range(stretches):
        places = pl.ds(pl.multiple_of((where_ref[0] ^ e) * chunk, chunk), chunk)
        total = x_ref[:, places].astype(f32)
        for side, lines_ref in enumerate((own_ref, far_ref)):
            w_ref = weights[e].at[side, 0] if e < 3 else weights[e + side].at[0, 0]
            for d in range(stretches):
                at = pl.ds(pl.multiple_of((where_ref[0] ^ d) * cols, cols), cols)
                total += dot(lines_ref[d], w_ref[at, :])
        out_ref[0, :, places] = total.astype(bf16)


def finished(prompt, prompts, where, x, own, far, weights, earlier):
    stretches, _, cols = own.shape
    rows = x.shape[0] // prompts
    _, groups, depth, chunk = weights[0].shape
    share = groups * stretches * chunk
    if chunk % 128:
        order = jnp.arange(stretches) ^ where[0]
        total = lax.dynamic_slice(x, (prompt * rows, where[1] * share), (rows, share)).astype(f32)
        weights = [*weights[:3], jnp.concatenate(weights[3:])]
        for side, lines in enumerate((own, far)):
            w = jnp.stack([w[side] for w in weights])[order]
            w = jnp.transpose(w, (2, 1, 0, 3)).reshape(depth, share)
            lines = jnp.transpose(lines[order, :rows], (1, 0, 2)).reshape(rows, depth)
            total += dot(lines, w)
        return jnp.concatenate([*earlier, total.astype(bf16)[None]], axis=0)
    block = stretches * chunk
    lines_spec = pl.BlockSpec((stretches, rows, cols), lambda g, w: (0, 0, 0))
    return pl.pallas_call(
        finish_kernel,
        grid_spec=pltpu.PrefetchScalarGridSpec(
            num_scalar_prefetch=1,
            grid=(groups,),
            in_specs=[pl.BlockSpec((rows, block), lambda g, w: (prompt, w[1] * groups + g)), lines_spec, lines_spec]
            + [pl.BlockSpec((a.shape[0], 1, depth, chunk), lambda g, w: (0, g, 0, 0)) for a in weights]
            + [pl.BlockSpec(memory_space=pl.ANY)] * len(earlier),
            out_specs=pl.BlockSpec((1, rows, block), lambda g, w: (prompt, 0, g)),
        ),
        out_shape=jax.ShapeDtypeStruct((prompts, rows, share), bf16),
        input_output_aliases={9: 0} if earlier else {},
        compiler_params=vmem(48),
        cost_estimate=SMALL,
    )(where, x, own, far, *weights, *earlier)


def states_kernel(where_ref, blocks_ref, pick_ref, *refs):
    out_ref = refs[-1]
    stretches, _, cols = blocks_ref.shape
    heads = cols // ATTEND_DIM
    half = ATTEND_DIM // 2
    for b in range(stretches):
        lines = dot_nt(pick_ref[...], blocks_ref[where_ref[0] ^ b])
        for h in range(heads):
            at = 2 * h * half
            pairs = jnp.concatenate([lines[at : at + half], lines[at + half : at + 2 * half]], axis=1)
            head = b * heads + h
            for i in range(half):
                out_ref[0, 0, head : head + 1, 2 * i * ATTEND_DIM : 2 * (i + 1) * ATTEND_DIM] = pairs[i : i + 1]


def states_laid(prompt, prompts, where, blocks, earlier):
    stretches, lines, cols = blocks.shape
    heads = cols // ATTEND_DIM
    order = np.arange(cols).reshape(heads, ATTEND_DIM // 2, 2).transpose(0, 2, 1).reshape(-1)
    pick = jnp.asarray(order[:, None] == np.arange(cols)[None, :], bf16)
    shape = (1, 1, stretches * heads, ATTEND_DIM * ATTEND_DIM)
    return pl.pallas_call(
        states_kernel,
        grid_spec=pltpu.PrefetchScalarGridSpec(
            num_scalar_prefetch=1,
            grid=(1,),
            in_specs=[
                pl.BlockSpec((stretches, ATTEND_DIM, cols), lambda n, w: (0, lines // ATTEND_DIM - 1, 0)),
                pl.BlockSpec((cols, cols), lambda n, w: (0, 0)),
            ]
            + [pl.BlockSpec(memory_space=pl.ANY)] * len(earlier),
            out_specs=pl.BlockSpec(shape, lambda n, w: (prompt, 0, 0, 0)),
        ),
        out_shape=jax.ShapeDtypeStruct((prompts, *shape[1:]), f32),
        input_output_aliases={3: 0} if earlier else {},
        compiler_params=vmem(32),
        cost_estimate=SMALL,
    )(where, blocks, pick, *earlier)


def moved(value, axis, by):
    peers = lax.axis_size(axis)
    return lax.ppermute(value, axis, [(i, i + by) for i in range(peers) if 0 <= i + by < peers])


def local(
    incoming_activations,
    standardize_scaling,
    lagged_blending_weights,
    learner_line_permutation,
    learner_acceptor_lookup_slices,
    learner_projection_slices,
    fading_left_matrix,
    fading_right_matrix,
    feature_fading_speed,
    self_reward,
    cluster_scaling_vector,
    prompt_extents,
):
    reqs, span, width = incoming_activations.shape
    rows = reqs * span
    stretches = lax.axis_size("seq")
    cores = lax.axis_size("tensor")
    groups = lax.axis_size("req")
    assert reqs == cores == 2 and stretches == 4
    local_width = feature_fading_speed.shape[0]
    cols = local_width // stretches
    t, s = lax.axis_index("tensor"), lax.axis_index("seq")
    where = jnp.stack([s, t, lax.axis_index("req")]).astype(jnp.int32)

    x = incoming_activations.reshape(rows, width)
    own_x = lax.dynamic_slice_in_dim(x, t * span, span, 0)
    past = moved(own_x[span - PAST :], "seq", 1)
    pieces = [
        lax.dynamic_slice_in_dim(learner_acceptor_lookup_slices, (s ^ d) * cols, cols, 2).astype(bf16)
        for d in range(stretches)
    ]
    out_half = learner_projection_slices.astype(bf16)
    out_lines = lax.all_gather(out_half, "req", axis=0, tiled=False)
    got = [swapped(pieces[d], "seq", d) for d in range(1, stretches)]

    def tied(*values):
        return lax.optimization_barrier(values)

    own_x, past, *_ = tied(own_x, past, out_half, *pieces)
    coeffs = jnp.pad(lagged_blending_weights, ((0, PREFIX - 4), (0, 0)))
    act, coeffs = ordered(
        jnp.concatenate([past, own_x], axis=0),
        standardize_scaling.reshape(1, width),
        coeffs,
        learner_line_permutation.reshape(1, width),
    )
    act, perm, *got = tied(act, learner_line_permutation, *got)
    lines = jnp.stack([pieces[0], *got])
    chained = groups == 4

    def mixed_in(values, side, apart, earlier):
        return shifted(where, values, coeffs, left, side, apart, stretches, earlier)

    left = fading_left_matrix[perm]
    near, other = swapped(act, "seq", 1), swapped(act, "seq", 2)
    hops = [moved(lines, "req", 1), moved(lines, "req", -1)] if chained else [lax.all_gather(lines, "req", axis=0)]
    results = mixed_in(act, 0, 0, ())
    results = mixed_in(swapped(act, "tensor", 1), 1, 0, results)
    share = groups // cores
    def mine(array):
        return lax.dynamic_slice_in_dim(array, s * cols, cols, array.ndim - 1).reshape(-1, cols)

    tables = [mine(a) for a in (fading_right_matrix, feature_fading_speed, self_reward, cluster_scaling_vector)]
    out_lines, *rest = tied(out_lines, *results, *tables)
    results, tables = rest[:2], rest[2:]
    kept = lax.dynamic_slice_in_dim(out_lines, t * share, share, 0)
    given = lax.dynamic_slice_in_dim(out_lines, (1 - t) * share, share, 0)
    out_lines = jnp.stack([kept, swapped(given, "tensor", 1)])
    near, other, out_lines, *rest = tied(near, other, out_lines, *results, *hops)
    results, hops = tuple(rest[:2]), rest[2:]

    cut = (span + PAST) // 32 * 16
    across = [swapped(near[:cut], "seq", 2), swapped(other[cut:], "seq", 1)]
    if chained:
        hops += [moved(hops[0], "req", 1), moved(hops[1], "req", -1)]
    results = mixed_in(near, 0, 1, results)
    results = mixed_in(other, 0, 2, results)
    results = mixed_in(swapped(near, "tensor", 1), 1, 1, results)
    results = mixed_in(swapped(other, "tensor", 1), 1, 2, results)
    out_lines, *rest = tied(out_lines, *results, *hops, *across)
    results, hops, across = tuple(rest[:2]), rest[2:-2], jnp.concatenate(rest[-2:], axis=0)

    near, other = swapped(out_lines, "seq", 1), swapped(out_lines, "seq", 2)
    ends = [moved(hops[2], "req", 1), moved(hops[3], "req", -1)] if chained else []
    last = swapped(across, "tensor", 1)
    results = mixed_in(across, 0, 3, results)
    mixed, lora = mixed_in(last, 1, 3, results)
    if chained:
        proj = projected(where, mixed, [lines, *hops])
    else:
        proj = projected_whole(where, mixed, *hops)
    mixed, proj, near, other, *ends = tied(mixed, proj, near, other, *ends)
    across = [swapped(near[:1], "seq", 2), swapped(other[1:], "seq", 1)]

    def one_prompt(prompt, proj):
        return recurrence(prompt, prompt_extents, where, mixed, proj, ends, lora, *tables)

    def exchanged(block):
        parts = [lax.dynamic_index_in_dim(block, s ^ d, 0, keepdims=False) for d in range(stretches)]
        return parts[:1] + [swapped(parts[d], "seq", d) for d in range(1, stretches)]

    def output(prompt, blocks, earlier):
        far_blocks = swapped(blocks, "tensor", 1)
        return finished(prompt, reqs, where, x, blocks, far_blocks, out_weights, earlier)

    block, proj = tied(one_prompt(0, proj), proj)
    first = exchanged(block)
    block, *rest = tied(one_prompt(1, proj), *first, *across)
    first, across = rest[:-2], rest[-2:]
    second = exchanged(block)
    first = jnp.stack(first)
    out_weights = [out_lines, near, other, *across]
    hidden_out = output(0, first, ())
    stretch_states = states_laid(0, reqs, where, first, ())
    hidden_out, stretch_states, *second = tied(hidden_out, stretch_states, *second)
    second = jnp.stack(second)
    hidden_out = output(1, second, (hidden_out,))
    stretch_states = states_laid(1, reqs, where, second, (stretch_states,))
    return (hidden_out, stretch_states)


def solution(mesh):
    in_specs = (
        P("req", "seq", None),
        P(),
        P(),
        P(),
        P(None, ("req", "seq"), "tensor"),
        P("tensor", ("req", "seq")),
        P(),
        P(None, "tensor"),
        P("tensor"),
        P("tensor"),
        P("tensor"),
        P("req"),
    )
    out_specs = (P("req", "seq", "tensor"), P("req", "seq", "tensor", None))
    return jax.shard_map(local, mesh=mesh, in_specs=in_specs, out_specs=out_specs, check_vma=False)
```

```python
import functools

import jax
import jax.numpy as jnp
import numpy as np
from jax import lax
from jax.experimental import pallas as pl
from jax.experimental.pallas import tpu as pltpu
from jax.sharding import PartitionSpec as P

ATTEND_DIM = 64
CHUNK = 64
LEVELS = 6
PREFIX = 8
PAST = 16

SMALL = pl.CostEstimate(flops=1024, bytes_accessed=1024, transcendentals=0)

eps = 1e-05
bf16 = jnp.bfloat16
f32 = jnp.float32


def dot(a, b):
    return jnp.dot(a, b, preferred_element_type=f32)


def dot_nt(a, b):
    return lax.dot_general(a, b, (((1,), (1,)), ((), ())), preferred_element_type=f32)


def dot_tn(a, b):
    return lax.dot_general(a, b, (((0,), (0,)), ((), ())), preferred_element_type=f32)


def swapped(value, axis, by):
    peers = lax.axis_size(axis)
    return lax.ppermute(value, axis, [(i, i ^ by) for i in range(peers)])


def vmem(mib):
    return pltpu.CompilerParams(vmem_limit_bytes=mib * 2**20)


def order_kernel(x_ref, gain_ref, coeff_ref, perm_ref, out_ref, coeff_out_ref, cur_ref):
    rows, width = x_ref.shape
    block = out_ref.shape[1]
    depth = 256

    @pl.when(pl.program_id(0) == 0)
    def _():
        x = x_ref[...].astype(f32)
        mean = jnp.mean(x, axis=-1, keepdims=True)
        centred = x - mean
        spread = jnp.mean(centred * centred, axis=-1, keepdims=True)
        cur_ref[:rows, :] = (centred * lax.rsqrt(spread + eps) * gain_ref[...]).astype(bf16)
        c = coeff_ref[...]
        high = c.astype(bf16)
        cur_ref[rows:, :] = jnp.concatenate([high, (c - high.astype(f32)).astype(bf16)], axis=0)

    perm = perm_ref[...]
    high, low = perm // depth, (perm % depth).astype(bf16)
    lines = lax.broadcasted_iota(jnp.int32, (depth, block), 0).astype(bf16)
    one, none = jnp.ones((depth, block), bf16), jnp.zeros((depth, block), bf16)
    total = jnp.zeros((rows + 2 * PREFIX, block), f32)
    for k in range(width // depth):
        mine = jnp.where(high == k, low, jnp.full_like(low, -1.0))
        total += dot(cur_ref[:, k * depth : (k + 1) * depth], jnp.where(lines == mine, one, none))
    out_ref[...] = total[:rows].astype(bf16)
    coeff_out_ref[...] = total[rows : rows + PREFIX] + total[rows + PREFIX :]


def ordered(x, gain, coeffs, perm):
    rows, width = x.shape
    block = 512
    return pl.pallas_call(
        order_kernel,
        grid=(width // block,),
        in_specs=[
            pl.BlockSpec((rows, width), lambda n: (0, 0)),
            pl.BlockSpec((1, width), lambda n: (0, 0)),
            pl.BlockSpec((PREFIX, width), lambda n: (0, 0)),
            pl.BlockSpec((1, block), lambda n: (0, n)),
        ],
        out_specs=[
            pl.BlockSpec((rows, block), lambda n: (0, n)),
            pl.BlockSpec((PREFIX, block), lambda n: (0, n)),
        ],
        out_shape=[
            jax.ShapeDtypeStruct((rows, width), bf16),
            jax.ShapeDtypeStruct((PREFIX, width), f32),
        ],
        scratch_shapes=[pltpu.VMEM((rows + 2 * PREFIX, width), bf16)],
        compiler_params=vmem(40),
        cost_estimate=SMALL,
    )(x, gain, coeffs, perm)


def mix_kernel(where_ref, act_ref, coeff_ref, left_ref, *refs):
    mixed_ref, lora_ref, inner_ref = refs[-3:]
    rows, block = mixed_ref.shape[-2:]
    width = 512
    n = pl.program_id(0)
    inner = jnp.zeros(inner_ref.shape, f32)
    for c in range(block // width):
        cols = slice(c * width, (c + 1) * width)
        cur = act_ref[PAST:, cols]
        delta = pltpu.roll(act_ref[:, cols].astype(f32), 1, 0)[PAST:].astype(bf16) - cur
        for j in range(3):
            mixed_ref[j, 0, 0, :, cols] = cur + delta * coeff_ref[j : j + 1, cols].astype(bf16)
        inner += dot(cur + delta * coeff_ref[3:4, cols].astype(bf16), left_ref[cols, :])

    @pl.when(n == 0)
    def _():
        inner_ref[...] = inner

    @pl.when(n > 0)
    def _():
        inner_ref[...] += inner

    @pl.when(n == pl.num_programs(0) - 1)
    def _():
        lora_ref[0, 0] = jnp.tanh(inner_ref[...]).astype(bf16)


def shifted(where, act, coeffs, left, side, apart, stretches, earlier):
    span, width = act.shape[0] - PAST, act.shape[1]
    inner = left.shape[1]
    block = 1024
    kept = pl.BlockSpec(memory_space=pl.ANY)
    return pl.pallas_call(
        mix_kernel,
        grid_spec=pltpu.PrefetchScalarGridSpec(
            num_scalar_prefetch=1,
            grid=(width // block,),
            in_specs=[
                pl.BlockSpec((span + PAST, block), lambda n, w: (0, n)),
                pl.BlockSpec((PREFIX, block), lambda n, w: (0, n)),
                pl.BlockSpec((block, inner), lambda n, w: (n, 0)),
            ]
            + [kept] * len(earlier),
            out_specs=[
                pl.BlockSpec((3, 1, 1, span, block), lambda n, w: (0, side, w[0] ^ apart, 0, n)),
                pl.BlockSpec((1, 1, span, inner), lambda n, w: (side, w[0] ^ apart, 0, 0)),
            ],
            scratch_shapes=[pltpu.VMEM((span, inner), f32)],
        ),
        out_shape=[
            jax.ShapeDtypeStruct((3, 2, stretches, span, width), bf16),
            jax.ShapeDtypeStruct((2, stretches, span, inner), bf16),
        ],
        input_output_aliases={4: 0, 5: 1} if earlier else {},
        compiler_params=vmem(32),
        cost_estimate=SMALL,
    )(where, act, coeffs, left, *earlier)


def project_kernel(where_ref, act_ref, *refs):
    *hops, out_ref, lines_ref = refs
    stretches, _, depth, _ = hops[0].shape
    reqs = lines_ref.shape[0] // (stretches * depth)
    reach = len(hops) // 2

    def place(r, values):
        for d in range(stretches):
            at = (r * stretches + (where_ref[0] ^ d)) * depth
            lines_ref[pl.ds(pl.multiple_of(at, depth), depth), :] = values(d)

    @pl.when(pl.program_id(1) == 0)
    def _():
        me = where_ref[2]
        place(me, lambda d: hops[0][d, 0])
        for hop in range(1, reqs):
            for r, ref in ((me - hop, 2 * hop - 1), (me + hop, 2 * hop)):

                @pl.when((r >= 0) & (r < reqs))
                def _():
                    if hop > reach:
                        place(r, lambda d: jnp.zeros_like(hops[0][d, 0]))
                    else:
                        place(r, lambda d: hops[ref][d, 0])

    act = act_ref[0, 0].reshape(-1, act_ref.shape[-1])
    half = act.shape[1] // 2
    total = dot(act[:, :half], lines_ref[:half, :]) + dot(act[:, half:], lines_ref[half:, :])
    out_ref[0, 0] = total.reshape(out_ref.shape[2:])


def projected(where, mixed, hops):
    stretches, kinds, depth, cols = hops[0].shape
    _, sides, _, span, width = mixed.shape
    return pl.pallas_call(
        project_kernel,
        grid_spec=pltpu.PrefetchScalarGridSpec(
            num_scalar_prefetch=1,
            grid=(kinds, sides),
            in_specs=[pl.BlockSpec((1, 1, stretches, span, width), lambda j, m, w: (j, m, 0, 0, 0))]
            + [pl.BlockSpec((stretches, 1, depth, cols), lambda j, m, w: (0, j, 0, 0))] * len(hops),
            out_specs=pl.BlockSpec((1, 1, stretches, span, cols), lambda j, m, w: (j, m, 0, 0, 0)),
            scratch_shapes=[pltpu.VMEM((width, cols), bf16)],
        ),
        out_shape=jax.ShapeDtypeStruct((kinds, sides, stretches, span, cols), f32),
        compiler_params=vmem(60),
        cost_estimate=SMALL,
    )(where, mixed, *hops)


def projected_whole(where, mixed, lines):
    _, stretches, kinds, depth, cols = lines.shape
    lines = lines[:, jnp.arange(stretches) ^ where[0]]
    lines = jnp.transpose(lines, (2, 0, 1, 3, 4)).reshape(kinds, mixed.shape[-1], cols)
    return jnp.einsum("jxbtk,jkc->jxbtc", mixed, lines, preferred_element_type=f32).astype(bf16)


def decay_sums():
    place = np.arange(CHUNK)
    of, by = place[:, None], place[None, :]
    parts = []
    for level in range(LEVELS):
        half = 1 << level
        middle = (of // (2 * half)) * 2 * half + half - 1
        later = (of % (2 * half)) >= half
        parts.append(np.where(later, (by > middle) & (by < of), (by > of) & (by <= middle)))
    parts += [by < of, by > of, np.ones((8, CHUNK), bool)]
    sums = np.concatenate(parts).astype(np.float32)
    return np.concatenate([sums, sums], axis=1)


def pair_levels(heads):
    of, by = np.arange(CHUNK)[:, None], np.arange(CHUNK)[None, :]
    level = np.full((CHUNK, CHUNK), -1.0, np.float32)
    for bit in range(LEVELS):
        level[((of ^ by) >> bit) == 1] = bit
    return np.tile(np.where(of > by, level, -1.0).astype(np.float32), (1, heads))


def wkv_kernel(extent_ref, where_ref, *refs, prompt, parted):
    if parted:
        act_ref, below_ref, above_ref, *refs, lines_ref = refs
    proj_ref, lora_ref, right_ref, speed_ref, reward_ref, scale_ref, sums_ref, level_ref, same_ref, *refs = refs
    out_ref, memory_ref = refs
    step = pl.program_id(0)
    tokens, cols = proj_ref.shape[3:]
    heads = cols // ATTEND_DIM
    same = same_ref[...]
    same_f32 = same.astype(f32)
    level = level_ref[...]

    @pl.when(step == 0)
    def _():
        memory_ref[...] = jnp.zeros_like(memory_ref)
        if parted:
            stretches, kinds, depth, _ = below_ref.shape
            for d in range(stretches):
                at = pl.ds(pl.multiple_of((where_ref[0] ^ d) * depth, depth), depth)
                for j in range(kinds):
                    lines_ref[j, at, :] = below_ref[d, j] + above_ref[d, j]

    def projection(j):
        if not parted:
            return proj_ref[j, 0, 0]
        return (proj_ref[j, 0, 0] + dot(act_ref[j, 0, 0], lines_ref[j])).astype(bf16)

    at = step * tokens + lax.broadcasted_iota(jnp.int32, (tokens, cols), 0)
    valid = jnp.where(at < extent_ref[prompt], 1.0, 0.0)
    r = projection(0)
    k = projection(1) * valid.astype(bf16)
    v = projection(2)
    decay = -speed_ref[...] * jnp.exp(dot(lora_ref[0, 0], right_ref[...])) * valid
    high = decay.astype(bf16)
    low = (decay - high.astype(f32)).astype(bf16)
    own = dot((r.astype(f32) * reward_ref[...] * k.astype(f32)).astype(bf16), same) * v.astype(f32)

    memory = memory_ref[...]
    rows = []
    for sub in range(tokens // CHUNK):
        lines = slice(sub * CHUNK, (sub + 1) * CHUNK)
        r_sub, k_sub, v_sub = r[lines], k[lines], v[lines]
        kept = jnp.exp(dot(sums_ref[...], jnp.concatenate([high[lines], low[lines]], axis=0)))
        scores = jnp.zeros((CHUNK, heads * CHUNK), f32)
        for bit in range(LEVELS):
            part = kept[bit * CHUNK : (bit + 1) * CHUNK].astype(bf16)
            lookup = jnp.concatenate([k_sub * part] * heads, axis=0) * same
            scores = jnp.where(level == bit, dot_nt(r_sub * part, lookup), scores)
        v_heads = jnp.concatenate([v_sub] * heads, axis=0) * same
        from_start = r_sub * kept[LEVELS * CHUNK : (LEVELS + 1) * CHUNK].astype(bf16)
        to_end = k_sub * kept[(LEVELS + 1) * CHUNK : (LEVELS + 2) * CHUNK].astype(bf16)
        whole = kept[(LEVELS + 2) * CHUNK : (LEVELS + 2) * CHUNK + 1]
        rows.append(dot_nt(from_start, memory.astype(bf16)) + dot(scores.astype(bf16), v_heads))
        memory = memory * whole + same_f32 * dot_tn(v_sub, to_end)
    memory_ref[...] = memory
    folded = memory[:ATTEND_DIM]
    for h in range(1, heads):
        folded += memory[h * ATTEND_DIM : (h + 1) * ATTEND_DIM]
    out_ref[0, tokens:] = folded.astype(bf16)

    y = jnp.concatenate(rows, axis=0) + own
    y_high = y.astype(bf16)
    y_low = (y - y_high.astype(f32)).astype(bf16)
    centred = y - (dot(y_high, same) + dot(y_low, same)) * (1.0 / ATTEND_DIM)
    spread = dot((centred * centred).astype(bf16), same) * (1.0 / ATTEND_DIM)
    out_ref[0, :tokens] = (centred * lax.rsqrt(spread + eps) * scale_ref[...] * valid).astype(bf16)


def recurrence(prompt, extents, where, mixed, proj, ends, lora, right, speed, reward, scale):
    kinds, _, stretches, span, cols = proj.shape
    width = mixed.shape[-1]
    inner = lora.shape[-1]
    heads = cols // ATTEND_DIM
    sums = jnp.asarray(decay_sums(), bf16)
    level = jnp.asarray(pair_levels(heads), f32)
    head = np.arange(cols) // ATTEND_DIM
    same = jnp.asarray(head[:, None] == head[None, :], bf16)

    def fixed(array):
        return pl.BlockSpec(array.shape, lambda c, e, w: (0,) * array.ndim)

    tables = (right, speed, reward, scale, sums, level, same)
    first, first_specs, scratch = (), [], [pltpu.VMEM((cols, cols), f32)]
    if ends:
        share = stretches * ends[0].shape[2]
        last = width // share - 1
        first = (mixed, *ends)
        first_specs = [
            pl.BlockSpec(
                (kinds, 1, 1, span, share),
                lambda c, e, w: (0, w[1] ^ prompt, c, 0, jnp.where(w[2] == last, 0, last)),
            ),
            *map(fixed, ends),
        ]
        scratch.append(pltpu.VMEM((kinds, share, cols), bf16))
    return pl.pallas_call(
        functools.partial(wkv_kernel, prompt=prompt, parted=bool(ends)),
        grid_spec=pltpu.PrefetchScalarGridSpec(
            num_scalar_prefetch=2,
            grid=(stretches,),
            in_specs=first_specs
            + [
                pl.BlockSpec((kinds, 1, 1, span, cols), lambda c, e, w: (0, w[1] ^ prompt, c, 0, 0)),
                pl.BlockSpec((1, 1, span, inner), lambda c, e, w: (w[1] ^ prompt, c, 0, 0)),
            ]
            + [fixed(a) for a in tables],
            out_specs=pl.BlockSpec((1, span + ATTEND_DIM, cols), lambda c, e, w: (c, 0, 0)),
            scratch_shapes=scratch,
        ),
        out_shape=jax.ShapeDtypeStruct((stretches, span + ATTEND_DIM, cols), bf16),
        compiler_params=vmem(56),
        cost_estimate=SMALL,
    )(extents, where, *first, proj, lora, *tables)


def finish_kernel(where_ref, x_ref, own_ref, far_ref, *refs):
    weights, out_ref = refs[:5], refs[-1]
    stretches, rows, cols = own_ref.shape
    chunk = weights[0].shape[-1]
    for e in range(stretches):
        places = pl.ds(pl.multiple_of((where_ref[0] ^ e) * chunk, chunk), chunk)
        total = x_ref[:, places].astype(f32)
        for side, lines_ref in enumerate((own_ref, far_ref)):
            w_ref = weights[e].at[side, 0] if e < 3 else weights[e + side].at[0, 0]
            for d in range(stretches):
                at = pl.ds(pl.multiple_of((where_ref[0] ^ d) * cols, cols), cols)
                total += dot(lines_ref[d], w_ref[at, :])
        out_ref[0, :, places] = total.astype(bf16)


def finished(prompt, prompts, where, x, own, far, weights, earlier):
    stretches, _, cols = own.shape
    rows = x.shape[0] // prompts
    _, groups, depth, chunk = weights[0].shape
    share = groups * stretches * chunk
    if chunk % 128:
        order = jnp.arange(stretches) ^ where[0]
        total = lax.dynamic_slice(x, (prompt * rows, where[1] * share), (rows, share)).astype(f32)
        weights = [*weights[:3], jnp.concatenate(weights[3:])]
        for side, lines in enumerate((own, far)):
            w = jnp.stack([w[side] for w in weights])[order]
            w = jnp.transpose(w, (2, 1, 0, 3)).reshape(depth, share)
            lines = jnp.transpose(lines[order, :rows], (1, 0, 2)).reshape(rows, depth)
            total += dot(lines, w)
        return jnp.concatenate([*earlier, total.astype(bf16)[None]], axis=0)
    block = stretches * chunk
    lines_spec = pl.BlockSpec((stretches, rows, cols), lambda g, w: (0, 0, 0))
    return pl.pallas_call(
        finish_kernel,
        grid_spec=pltpu.PrefetchScalarGridSpec(
            num_scalar_prefetch=1,
            grid=(groups,),
            in_specs=[pl.BlockSpec((rows, block), lambda g, w: (prompt, w[1] * groups + g)), lines_spec, lines_spec]
            + [pl.BlockSpec((a.shape[0], 1, depth, chunk), lambda g, w: (0, g, 0, 0)) for a in weights]
            + [pl.BlockSpec(memory_space=pl.ANY)] * len(earlier),
            out_specs=pl.BlockSpec((1, rows, block), lambda g, w: (prompt, 0, g)),
        ),
        out_shape=jax.ShapeDtypeStruct((prompts, rows, share), bf16),
        input_output_aliases={9: 0} if earlier else {},
        compiler_params=vmem(48),
        cost_estimate=SMALL,
    )(where, x, own, far, *weights, *earlier)


def states_kernel(where_ref, blocks_ref, pick_ref, *refs):
    out_ref = refs[-1]
    stretches, _, cols = blocks_ref.shape
    heads = cols // ATTEND_DIM
    half = ATTEND_DIM // 2
    for b in range(stretches):
        lines = dot_nt(pick_ref[...], blocks_ref[where_ref[0] ^ b])
        for h in range(heads):
            at = 2 * h * half
            pairs = jnp.concatenate([lines[at : at + half], lines[at + half : at + 2 * half]], axis=1)
            head = b * heads + h
            for i in range(half):
                out_ref[0, 0, head : head + 1, 2 * i * ATTEND_DIM : 2 * (i + 1) * ATTEND_DIM] = pairs[i : i + 1]


def states_laid(prompt, prompts, where, blocks, earlier):
    stretches, lines, cols = blocks.shape
    heads = cols // ATTEND_DIM
    order = np.arange(cols).reshape(heads, ATTEND_DIM // 2, 2).transpose(0, 2, 1).reshape(-1)
    pick = jnp.asarray(order[:, None] == np.arange(cols)[None, :], bf16)
    shape = (1, 1, stretches * heads, ATTEND_DIM * ATTEND_DIM)
    return pl.pallas_call(
        states_kernel,
        grid_spec=pltpu.PrefetchScalarGridSpec(
            num_scalar_prefetch=1,
            grid=(1,),
            in_specs=[
                pl.BlockSpec((stretches, ATTEND_DIM, cols), lambda n, w: (0, lines // ATTEND_DIM - 1, 0)),
                pl.BlockSpec((cols, cols), lambda n, w: (0, 0)),
            ]
            + [pl.BlockSpec(memory_space=pl.ANY)] * len(earlier),
            out_specs=pl.BlockSpec(shape, lambda n, w: (prompt, 0, 0, 0)),
        ),
        out_shape=jax.ShapeDtypeStruct((prompts, *shape[1:]), f32),
        input_output_aliases={3: 0} if earlier else {},
        compiler_params=vmem(32),
        cost_estimate=SMALL,
    )(where, blocks, pick, *earlier)


def tied(*values):
    return lax.optimization_barrier(values)


def moved(value, axis, by):
    peers = lax.axis_size(axis)
    return lax.ppermute(value, axis, [(i, i + by) for i in range(peers) if 0 <= i + by < peers])


def local(
    incoming_activations,
    standardize_scaling,
    lagged_blending_weights,
    learner_line_permutation,
    learner_acceptor_lookup_slices,
    learner_projection_slices,
    fading_left_matrix,
    fading_right_matrix,
    feature_fading_speed,
    self_reward,
    cluster_scaling_vector,
    prompt_extents,
):
    reqs, span, width = incoming_activations.shape
    rows = reqs * span
    stretches = lax.axis_size("seq")
    cores = lax.axis_size("tensor")
    groups = lax.axis_size("req")
    assert reqs == cores == 2 and stretches == 4
    local_width = feature_fading_speed.shape[0]
    cols = local_width // stretches
    t, s = lax.axis_index("tensor"), lax.axis_index("seq")
    where = jnp.stack([s, t, lax.axis_index("req")]).astype(jnp.int32)

    x = incoming_activations.reshape(rows, width)
    own_x = lax.dynamic_slice_in_dim(x, t * span, span, 0)
    past = moved(own_x[span - PAST :], "seq", 1)
    out_half, shards = tied(learner_projection_slices.astype(bf16), learner_acceptor_lookup_slices)
    out_lines = lax.all_gather(out_half, "req", axis=0, tiled=False)
    pieces = [
        lax.dynamic_slice_in_dim(shards, (s ^ d) * cols, cols, 2).astype(bf16)
        for d in range(stretches)
    ]
    got = [swapped(pieces[d], "seq", d) for d in range(1, stretches)]

    own_x, past, *_ = tied(own_x, past, *pieces)
    coeffs = jnp.pad(lagged_blending_weights, ((0, PREFIX - 4), (0, 0)))
    act, coeffs = ordered(
        jnp.concatenate([past, own_x], axis=0),
        standardize_scaling.reshape(1, width),
        coeffs,
        learner_line_permutation.reshape(1, width),
    )
    act, perm, *got = tied(act, learner_line_permutation, *got)
    lines = jnp.stack([pieces[0], *got])
    chained = groups == 4

    def mixed_in(values, side, apart, earlier):
        return shifted(where, values, coeffs, left, side, apart, stretches, earlier)

    left = fading_left_matrix[perm]
    near, other = swapped(act, "seq", 1), swapped(act, "seq", 2)
    hops = [moved(lines, "req", 1), moved(lines, "req", -1)] if chained else [lax.all_gather(lines, "req", axis=0)]
    results = mixed_in(act, 0, 0, ())
    results = mixed_in(swapped(act, "tensor", 1), 1, 0, results)
    share = groups // cores
    def mine(array):
        return lax.dynamic_slice_in_dim(array, s * cols, cols, array.ndim - 1).reshape(-1, cols)

    tables = (fading_right_matrix, feature_fading_speed, self_reward, cluster_scaling_vector)
    out_lines, *rest = tied(out_lines, *results, *tables)
    results, tables = rest[:2], [mine(a) for a in rest[2:]]
    kept = lax.dynamic_slice_in_dim(out_lines, t * share, share, 0)
    given = lax.dynamic_slice_in_dim(out_lines, (1 - t) * share, share, 0)
    out_lines = jnp.stack([kept, swapped(given, "tensor", 1)])
    near, other, out_lines, *rest = tied(near, other, out_lines, *results, *tables, *hops)
    results, tables, hops = tuple(rest[:2]), rest[2:6], rest[6:]

    cut = (span + PAST) // 32 * 16
    across = [swapped(near[:cut], "seq", 2), swapped(other[cut:], "seq", 1)]
    if chained:
        hops += [moved(hops[0], "req", 1), moved(hops[1], "req", -1)]
    results = mixed_in(near, 0, 1, results)
    results = mixed_in(other, 0, 2, results)
    results = mixed_in(swapped(near, "tensor", 1), 1, 1, results)
    results = mixed_in(swapped(other, "tensor", 1), 1, 2, results)
    out_lines, *rest = tied(out_lines, *results, *across)
    results, across = tuple(rest[:2]), rest[2:]
    near, other = swapped(out_lines, "seq", 1), swapped(out_lines, "seq", 2)
    across = jnp.concatenate(across, axis=0)
    across, *hops = tied(across, *hops)

    ends = [moved(hops[2], "req", 1), moved(hops[3], "req", -1)] if chained else []
    last = swapped(across, "tensor", 1)
    results = mixed_in(across, 0, 3, results)
    mixed, lora = mixed_in(last, 1, 3, results)
    if chained:
        proj = projected(where, mixed, [lines, *hops])
    else:
        proj = projected_whole(where, mixed, *hops)
    mixed, proj, near, other, *ends = tied(mixed, proj, near, other, *ends)
    across = [swapped(near[:1], "seq", 2), swapped(other[1:], "seq", 1)]

    def one_prompt(prompt, proj):
        return recurrence(prompt, prompt_extents, where, mixed, proj, ends, lora, *tables)

    def exchanged(block):
        parts = [lax.dynamic_index_in_dim(block, s ^ d, 0, keepdims=False) for d in range(stretches)]
        return parts[:1] + [swapped(parts[d], "seq", d) for d in range(1, stretches)]

    def output(prompt, blocks, earlier):
        far_blocks = swapped(blocks, "tensor", 1)
        return finished(prompt, reqs, where, x, blocks, far_blocks, out_weights, earlier)

    block, proj = tied(one_prompt(0, proj), proj)
    first = exchanged(block)
    block, *rest = tied(one_prompt(1, proj), *first, *across)
    first, across = rest[:-2], rest[-2:]
    second = exchanged(block)
    first = jnp.stack(first)
    out_weights = [out_lines, near, other, *across]
    hidden_out = output(0, first, ())
    stretch_states = states_laid(0, reqs, where, first, ())
    hidden_out, stretch_states, *second = tied(hidden_out, stretch_states, *second)
    second = jnp.stack(second)
    hidden_out = output(1, second, (hidden_out,))
    stretch_states = states_laid(1, reqs, where, second, (stretch_states,))
    return (hidden_out, stretch_states)


def solution(mesh):
    in_specs = (
        P("req", "seq", None),
        P(),
        P(),
        P(),
        P(None, ("req", "seq"), "tensor"),
        P("tensor", ("req", "seq")),
        P(),
        P(None, "tensor"),
        P("tensor"),
        P("tensor"),
        P("tensor"),
        P("req"),
    )
    out_specs = (P("req", "seq", "tensor"), P("req", "seq", "tensor", None))
    return jax.shard_map(local, mesh=mesh, in_specs=in_specs, out_specs=out_specs, check_vma=False)
```

```python
import functools

import jax
import jax.numpy as jnp
import numpy as np
from jax import lax
from jax.experimental import pallas as pl
from jax.experimental.pallas import tpu as pltpu
from jax.sharding import PartitionSpec as P

ATTEND_DIM = 64
CHUNK = 64
LEVELS = 6
PREFIX = 8
PAST = 16

SMALL = pl.CostEstimate(flops=1024, bytes_accessed=1024, transcendentals=0)

eps = 1e-05
bf16 = jnp.bfloat16
f32 = jnp.float32


def dot(a, b):
    return jnp.dot(a, b, preferred_element_type=f32)


def dot_nt(a, b):
    return lax.dot_general(a, b, (((1,), (1,)), ((), ())), preferred_element_type=f32)


def dot_tn(a, b):
    return lax.dot_general(a, b, (((0,), (0,)), ((), ())), preferred_element_type=f32)


def swapped(value, axis, by):
    peers = lax.axis_size(axis)
    return lax.ppermute(value, axis, [(i, i ^ by) for i in range(peers)])


def vmem(mib):
    return pltpu.CompilerParams(vmem_limit_bytes=mib * 2**20)


def order_kernel(where_ref, past_ref, x_ref, gain_ref, coeff_ref, perm_ref, out_ref, coeff_out_ref, cur_ref):
    rows, block = out_ref.shape
    width = x_ref.shape[1]
    depth = 256

    @pl.when(pl.program_id(0) == 0)
    def _():
        x = jnp.concatenate([past_ref[...], x_ref[...]], axis=0).astype(f32)
        mean = jnp.mean(x, axis=-1, keepdims=True)
        centred = x - mean
        spread = jnp.mean(centred * centred, axis=-1, keepdims=True)
        cur_ref[:rows, :] = (centred * lax.rsqrt(spread + eps) * gain_ref[...]).astype(bf16)
        c = coeff_ref[...]
        high = c.astype(bf16)
        cur_ref[rows:, :] = jnp.concatenate([high, (c - high.astype(f32)).astype(bf16)], axis=0)

    perm = perm_ref[...]
    high, low = perm // depth, (perm % depth).astype(bf16)
    lines = lax.broadcasted_iota(jnp.int32, (depth, block), 0).astype(bf16)
    one, none = jnp.ones((depth, block), bf16), jnp.zeros((depth, block), bf16)
    total = jnp.zeros((rows + 2 * PREFIX, block), f32)
    for k in range(width // depth):
        mine = jnp.where(high == k, low, jnp.full_like(low, -1.0))
        total += dot(cur_ref[:, k * depth : (k + 1) * depth], jnp.where(lines == mine, one, none))
    out_ref[...] = total[:rows].astype(bf16)
    coeff_out_ref[...] = total[rows : rows + PREFIX] + total[rows + PREFIX :]


def ordered(where, past, x, gain, coeffs, perm):
    span, width = x.shape[0] // 2, x.shape[1]
    rows = span + PAST
    block = 512
    return pl.pallas_call(
        order_kernel,
        grid_spec=pltpu.PrefetchScalarGridSpec(
            num_scalar_prefetch=1,
            grid=(width // block,),
            in_specs=[
                pl.BlockSpec((PAST, width), lambda n, w: (0, 0)),
                pl.BlockSpec((span, width), lambda n, w: (w[1], 0)),
                pl.BlockSpec((1, width), lambda n, w: (0, 0)),
                pl.BlockSpec((PREFIX, width), lambda n, w: (0, 0)),
                pl.BlockSpec((1, block), lambda n, w: (0, n)),
            ],
            out_specs=[
                pl.BlockSpec((rows, block), lambda n, w: (0, n)),
                pl.BlockSpec((PREFIX, block), lambda n, w: (0, n)),
            ],
            scratch_shapes=[pltpu.VMEM((rows + 2 * PREFIX, width), bf16)],
        ),
        out_shape=[
            jax.ShapeDtypeStruct((rows, width), bf16),
            jax.ShapeDtypeStruct((PREFIX, width), f32),
        ],
        compiler_params=vmem(40),
        cost_estimate=SMALL,
    )(where, past, x, gain, coeffs, perm)


def mix_kernel(where_ref, act_ref, coeff_ref, left_ref, *refs):
    mixed_ref, lora_ref, inner_ref = refs[-3:]
    rows, block = mixed_ref.shape[-2:]
    width = 512
    n = pl.program_id(0)
    inner = jnp.zeros(inner_ref.shape, f32)
    for c in range(block // width):
        cols = slice(c * width, (c + 1) * width)
        cur = act_ref[PAST:, cols]
        delta = pltpu.roll(act_ref[:, cols].astype(f32), 1, 0)[PAST:].astype(bf16) - cur
        for j in range(3):
            mixed_ref[j, 0, 0, :, cols] = cur + delta * coeff_ref[j : j + 1, cols].astype(bf16)
        inner += dot(cur + delta * coeff_ref[3:4, cols].astype(bf16), left_ref[cols, :])

    @pl.when(n == 0)
    def _():
        inner_ref[...] = inner

    @pl.when(n > 0)
    def _():
        inner_ref[...] += inner

    @pl.when(n == pl.num_programs(0) - 1)
    def _():
        lora_ref[0, 0] = jnp.tanh(inner_ref[...]).astype(bf16)


def shifted(where, act, coeffs, left, side, apart, stretches, earlier):
    span, width = act.shape[-2] - PAST, act.shape[-1]
    inner = left.shape[1]
    block = 1024
    act_spec = pl.BlockSpec((span + PAST, block), lambda n, w: (0, n))
    if act.ndim == 3:
        act_spec = pl.BlockSpec((None, span + PAST, block), lambda n, w: (1 - w[1], 0, n))
    kept = pl.BlockSpec(memory_space=pl.ANY)
    return pl.pallas_call(
        mix_kernel,
        grid_spec=pltpu.PrefetchScalarGridSpec(
            num_scalar_prefetch=1,
            grid=(width // block,),
            in_specs=[
                act_spec,
                pl.BlockSpec((PREFIX, block), lambda n, w: (0, n)),
                pl.BlockSpec((block, inner), lambda n, w: (n, 0)),
            ]
            + [kept] * len(earlier),
            out_specs=[
                pl.BlockSpec((3, 1, 1, span, block), lambda n, w: (0, side, w[0] ^ apart, 0, n)),
                pl.BlockSpec((1, 1, span, inner), lambda n, w: (side, w[0] ^ apart, 0, 0)),
            ],
            scratch_shapes=[pltpu.VMEM((span, inner), f32)],
        ),
        out_shape=[
            jax.ShapeDtypeStruct((3, 2, stretches, span, width), bf16),
            jax.ShapeDtypeStruct((2, stretches, span, inner), bf16),
        ],
        input_output_aliases={4: 0, 5: 1} if earlier else {},
        compiler_params=vmem(32),
        cost_estimate=SMALL,
    )(where, act, coeffs, left, *earlier)


def project_kernel(where_ref, *refs):
    *refs, out_ref, lines_ref = refs
    parts = where_ref[2] // 2
    acts, hops = refs[:3], refs[3:]
    stretches, _, depth, _ = hops[0].shape
    share = stretches * depth

    def place(r, ref):
        slot = r - parts

        @pl.when((slot >= 0) & (slot < len(acts)))
        def _():
            for d in range(stretches):
                at = slot * share + (where_ref[0] ^ d) * depth
                lines_ref[pl.ds(pl.multiple_of(at, depth), depth), :] = ref[d, 0]

    @pl.when(pl.program_id(1) == 0)
    def _():
        place(where_ref[2], hops[0])
        for hop in range(1, len(hops) // 2 + 1):
            place(where_ref[2] - hop, hops[2 * hop - 1])
            place(where_ref[2] + hop, hops[2 * hop])

    total = None
    for i, act_ref in enumerate(acts):
        found = dot(act_ref[0, 0].reshape(-1, share), lines_ref[i * share : (i + 1) * share, :])
        total = found if total is None else total + found
    out_ref[0, 0] = total.reshape(out_ref.shape[2:])


def projected(where, mixed, hops):
    stretches, kinds, depth, cols = hops[0].shape
    _, sides, _, span, width = mixed.shape
    share = stretches * depth
    parts = width // share - 1

    def act_spec(i):
        return pl.BlockSpec((1, 1, stretches, span, share), lambda j, m, w: (j, m, 0, 0, w[2] // 2 + i))

    return pl.pallas_call(
        project_kernel,
        grid_spec=pltpu.PrefetchScalarGridSpec(
            num_scalar_prefetch=1,
            grid=(kinds, sides),
            in_specs=[act_spec(i) for i in range(parts)]
            + [pl.BlockSpec((stretches, 1, depth, cols), lambda j, m, w: (0, j, 0, 0))] * len(hops),
            out_specs=pl.BlockSpec((1, 1, stretches, span, cols), lambda j, m, w: (j, m, 0, 0, 0)),
            scratch_shapes=[pltpu.VMEM((parts * share, cols), bf16)],
        ),
        out_shape=jax.ShapeDtypeStruct((kinds, sides, stretches, span, cols), f32),
        compiler_params=vmem(60),
        cost_estimate=SMALL,
    )(where, *[mixed] * parts, *hops)


def projected_whole(where, mixed, lines):
    _, stretches, kinds, depth, cols = lines.shape
    lines = lines[:, jnp.arange(stretches) ^ where[0]]
    lines = jnp.transpose(lines, (2, 0, 1, 3, 4)).reshape(kinds, mixed.shape[-1], cols)
    return jnp.einsum("jxbtk,jkc->jxbtc", mixed, lines, preferred_element_type=f32).astype(bf16)


def decay_sums():
    place = np.arange(CHUNK)
    of, by = place[:, None], place[None, :]
    parts = []
    for level in range(LEVELS):
        half = 1 << level
        middle = (of // (2 * half)) * 2 * half + half - 1
        later = (of % (2 * half)) >= half
        parts.append(np.where(later, (by > middle) & (by < of), (by > of) & (by <= middle)))
    parts += [by < of, by > of, np.ones((8, CHUNK), bool)]
    sums = np.concatenate(parts).astype(np.float32)
    return np.concatenate([sums, sums], axis=1)


def pair_levels(heads):
    of, by = np.arange(CHUNK)[:, None], np.arange(CHUNK)[None, :]
    level = np.full((CHUNK, CHUNK), -1.0, np.float32)
    for bit in range(LEVELS):
        level[((of ^ by) >> bit) == 1] = bit
    return np.tile(np.where(of > by, level, -1.0).astype(np.float32), (1, heads))


def wkv_kernel(extent_ref, where_ref, *refs, prompt, parted):
    if parted:
        act_ref, *last_refs = refs[:5]
        *refs, lines_ref = refs[5:]
    proj_ref, lora_ref, right_ref, speed_ref, reward_ref, scale_ref, sums_ref, level_ref, same_ref, *refs = refs
    out_ref, memory_ref = refs
    step = pl.program_id(0)
    tokens, cols = proj_ref.shape[3:]
    heads = cols // ATTEND_DIM
    same = same_ref[...]
    same_f32 = same.astype(f32)
    level = level_ref[...]

    @pl.when(step == 0)
    def _():
        memory_ref[...] = jnp.zeros_like(memory_ref)
        if parted:
            for r, last_ref in enumerate(last_refs):

                @pl.when(where_ref[2] == r)
                def _():
                    stretches, kinds, depth, _ = last_ref.shape
                    for d in range(stretches):
                        at = pl.ds(pl.multiple_of((where_ref[0] ^ d) * depth, depth), depth)
                        for j in range(kinds):
                            lines_ref[j, at, :] = last_ref[d, j]

    def projection(j):
        if not parted:
            return proj_ref[j, 0, 0]
        return (proj_ref[j, 0, 0] + dot(act_ref[j, 0, 0], lines_ref[j])).astype(bf16)

    at = step * tokens + lax.broadcasted_iota(jnp.int32, (tokens, cols), 0)
    valid = jnp.where(at < extent_ref[prompt], 1.0, 0.0)
    r = projection(0)
    k = projection(1) * valid.astype(bf16)
    v = projection(2)
    decay = -speed_ref[...] * jnp.exp(dot(lora_ref[0, 0], right_ref[...])) * valid
    high = decay.astype(bf16)
    low = (decay - high.astype(f32)).astype(bf16)
    own = dot((r.astype(f32) * reward_ref[...] * k.astype(f32)).astype(bf16), same) * v.astype(f32)

    memory = memory_ref[...]
    rows = []
    for sub in range(tokens // CHUNK):
        lines = slice(sub * CHUNK, (sub + 1) * CHUNK)
        r_sub, k_sub, v_sub = r[lines], k[lines], v[lines]
        kept = jnp.exp(dot(sums_ref[...], jnp.concatenate([high[lines], low[lines]], axis=0)))
        scores = jnp.zeros((CHUNK, heads * CHUNK), f32)
        for bit in range(LEVELS):
            part = kept[bit * CHUNK : (bit + 1) * CHUNK].astype(bf16)
            lookup = jnp.concatenate([k_sub * part] * heads, axis=0) * same
            scores = jnp.where(level == bit, dot_nt(r_sub * part, lookup), scores)
        v_heads = jnp.concatenate([v_sub] * heads, axis=0) * same
        from_start = r_sub * kept[LEVELS * CHUNK : (LEVELS + 1) * CHUNK].astype(bf16)
        to_end = k_sub * kept[(LEVELS + 1) * CHUNK : (LEVELS + 2) * CHUNK].astype(bf16)
        whole = kept[(LEVELS + 2) * CHUNK : (LEVELS + 2) * CHUNK + 1]
        rows.append(dot_nt(from_start, memory.astype(bf16)) + dot(scores.astype(bf16), v_heads))
        memory = memory * whole + same_f32 * dot_tn(v_sub, to_end)
    memory_ref[...] = memory
    folded = memory[:ATTEND_DIM]
    for h in range(1, heads):
        folded += memory[h * ATTEND_DIM : (h + 1) * ATTEND_DIM]
    out_ref[0, tokens:] = folded.astype(bf16)

    y = jnp.concatenate(rows, axis=0) + own
    y_high = y.astype(bf16)
    y_low = (y - y_high.astype(f32)).astype(bf16)
    centred = y - (dot(y_high, same) + dot(y_low, same)) * (1.0 / ATTEND_DIM)
    spread = dot((centred * centred).astype(bf16), same) * (1.0 / ATTEND_DIM)
    out_ref[0, :tokens] = (centred * lax.rsqrt(spread + eps) * scale_ref[...] * valid).astype(bf16)


def recurrence(prompt, extents, where, mixed, proj, ends, lora, right, speed, reward, scale):
    kinds, _, stretches, span, cols = proj.shape
    width = mixed.shape[-1]
    inner = lora.shape[-1]
    heads = cols // ATTEND_DIM
    sums = jnp.asarray(decay_sums(), bf16)
    level = jnp.asarray(pair_levels(heads), f32)
    head = np.arange(cols) // ATTEND_DIM
    same = jnp.asarray(head[:, None] == head[None, :], bf16)

    def fixed(array):
        return pl.BlockSpec(array.shape, lambda c, e, w: (0,) * array.ndim)

    tables = (right, speed, reward, scale, sums, level, same)
    first, first_specs, scratch = (), [], [pltpu.VMEM((cols, cols), f32)]
    if ends:
        share = stretches * ends[0].shape[2]
        last = width // share - 1
        first = (mixed, *ends)
        first_specs = [
            pl.BlockSpec(
                (kinds, 1, 1, span, share),
                lambda c, e, w: (0, w[1] ^ prompt, c, 0, jnp.where(w[2] < 2, last, 0)),
            ),
            *map(fixed, ends),
        ]
        scratch.append(pltpu.VMEM((kinds, share, cols), bf16))
    return pl.pallas_call(
        functools.partial(wkv_kernel, prompt=prompt, parted=bool(ends)),
        grid_spec=pltpu.PrefetchScalarGridSpec(
            num_scalar_prefetch=2,
            grid=(stretches,),
            in_specs=first_specs
            + [
                pl.BlockSpec((kinds, 1, 1, span, cols), lambda c, e, w: (0, w[1] ^ prompt, c, 0, 0)),
                pl.BlockSpec((1, 1, span, inner), lambda c, e, w: (w[1] ^ prompt, c, 0, 0)),
            ]
            + [fixed(a) for a in tables],
            out_specs=pl.BlockSpec((1, span + ATTEND_DIM, cols), lambda c, e, w: (c, 0, 0)),
            scratch_shapes=scratch,
        ),
        out_shape=jax.ShapeDtypeStruct((stretches, span + ATTEND_DIM, cols), bf16),
        compiler_params=vmem(56),
        cost_estimate=SMALL,
    )(extents, where, *first, proj, lora, *tables)


def finish_kernel(where_ref, x_ref, own_ref, far_ref, *refs):
    weights, out_ref = refs[:5], refs[-1]
    stretches, rows, cols = own_ref.shape
    chunk = weights[0].shape[-1]
    for e in range(stretches):
        places = pl.ds(pl.multiple_of((where_ref[0] ^ e) * chunk, chunk), chunk)
        total = x_ref[:, places].astype(f32)
        for side, lines_ref in enumerate((own_ref, far_ref)):
            w_ref = weights[e].at[side, 0] if e < 3 else weights[e + side].at[0, 0]
            for d in range(stretches):
                at = pl.ds(pl.multiple_of((where_ref[0] ^ d) * cols, cols), cols)
                total += dot(lines_ref[d], w_ref[at, :])
        out_ref[0, :, places] = total.astype(bf16)


def finished(prompt, prompts, where, x, own, far, weights, earlier):
    stretches, _, cols = own.shape
    rows = x.shape[0] // prompts
    _, groups, depth, chunk = weights[0].shape
    share = groups * stretches * chunk
    if chunk % 128:
        order = jnp.arange(stretches) ^ where[0]
        total = lax.dynamic_slice(x, (prompt * rows, where[1] * share), (rows, share)).astype(f32)
        weights = [*weights[:3], jnp.concatenate(weights[3:])]
        for side, lines in enumerate((own, far)):
            w = jnp.stack([w[side] for w in weights])[order]
            w = jnp.transpose(w, (2, 1, 0, 3)).reshape(depth, share)
            lines = jnp.transpose(lines[order, :rows], (1, 0, 2)).reshape(rows, depth)
            total += dot(lines, w)
        return jnp.concatenate([*earlier, total.astype(bf16)[None]], axis=0)
    block = stretches * chunk
    lines_spec = pl.BlockSpec((stretches, rows, cols), lambda g, w: (0, 0, 0))
    return pl.pallas_call(
        finish_kernel,
        grid_spec=pltpu.PrefetchScalarGridSpec(
            num_scalar_prefetch=1,
            grid=(groups,),
            in_specs=[pl.BlockSpec((rows, block), lambda g, w: (prompt, w[1] * groups + g)), lines_spec, lines_spec]
            + [pl.BlockSpec((a.shape[0], 1, depth, chunk), lambda g, w: (0, g, 0, 0)) for a in weights]
            + [pl.BlockSpec(memory_space=pl.ANY)] * len(earlier),
            out_specs=pl.BlockSpec((1, rows, block), lambda g, w: (prompt, 0, g)),
        ),
        out_shape=jax.ShapeDtypeStruct((prompts, rows, share), bf16),
        input_output_aliases={9: 0} if earlier else {},
        compiler_params=vmem(48),
        cost_estimate=SMALL,
    )(where, x, own, far, *weights, *earlier)


def states_kernel(where_ref, blocks_ref, pick_ref, *refs):
    out_ref = refs[-1]
    stretches, _, cols = blocks_ref.shape
    heads = cols // ATTEND_DIM
    half = ATTEND_DIM // 2
    for b in range(stretches):
        lines = dot_nt(pick_ref[...], blocks_ref[where_ref[0] ^ b])
        for h in range(heads):
            at = 2 * h * half
            pairs = jnp.concatenate([lines[at : at + half], lines[at + half : at + 2 * half]], axis=1)
            head = b * heads + h
            for i in range(half):
                out_ref[0, 0, head : head + 1, 2 * i * ATTEND_DIM : 2 * (i + 1) * ATTEND_DIM] = pairs[i : i + 1]


def states_laid(prompt, prompts, where, blocks, earlier):
    stretches, lines, cols = blocks.shape
    heads = cols // ATTEND_DIM
    order = np.arange(cols).reshape(heads, ATTEND_DIM // 2, 2).transpose(0, 2, 1).reshape(-1)
    pick = jnp.asarray(order[:, None] == np.arange(cols)[None, :], bf16)
    shape = (1, 1, stretches * heads, ATTEND_DIM * ATTEND_DIM)
    return pl.pallas_call(
        states_kernel,
        grid_spec=pltpu.PrefetchScalarGridSpec(
            num_scalar_prefetch=1,
            grid=(1,),
            in_specs=[
                pl.BlockSpec((stretches, ATTEND_DIM, cols), lambda n, w: (0, lines // ATTEND_DIM - 1, 0)),
                pl.BlockSpec((cols, cols), lambda n, w: (0, 0)),
            ]
            + [pl.BlockSpec(memory_space=pl.ANY)] * len(earlier),
            out_specs=pl.BlockSpec(shape, lambda n, w: (prompt, 0, 0, 0)),
        ),
        out_shape=jax.ShapeDtypeStruct((prompts, *shape[1:]), f32),
        input_output_aliases={3: 0} if earlier else {},
        compiler_params=vmem(32),
        cost_estimate=SMALL,
    )(where, blocks, pick, *earlier)


def tied(*values):
    return lax.optimization_barrier(values)


def moved(value, axis, by):
    peers = lax.axis_size(axis)
    return lax.ppermute(value, axis, [(i, i + by) for i in range(peers) if 0 <= i + by < peers])


def local(
    incoming_activations,
    standardize_scaling,
    lagged_blending_weights,
    learner_line_permutation,
    learner_acceptor_lookup_slices,
    learner_projection_slices,
    fading_left_matrix,
    fading_right_matrix,
    feature_fading_speed,
    self_reward,
    cluster_scaling_vector,
    prompt_extents,
):
    reqs, span, width = incoming_activations.shape
    rows = reqs * span
    stretches = lax.axis_size("seq")
    cores = lax.axis_size("tensor")
    groups = lax.axis_size("req")
    assert reqs == cores == 2 and stretches == 4
    local_width = feature_fading_speed.shape[0]
    cols = local_width // stretches
    t, s = lax.axis_index("tensor"), lax.axis_index("seq")
    where = jnp.stack([s, t, lax.axis_index("req")]).astype(jnp.int32)

    x = incoming_activations.reshape(rows, width)
    past = moved(lax.dynamic_slice_in_dim(x, t * span + span - PAST, PAST, 0), "seq", 1)
    out_half, shards = tied(learner_projection_slices.astype(bf16), learner_acceptor_lookup_slices)
    out_lines = lax.all_gather(out_half, "req", axis=0, tiled=False)
    pieces = [
        lax.dynamic_slice_in_dim(shards, (s ^ d) * cols, cols, 2).astype(bf16)
        for d in range(stretches)
    ]
    got = [swapped(pieces[d], "seq", d) for d in range(1, stretches)]

    past, *_ = tied(past, *pieces)
    coeffs = jnp.pad(lagged_blending_weights, ((0, PREFIX - 4), (0, 0)))
    act, coeffs = ordered(
        where,
        past,
        x,
        standardize_scaling.reshape(1, width),
        coeffs,
        learner_line_permutation.reshape(1, width),
    )
    act, perm, *got = tied(act, learner_line_permutation, *got)
    lines = jnp.stack([pieces[0], *got])
    chained = groups == 4

    def mixed_in(values, side, apart, earlier):
        return shifted(where, values, coeffs, left, side, apart, stretches, earlier)

    left = fading_left_matrix[perm]
    near, other = swapped(act, "seq", 1), swapped(act, "seq", 2)
    hops = [moved(lines, "req", 1), moved(lines, "req", -1)] if chained else [lax.all_gather(lines, "req", axis=0)]
    results = mixed_in(act, 0, 0, ())
    results = mixed_in(swapped(act, "tensor", 1), 1, 0, results)
    share = groups // cores
    def mine(array):
        return lax.dynamic_slice_in_dim(array, s * cols, cols, array.ndim - 1).reshape(-1, cols)

    tables = (fading_right_matrix, feature_fading_speed, self_reward, cluster_scaling_vector)
    out_lines, *rest = tied(out_lines, *results, *tables)
    results, tables = rest[:2], [mine(a) for a in rest[2:]]
    kept = lax.dynamic_slice_in_dim(out_lines, t * share, share, 0)
    given = lax.dynamic_slice_in_dim(out_lines, (1 - t) * share, share, 0)
    out_lines = jnp.stack([kept, swapped(given, "tensor", 1)])
    near, other, out_lines, *rest = tied(near, other, out_lines, *results, *tables, *hops)
    results, tables, hops = tuple(rest[:2]), rest[2:6], rest[6:]

    cut = (span + PAST) // 32 * 16
    across = [swapped(near[:cut], "seq", 2), swapped(other[cut:], "seq", 1)]
    if chained:
        hops += [moved(hops[0], "req", 1), moved(hops[1], "req", -1)]
    results = mixed_in(near, 0, 1, results)
    results = mixed_in(other, 0, 2, results)
    results = mixed_in(swapped(near, "tensor", 1), 1, 1, results)
    results = mixed_in(lax.all_gather(other, "tensor", axis=0), 1, 2, results)
    out_lines, *rest = tied(out_lines, *results, *across)
    results, across = tuple(rest[:2]), rest[2:]
    near, other = swapped(out_lines, "seq", 1), swapped(out_lines, "seq", 2)
    across = jnp.concatenate(across, axis=0)
    last = swapped(across, "tensor", 1)
    results = mixed_in(across, 0, 3, results)
    *results, = tied(*results, *hops)
    results, hops = tuple(results[:2]), results[2:]

    ends = [moved(hops[2], "req", 1), moved(hops[3], "req", -1)] if chained else []
    mixed, lora = mixed_in(last, 1, 3, results)
    if chained:
        proj = projected(where, mixed, [lines, *hops])
    else:
        proj = projected_whole(where, mixed, *hops)
    proj, near, other = tied(proj, near, other)
    across = [swapped(near[:1], "seq", 2), swapped(other[1:], "seq", 1)]
    if chained:
        ends = [ends[1], hops[3], hops[2], ends[0]]

    def one_prompt(prompt, proj):
        return recurrence(prompt, prompt_extents, where, mixed, proj, ends, lora, *tables)

    def exchanged(block):
        parts = [lax.dynamic_index_in_dim(block, s ^ d, 0, keepdims=False) for d in range(stretches)]
        return parts[:1] + [swapped(parts[d], "seq", d) for d in range(1, stretches)]

    def output(prompt, blocks, earlier):
        far_blocks = swapped(blocks, "tensor", 1)
        return finished(prompt, reqs, where, x, blocks, far_blocks, out_weights, earlier)

    block, proj = tied(one_prompt(0, proj), proj)
    first = exchanged(block)
    block, *rest = tied(one_prompt(1, proj), *first, *across)
    first, across = rest[:-2], rest[-2:]
    second = exchanged(block)
    first = jnp.stack(first)
    out_weights = [out_lines, near, other, *across]
    hidden_out = output(0, first, ())
    stretch_states = states_laid(0, reqs, where, first, ())
    hidden_out, stretch_states, *second = tied(hidden_out, stretch_states, *second)
    second = jnp.stack(second)
    hidden_out = output(1, second, (hidden_out,))
    stretch_states = states_laid(1, reqs, where, second, (stretch_states,))
    return (hidden_out, stretch_states)


def solution(mesh):
    in_specs = (
        P("req", "seq", None),
        P(),
        P(),
        P(),
        P(None, ("req", "seq"), "tensor"),
        P("tensor", ("req", "seq")),
        P(),
        P(None, "tensor"),
        P("tensor"),
        P("tensor"),
        P("tensor"),
        P("req"),
    )
    out_specs = (P("req", "seq", "tensor"), P("req", "seq", "tensor", None))
    return jax.shard_map(local, mesh=mesh, in_specs=in_specs, out_specs=out_specs, check_vma=False)
```

```python
import functools

import jax
import jax.numpy as jnp
import numpy as np
from jax import lax
from jax.experimental import pallas as pl
from jax.experimental.pallas import tpu as pltpu
from jax.sharding import PartitionSpec as P

ATTEND_DIM = 64
CHUNK = 64
LEVELS = 6
PREFIX = 8
PAST = 16

SMALL = pl.CostEstimate(flops=1024, bytes_accessed=1024, transcendentals=0)

eps = 1e-05
bf16 = jnp.bfloat16
f32 = jnp.float32


def dot(a, b):
    return jnp.dot(a, b, preferred_element_type=f32)


def dot_nt(a, b):
    return lax.dot_general(a, b, (((1,), (1,)), ((), ())), preferred_element_type=f32)


def dot_tn(a, b):
    return lax.dot_general(a, b, (((0,), (0,)), ((), ())), preferred_element_type=f32)


def swapped(value, axis, by):
    peers = lax.axis_size(axis)
    return lax.ppermute(value, axis, [(i, i ^ by) for i in range(peers)])


def vmem(mib):
    return pltpu.CompilerParams(vmem_limit_bytes=mib * 2**20)


def order_kernel(x_ref, gain_ref, coeff_ref, perm_ref, out_ref, coeff_out_ref, cur_ref):
    rows, width = x_ref.shape
    block = out_ref.shape[1]
    depth = 256

    @pl.when(pl.program_id(0) == 0)
    def _():
        x = x_ref[...].astype(f32)
        mean = jnp.mean(x, axis=-1, keepdims=True)
        centred = x - mean
        spread = jnp.mean(centred * centred, axis=-1, keepdims=True)
        cur_ref[:rows, :] = (centred * lax.rsqrt(spread + eps) * gain_ref[...]).astype(bf16)
        c = coeff_ref[...]
        high = c.astype(bf16)
        cur_ref[rows:, :] = jnp.concatenate([high, (c - high.astype(f32)).astype(bf16)], axis=0)

    perm = perm_ref[...]
    high, low = perm // depth, (perm % depth).astype(bf16)
    lines = lax.broadcasted_iota(jnp.int32, (depth, block), 0).astype(bf16)
    one, none = jnp.ones((depth, block), bf16), jnp.zeros((depth, block), bf16)
    total = jnp.zeros((rows + 2 * PREFIX, block), f32)
    for k in range(width // depth):
        mine = jnp.where(high == k, low, jnp.full_like(low, -1.0))
        total += dot(cur_ref[:, k * depth : (k + 1) * depth], jnp.where(lines == mine, one, none))
    out_ref[...] = total[:rows].astype(bf16)
    coeff_out_ref[...] = total[rows : rows + PREFIX] + total[rows + PREFIX :]


def ordered(x, gain, coeffs, perm):
    rows, width = x.shape
    block = 512
    return pl.pallas_call(
        order_kernel,
        grid=(width // block,),
        in_specs=[
            pl.BlockSpec((rows, width), lambda n: (0, 0)),
            pl.BlockSpec((1, width), lambda n: (0, 0)),
            pl.BlockSpec((PREFIX, width), lambda n: (0, 0)),
            pl.BlockSpec((1, block), lambda n: (0, n)),
        ],
        out_specs=[
            pl.BlockSpec((rows, block), lambda n: (0, n)),
            pl.BlockSpec((PREFIX, block), lambda n: (0, n)),
        ],
        out_shape=[
            jax.ShapeDtypeStruct((rows, width), bf16),
            jax.ShapeDtypeStruct((PREFIX, width), f32),
        ],
        scratch_shapes=[pltpu.VMEM((rows + 2 * PREFIX, width), bf16)],
        compiler_params=vmem(40),
        cost_estimate=SMALL,
    )(x, gain, coeffs, perm)


def mix_kernel(where_ref, act_ref, coeff_ref, left_ref, *refs):
    mixed_ref, lora_ref, inner_ref = refs[-3:]
    rows, block = mixed_ref.shape[-2:]
    width = 512
    n = pl.program_id(0)
    inner = jnp.zeros(inner_ref.shape, f32)
    for c in range(block // width):
        cols = slice(c * width, (c + 1) * width)
        cur = act_ref[PAST:, cols]
        delta = pltpu.roll(act_ref[:, cols].astype(f32), 1, 0)[PAST:].astype(bf16) - cur
        for j in range(3):
            mixed_ref[j, 0, 0, :, cols] = cur + delta * coeff_ref[j : j + 1, cols].astype(bf16)
        inner += dot(cur + delta * coeff_ref[3:4, cols].astype(bf16), left_ref[cols, :])

    @pl.when(n == 0)
    def _():
        inner_ref[...] = inner

    @pl.when(n > 0)
    def _():
        inner_ref[...] += inner

    @pl.when(n == pl.num_programs(0) - 1)
    def _():
        lora_ref[0, 0] = jnp.tanh(inner_ref[...]).astype(bf16)


def shifted(where, act, coeffs, left, side, apart, stretches, earlier):
    span, width = act.shape[-2] - PAST, act.shape[-1]
    inner = left.shape[1]
    block = 1024
    act_spec = pl.BlockSpec((span + PAST, block), lambda n, w: (0, n))
    if act.ndim == 3:
        act_spec = pl.BlockSpec((None, span + PAST, block), lambda n, w: (1 - w[1], 0, n))
    kept = pl.BlockSpec(memory_space=pl.ANY)
    return pl.pallas_call(
        mix_kernel,
        grid_spec=pltpu.PrefetchScalarGridSpec(
            num_scalar_prefetch=1,
            grid=(width // block,),
            in_specs=[
                act_spec,
                pl.BlockSpec((PREFIX, block), lambda n, w: (0, n)),
                pl.BlockSpec((block, inner), lambda n, w: (n, 0)),
            ]
            + [kept] * len(earlier),
            out_specs=[
                pl.BlockSpec((3, 1, 1, span, block), lambda n, w: (0, side, w[0] ^ apart, 0, n)),
                pl.BlockSpec((1, 1, span, inner), lambda n, w: (side, w[0] ^ apart, 0, 0)),
            ],
            scratch_shapes=[pltpu.VMEM((span, inner), f32)],
        ),
        out_shape=[
            jax.ShapeDtypeStruct((3, 2, stretches, span, width), bf16),
            jax.ShapeDtypeStruct((2, stretches, span, inner), bf16),
        ],
        input_output_aliases={4: 0, 5: 1} if earlier else {},
        compiler_params=vmem(32),
        cost_estimate=SMALL,
    )(where, act, coeffs, left, *earlier)


def project_kernel(where_ref, *refs):
    *refs, out_ref, lines_ref = refs
    parts = where_ref[2] // 2
    acts, hops = refs[:3], refs[3:]
    stretches, _, depth, _ = hops[0].shape
    share = stretches * depth

    def place(r, ref):
        slot = r - parts

        @pl.when((slot >= 0) & (slot < len(acts)))
        def _():
            for d in range(stretches):
                at = slot * share + (where_ref[0] ^ d) * depth
                lines_ref[pl.ds(pl.multiple_of(at, depth), depth), :] = ref[d, 0]

    @pl.when(pl.program_id(1) == 0)
    def _():
        place(where_ref[2], hops[0])
        for hop in range(1, len(hops) // 2 + 1):
            place(where_ref[2] - hop, hops[2 * hop - 1])
            place(where_ref[2] + hop, hops[2 * hop])

    total = None
    for i, act_ref in enumerate(acts):
        found = dot(act_ref[0, 0].reshape(-1, share), lines_ref[i * share : (i + 1) * share, :])
        total = found if total is None else total + found
    out_ref[0, 0] = total.reshape(out_ref.shape[2:])


def projected(where, mixed, hops):
    stretches, kinds, depth, cols = hops[0].shape
    _, sides, _, span, width = mixed.shape
    share = stretches * depth
    parts = width // share - 1

    def act_spec(i):
        return pl.BlockSpec((1, 1, stretches, span, share), lambda j, m, w: (j, m, 0, 0, w[2] // 2 + i))

    return pl.pallas_call(
        project_kernel,
        grid_spec=pltpu.PrefetchScalarGridSpec(
            num_scalar_prefetch=1,
            grid=(kinds, sides),
            in_specs=[act_spec(i) for i in range(parts)]
            + [pl.BlockSpec((stretches, 1, depth, cols), lambda j, m, w: (0, j, 0, 0))] * len(hops),
            out_specs=pl.BlockSpec((1, 1, stretches, span, cols), lambda j, m, w: (j, m, 0, 0, 0)),
            scratch_shapes=[pltpu.VMEM((parts * share, cols), bf16)],
        ),
        out_shape=jax.ShapeDtypeStruct((kinds, sides, stretches, span, cols), f32),
        compiler_params=vmem(60),
        cost_estimate=SMALL,
    )(where, *[mixed] * parts, *hops)


def projected_whole(where, mixed, lines):
    _, stretches, kinds, depth, cols = lines.shape
    lines = lines[:, jnp.arange(stretches) ^ where[0]]
    lines = jnp.transpose(lines, (2, 0, 1, 3, 4)).reshape(kinds, mixed.shape[-1], cols)
    return jnp.einsum("jxbtk,jkc->jxbtc", mixed, lines, preferred_element_type=f32).astype(bf16)


def decay_sums():
    place = np.arange(CHUNK)
    of, by = place[:, None], place[None, :]
    parts = []
    for level in range(LEVELS):
        half = 1 << level
        middle = (of // (2 * half)) * 2 * half + half - 1
        later = (of % (2 * half)) >= half
        parts.append(np.where(later, (by > middle) & (by < of), (by > of) & (by <= middle)))
    parts += [by < of, by > of, np.ones((8, CHUNK), bool)]
    sums = np.concatenate(parts).astype(np.float32)
    return np.concatenate([sums, sums], axis=1)


def pair_levels(heads):
    of, by = np.arange(CHUNK)[:, None], np.arange(CHUNK)[None, :]
    level = np.full((CHUNK, CHUNK), -1.0, np.float32)
    for bit in range(LEVELS):
        level[((of ^ by) >> bit) == 1] = bit
    return np.tile(np.where(of > by, level, -1.0).astype(np.float32), (1, heads))


def wkv_kernel(extent_ref, where_ref, *refs, prompt, parted):
    if parted:
        act_ref, *last_refs = refs[:5]
        *refs, lines_ref = refs[5:]
    proj_ref, lora_ref, right_ref, speed_ref, reward_ref, scale_ref, sums_ref, level_ref, same_ref, *refs = refs
    out_ref, memory_ref = refs
    step = pl.program_id(0)
    tokens, cols = proj_ref.shape[3:]
    heads = cols // ATTEND_DIM
    same = same_ref[...]
    same_f32 = same.astype(f32)
    level = level_ref[...]

    @pl.when(step == 0)
    def _():
        memory_ref[...] = jnp.zeros_like(memory_ref)
        if parted:
            for r, last_ref in enumerate(last_refs):

                @pl.when(where_ref[2] == r)
                def _():
                    stretches, kinds, depth, _ = last_ref.shape
                    for d in range(stretches):
                        at = pl.ds(pl.multiple_of((where_ref[0] ^ d) * depth, depth), depth)
                        for j in range(kinds):
                            lines_ref[j, at, :] = last_ref[d, j]

    def projection(j):
        if not parted:
            return proj_ref[j, 0, 0]
        return (proj_ref[j, 0, 0] + dot(act_ref[j, 0, 0], lines_ref[j])).astype(bf16)

    at = step * tokens + lax.broadcasted_iota(jnp.int32, (tokens, cols), 0)
    valid = jnp.where(at < extent_ref[prompt], 1.0, 0.0)
    r = projection(0)
    k = projection(1) * valid.astype(bf16)
    v = projection(2)
    decay = -speed_ref[...] * jnp.exp(dot(lora_ref[0, 0], right_ref[...])) * valid
    high = decay.astype(bf16)
    low = (decay - high.astype(f32)).astype(bf16)
    own = dot((r.astype(f32) * reward_ref[...] * k.astype(f32)).astype(bf16), same) * v.astype(f32)

    memory = memory_ref[...]
    rows = []
    for sub in range(tokens // CHUNK):
        lines = slice(sub * CHUNK, (sub + 1) * CHUNK)
        r_sub, k_sub, v_sub = r[lines], k[lines], v[lines]
        kept = jnp.exp(dot(sums_ref[...], jnp.concatenate([high[lines], low[lines]], axis=0)))
        scores = jnp.zeros((CHUNK, heads * CHUNK), f32)
        for bit in range(LEVELS):
            part = kept[bit * CHUNK : (bit + 1) * CHUNK].astype(bf16)
            lookup = jnp.concatenate([k_sub * part] * heads, axis=0) * same
            scores = jnp.where(level == bit, dot_nt(r_sub * part, lookup), scores)
        v_heads = jnp.concatenate([v_sub] * heads, axis=0) * same
        from_start = r_sub * kept[LEVELS * CHUNK : (LEVELS + 1) * CHUNK].astype(bf16)
        to_end = k_sub * kept[(LEVELS + 1) * CHUNK : (LEVELS + 2) * CHUNK].astype(bf16)
        whole = kept[(LEVELS + 2) * CHUNK : (LEVELS + 2) * CHUNK + 1]
        rows.append(dot_nt(from_start, memory.astype(bf16)) + dot(scores.astype(bf16), v_heads))
        memory = memory * whole + same_f32 * dot_tn(v_sub, to_end)
    memory_ref[...] = memory
    folded = memory[:ATTEND_DIM]
    for h in range(1, heads):
        folded += memory[h * ATTEND_DIM : (h + 1) * ATTEND_DIM]
    out_ref[0, tokens:] = folded.astype(bf16)

    y = jnp.concatenate(rows, axis=0) + own
    y_high = y.astype(bf16)
    y_low = (y - y_high.astype(f32)).astype(bf16)
    centred = y - (dot(y_high, same) + dot(y_low, same)) * (1.0 / ATTEND_DIM)
    spread = dot((centred * centred).astype(bf16), same) * (1.0 / ATTEND_DIM)
    out_ref[0, :tokens] = (centred * lax.rsqrt(spread + eps) * scale_ref[...] * valid).astype(bf16)


def recurrence(prompt, extents, where, mixed, proj, ends, lora, right, speed, reward, scale):
    kinds, _, stretches, span, cols = proj.shape
    width = mixed.shape[-1]
    inner = lora.shape[-1]
    heads = cols // ATTEND_DIM
    sums = jnp.asarray(decay_sums(), bf16)
    level = jnp.asarray(pair_levels(heads), f32)
    head = np.arange(cols) // ATTEND_DIM
    same = jnp.asarray(head[:, None] == head[None, :], bf16)

    def fixed(array):
        return pl.BlockSpec(array.shape, lambda c, e, w: (0,) * array.ndim)

    tables = (right, speed, reward, scale, sums, level, same)
    first, first_specs, scratch = (), [], [pltpu.VMEM((cols, cols), f32)]
    if ends:
        share = stretches * ends[0].shape[2]
        last = width // share - 1
        first = (mixed, *ends)
        first_specs = [
            pl.BlockSpec(
                (kinds, 1, 1, span, share),
                lambda c, e, w: (0, w[1] ^ prompt, c, 0, jnp.where(w[2] < 2, last, 0)),
            ),
            *map(fixed, ends),
        ]
        scratch.append(pltpu.VMEM((kinds, share, cols), bf16))
    return pl.pallas_call(
        functools.partial(wkv_kernel, prompt=prompt, parted=bool(ends)),
        grid_spec=pltpu.PrefetchScalarGridSpec(
            num_scalar_prefetch=2,
            grid=(stretches,),
            in_specs=first_specs
            + [
                pl.BlockSpec((kinds, 1, 1, span, cols), lambda c, e, w: (0, w[1] ^ prompt, c, 0, 0)),
                pl.BlockSpec((1, 1, span, inner), lambda c, e, w: (w[1] ^ prompt, c, 0, 0)),
            ]
            + [fixed(a) for a in tables],
            out_specs=pl.BlockSpec((1, span + ATTEND_DIM, cols), lambda c, e, w: (c, 0, 0)),
            scratch_shapes=scratch,
        ),
        out_shape=jax.ShapeDtypeStruct((stretches, span + ATTEND_DIM, cols), bf16),
        compiler_params=vmem(56),
        cost_estimate=SMALL,
    )(extents, where, *first, proj, lora, *tables)


def finish_kernel(where_ref, x_ref, own_ref, far_ref, *refs):
    weights, out_ref = refs[:5], refs[-1]
    stretches, rows, cols = own_ref.shape
    chunk = weights[0].shape[-1]
    for e in range(stretches):
        places = pl.ds(pl.multiple_of((where_ref[0] ^ e) * chunk, chunk), chunk)
        total = x_ref[:, places].astype(f32)
        for side, lines_ref in enumerate((own_ref, far_ref)):
            w_ref = weights[e].at[side, 0] if e < 3 else weights[e + side].at[0, 0]
            for d in range(stretches):
                at = pl.ds(pl.multiple_of((where_ref[0] ^ d) * cols, cols), cols)
                total += dot(lines_ref[d], w_ref[at, :])
        out_ref[0, :, places] = total.astype(bf16)


def finished(prompt, prompts, where, x, own, far, weights, earlier):
    stretches, _, cols = own.shape
    rows = x.shape[0] // prompts
    _, groups, depth, chunk = weights[0].shape
    share = groups * stretches * chunk
    if chunk % 128:
        order = jnp.arange(stretches) ^ where[0]
        total = lax.dynamic_slice(x, (prompt * rows, where[1] * share), (rows, share)).astype(f32)
        weights = [*weights[:3], jnp.concatenate(weights[3:])]
        for side, lines in enumerate((own, far)):
            w = jnp.stack([w[side] for w in weights])[order]
            w = jnp.transpose(w, (2, 1, 0, 3)).reshape(depth, share)
            lines = jnp.transpose(lines[order, :rows], (1, 0, 2)).reshape(rows, depth)
            total += dot(lines, w)
        return jnp.concatenate([*earlier, total.astype(bf16)[None]], axis=0)
    block = stretches * chunk
    lines_spec = pl.BlockSpec((stretches, rows, cols), lambda g, w: (0, 0, 0))
    return pl.pallas_call(
        finish_kernel,
        grid_spec=pltpu.PrefetchScalarGridSpec(
            num_scalar_prefetch=1,
            grid=(groups,),
            in_specs=[pl.BlockSpec((rows, block), lambda g, w: (prompt, w[1] * groups + g)), lines_spec, lines_spec]
            + [pl.BlockSpec((a.shape[0], 1, depth, chunk), lambda g, w: (0, g, 0, 0)) for a in weights]
            + [pl.BlockSpec(memory_space=pl.ANY)] * len(earlier),
            out_specs=pl.BlockSpec((1, rows, block), lambda g, w: (prompt, 0, g)),
        ),
        out_shape=jax.ShapeDtypeStruct((prompts, rows, share), bf16),
        input_output_aliases={9: 0} if earlier else {},
        compiler_params=vmem(48),
        cost_estimate=SMALL,
    )(where, x, own, far, *weights, *earlier)


def states_kernel(where_ref, blocks_ref, pick_ref, *refs):
    out_ref = refs[-1]
    stretches, _, cols = blocks_ref.shape
    heads = cols // ATTEND_DIM
    half = ATTEND_DIM // 2
    for b in range(stretches):
        lines = dot_nt(pick_ref[...], blocks_ref[where_ref[0] ^ b])
        for h in range(heads):
            at = 2 * h * half
            pairs = jnp.concatenate([lines[at : at + half], lines[at + half : at + 2 * half]], axis=1)
            head = b * heads + h
            for i in range(half):
                out_ref[0, 0, head : head + 1, 2 * i * ATTEND_DIM : 2 * (i + 1) * ATTEND_DIM] = pairs[i : i + 1]


def states_laid(prompt, prompts, where, blocks, earlier):
    stretches, lines, cols = blocks.shape
    heads = cols // ATTEND_DIM
    order = np.arange(cols).reshape(heads, ATTEND_DIM // 2, 2).transpose(0, 2, 1).reshape(-1)
    pick = jnp.asarray(order[:, None] == np.arange(cols)[None, :], bf16)
    shape = (1, 1, stretches * heads, ATTEND_DIM * ATTEND_DIM)
    return pl.pallas_call(
        states_kernel,
        grid_spec=pltpu.PrefetchScalarGridSpec(
            num_scalar_prefetch=1,
            grid=(1,),
            in_specs=[
                pl.BlockSpec((stretches, ATTEND_DIM, cols), lambda n, w: (0, lines // ATTEND_DIM - 1, 0)),
                pl.BlockSpec((cols, cols), lambda n, w: (0, 0)),
            ]
            + [pl.BlockSpec(memory_space=pl.ANY)] * len(earlier),
            out_specs=pl.BlockSpec(shape, lambda n, w: (prompt, 0, 0, 0)),
        ),
        out_shape=jax.ShapeDtypeStruct((prompts, *shape[1:]), f32),
        input_output_aliases={3: 0} if earlier else {},
        compiler_params=vmem(32),
        cost_estimate=SMALL,
    )(where, blocks, pick, *earlier)


def tied(*values):
    return lax.optimization_barrier(values)


def moved(value, axis, by):
    peers = lax.axis_size(axis)
    return lax.ppermute(value, axis, [(i, i + by) for i in range(peers) if 0 <= i + by < peers])


def local(
    incoming_activations,
    standardize_scaling,
    lagged_blending_weights,
    learner_line_permutation,
    learner_acceptor_lookup_slices,
    learner_projection_slices,
    fading_left_matrix,
    fading_right_matrix,
    feature_fading_speed,
    self_reward,
    cluster_scaling_vector,
    prompt_extents,
):
    reqs, span, width = incoming_activations.shape
    rows = reqs * span
    stretches = lax.axis_size("seq")
    cores = lax.axis_size("tensor")
    groups = lax.axis_size("req")
    assert reqs == cores == 2 and stretches == 4
    local_width = feature_fading_speed.shape[0]
    cols = local_width // stretches
    t, s = lax.axis_index("tensor"), lax.axis_index("seq")
    where = jnp.stack([s, t, lax.axis_index("req")]).astype(jnp.int32)

    x = incoming_activations.reshape(rows, width)
    own_x = lax.dynamic_slice_in_dim(x, t * span, span, 0)
    past = moved(own_x[span - PAST :], "seq", 1)
    out_half, shards = tied(learner_projection_slices.astype(bf16), learner_acceptor_lookup_slices)
    out_lines = lax.all_gather(out_half, "req", axis=0, tiled=False)
    pieces = [
        lax.dynamic_slice_in_dim(shards, (s ^ d) * cols, cols, 2).astype(bf16)
        for d in range(stretches)
    ]
    got = [swapped(pieces[d], "seq", d) for d in range(1, stretches)]

    own_x, past, *_ = tied(own_x, past, *pieces)
    coeffs = jnp.pad(lagged_blending_weights, ((0, PREFIX - 4), (0, 0)))
    act, coeffs = ordered(
        jnp.concatenate([past, own_x], axis=0),
        standardize_scaling.reshape(1, width),
        coeffs,
        learner_line_permutation.reshape(1, width),
    )
    act, perm, *got = tied(act, learner_line_permutation, *got)
    lines = jnp.stack([pieces[0], *got])
    chained = groups == 4

    def mixed_in(values, side, apart, earlier):
        return shifted(where, values, coeffs, left, side, apart, stretches, earlier)

    left = fading_left_matrix[perm]
    near, other = swapped(act, "seq", 1), swapped(act, "seq", 2)
    hops = [moved(lines, "req", 1), moved(lines, "req", -1)] if chained else [lax.all_gather(lines, "req", axis=0)]
    results = mixed_in(act, 0, 0, ())
    results = mixed_in(swapped(act, "tensor", 1), 1, 0, results)
    share = groups // cores
    def mine(array):
        return lax.dynamic_slice_in_dim(array, s * cols, cols, array.ndim - 1).reshape(-1, cols)

    tables = (fading_right_matrix, feature_fading_speed, self_reward, cluster_scaling_vector)
    out_lines, *rest = tied(out_lines, *results, *tables)
    results, tables = rest[:2], [mine(a) for a in rest[2:]]
    kept = lax.dynamic_slice_in_dim(out_lines, t * share, share, 0)
    given = lax.dynamic_slice_in_dim(out_lines, (1 - t) * share, share, 0)
    out_lines = jnp.stack([kept, swapped(given, "tensor", 1)])
    near, other, out_lines, *rest = tied(near, other, out_lines, *results, *tables, *hops)
    results, tables, hops = tuple(rest[:2]), rest[2:6], rest[6:]

    cut = (span + PAST) // 32 * 16
    across = [swapped(near[:cut], "seq", 2), swapped(other[cut:], "seq", 1)]
    if chained:
        hops += [moved(hops[0], "req", 1), moved(hops[1], "req", -1)]
    results = mixed_in(near, 0, 1, results)
    results = mixed_in(other, 0, 2, results)
    results = mixed_in(swapped(near, "tensor", 1), 1, 1, results)
    both = lax.all_gather(other, "tensor", axis=0)
    out_lines, *rest = tied(out_lines, *results, *across)
    results, across = tuple(rest[:2]), rest[2:]
    near, other = swapped(out_lines, "seq", 1), swapped(out_lines, "seq", 2)
    results = mixed_in(both, 1, 2, results)
    across = jnp.concatenate(across, axis=0)
    last = swapped(across, "tensor", 1)
    results = mixed_in(across, 0, 3, results)
    *results, = tied(*results, *hops)
    results, hops = tuple(results[:2]), results[2:]

    ends = [moved(hops[2], "req", 1), moved(hops[3], "req", -1)] if chained else []
    mixed, lora = mixed_in(last, 1, 3, results)
    if chained:
        proj = projected(where, mixed, [lines, *hops])
    else:
        proj = projected_whole(where, mixed, *hops)
    proj, near, other = tied(proj, near, other)
    across = [swapped(near[:1], "seq", 2), swapped(other[1:], "seq", 1)]
    if chained:
        ends = [ends[1], hops[3], hops[2], ends[0]]

    def one_prompt(prompt, proj):
        return recurrence(prompt, prompt_extents, where, mixed, proj, ends, lora, *tables)

    def exchanged(block):
        parts = [lax.dynamic_index_in_dim(block, s ^ d, 0, keepdims=False) for d in range(stretches)]
        return parts[:1] + [swapped(parts[d], "seq", d) for d in range(1, stretches)]

    def output(prompt, blocks, earlier):
        far_blocks = swapped(blocks, "tensor", 1)
        return finished(prompt, reqs, where, x, blocks, far_blocks, out_weights, earlier)

    block, proj = tied(one_prompt(0, proj), proj)
    first = exchanged(block)
    block, *rest = tied(one_prompt(1, proj), *first, *across)
    first, across = rest[:-2], rest[-2:]
    second = exchanged(block)
    first = jnp.stack(first)
    out_weights = [out_lines, near, other, *across]
    hidden_out = output(0, first, ())
    stretch_states = states_laid(0, reqs, where, first, ())
    hidden_out, stretch_states, *second = tied(hidden_out, stretch_states, *second)
    second = jnp.stack(second)
    hidden_out = output(1, second, (hidden_out,))
    stretch_states = states_laid(1, reqs, where, second, (stretch_states,))
    return (hidden_out, stretch_states)


def solution(mesh):
    in_specs = (
        P("req", "seq", None),
        P(),
        P(),
        P(),
        P(None, ("req", "seq"), "tensor"),
        P("tensor", ("req", "seq")),
        P(),
        P(None, "tensor"),
        P("tensor"),
        P("tensor"),
        P("tensor"),
        P("req"),
    )
    out_specs = (P("req", "seq", "tensor"), P("req", "seq", "tensor", None))
    return jax.shard_map(local, mesh=mesh, in_specs=in_specs, out_specs=out_specs, check_vma=False)
```

```python
import functools

import jax
import jax.numpy as jnp
import numpy as np
from jax import lax
from jax.experimental import pallas as pl
from jax.experimental.pallas import tpu as pltpu
from jax.sharding import PartitionSpec as P

ATTEND_DIM = 64
CHUNK = 64
LEVELS = 6
PREFIX = 8
PAST = 16

SMALL = pl.CostEstimate(flops=1024, bytes_accessed=1024, transcendentals=0)

eps = 1e-05
bf16 = jnp.bfloat16
f32 = jnp.float32


def dot(a, b):
    return jnp.dot(a, b, preferred_element_type=f32)


def dot_nt(a, b):
    return lax.dot_general(a, b, (((1,), (1,)), ((), ())), preferred_element_type=f32)


def dot_tn(a, b):
    return lax.dot_general(a, b, (((0,), (0,)), ((), ())), preferred_element_type=f32)


def swapped(value, axis, by):
    peers = lax.axis_size(axis)
    return lax.ppermute(value, axis, [(i, i ^ by) for i in range(peers)])


def vmem(mib):
    return pltpu.CompilerParams(vmem_limit_bytes=mib * 2**20)


def order_kernel(x_ref, gain_ref, coeff_ref, perm_ref, out_ref, coeff_out_ref, cur_ref):
    rows, width = x_ref.shape
    block = out_ref.shape[1]
    depth = 256

    @pl.when(pl.program_id(0) == 0)
    def _():
        x = x_ref[...].astype(f32)
        mean = jnp.mean(x, axis=-1, keepdims=True)
        centred = x - mean
        spread = jnp.mean(centred * centred, axis=-1, keepdims=True)
        cur_ref[:rows, :] = (centred * lax.rsqrt(spread + eps) * gain_ref[...]).astype(bf16)
        c = coeff_ref[...]
        high = c.astype(bf16)
        cur_ref[rows:, :] = jnp.concatenate([high, (c - high.astype(f32)).astype(bf16)], axis=0)

    perm = perm_ref[...]
    high, low = perm // depth, (perm % depth).astype(bf16)
    lines = lax.broadcasted_iota(jnp.int32, (depth, block), 0).astype(bf16)
    one, none = jnp.ones((depth, block), bf16), jnp.zeros((depth, block), bf16)
    total = jnp.zeros((rows + 2 * PREFIX, block), f32)
    for k in range(width // depth):
        mine = jnp.where(high == k, low, jnp.full_like(low, -1.0))
        total += dot(cur_ref[:, k * depth : (k + 1) * depth], jnp.where(lines == mine, one, none))
    out_ref[...] = total[:rows].astype(bf16)
    coeff_out_ref[...] = total[rows : rows + PREFIX] + total[rows + PREFIX :]


def ordered(x, gain, coeffs, perm):
    rows, width = x.shape
    block = 512
    return pl.pallas_call(
        order_kernel,
        grid=(width // block,),
        in_specs=[
            pl.BlockSpec((rows, width), lambda n: (0, 0)),
            pl.BlockSpec((1, width), lambda n: (0, 0)),
            pl.BlockSpec((PREFIX, width), lambda n: (0, 0)),
            pl.BlockSpec((1, block), lambda n: (0, n)),
        ],
        out_specs=[
            pl.BlockSpec((rows, block), lambda n: (0, n)),
            pl.BlockSpec((PREFIX, block), lambda n: (0, n)),
        ],
        out_shape=[
            jax.ShapeDtypeStruct((rows, width), bf16),
            jax.ShapeDtypeStruct((PREFIX, width), f32),
        ],
        scratch_shapes=[pltpu.VMEM((rows + 2 * PREFIX, width), bf16)],
        compiler_params=vmem(40),
        cost_estimate=SMALL,
    )(x, gain, coeffs, perm)


def mix_kernel(where_ref, act_ref, coeff_ref, left_ref, *refs):
    mixed_ref, lora_ref, inner_ref = refs[-3:]
    rows, block = mixed_ref.shape[-2:]
    width = 512
    n = pl.program_id(0)
    inner = jnp.zeros(inner_ref.shape, f32)
    for c in range(block // width):
        cols = slice(c * width, (c + 1) * width)
        cur = act_ref[PAST:, cols]
        delta = pltpu.roll(act_ref[:, cols].astype(f32), 1, 0)[PAST:].astype(bf16) - cur
        for j in range(3):
            mixed_ref[j, 0, 0, :, cols] = cur + delta * coeff_ref[j : j + 1, cols].astype(bf16)
        inner += dot(cur + delta * coeff_ref[3:4, cols].astype(bf16), left_ref[cols, :])

    @pl.when(n == 0)
    def _():
        inner_ref[...] = inner

    @pl.when(n > 0)
    def _():
        inner_ref[...] += inner

    @pl.when(n == pl.num_programs(0) - 1)
    def _():
        lora_ref[0, 0] = jnp.tanh(inner_ref[...]).astype(bf16)


def shifted(where, act, coeffs, left, side, apart, stretches, earlier):
    span, width = act.shape[-2] - PAST, act.shape[-1]
    inner = left.shape[1]
    block = 1024
    act_spec = pl.BlockSpec((span + PAST, block), lambda n, w: (0, n))
    if act.ndim == 3:
        act_spec = pl.BlockSpec((None, span + PAST, block), lambda n, w: (1 - w[1], 0, n))
    kept = pl.BlockSpec(memory_space=pl.ANY)
    return pl.pallas_call(
        mix_kernel,
        grid_spec=pltpu.PrefetchScalarGridSpec(
            num_scalar_prefetch=1,
            grid=(width // block,),
            in_specs=[
                act_spec,
                pl.BlockSpec((PREFIX, block), lambda n, w: (0, n)),
                pl.BlockSpec((block, inner), lambda n, w: (n, 0)),
            ]
            + [kept] * len(earlier),
            out_specs=[
                pl.BlockSpec((3, 1, 1, span, block), lambda n, w: (0, side, w[0] ^ apart, 0, n)),
                pl.BlockSpec((1, 1, span, inner), lambda n, w: (side, w[0] ^ apart, 0, 0)),
            ],
            scratch_shapes=[pltpu.VMEM((span, inner), f32)],
        ),
        out_shape=[
            jax.ShapeDtypeStruct((3, 2, stretches, span, width), bf16),
            jax.ShapeDtypeStruct((2, stretches, span, inner), bf16),
        ],
        input_output_aliases={4: 0, 5: 1} if earlier else {},
        compiler_params=vmem(32),
        cost_estimate=SMALL,
    )(where, act, coeffs, left, *earlier)


def project_kernel(where_ref, *refs):
    *refs, out_ref, lines_ref = refs
    parts = where_ref[2] // 2
    acts, hops = refs[:3], refs[3:]
    stretches, _, depth, _ = hops[0].shape
    share = stretches * depth

    def place(r, ref):
        slot = r - parts

        @pl.when((slot >= 0) & (slot < len(acts)))
        def _():
            for d in range(stretches):
                at = slot * share + (where_ref[0] ^ d) * depth
                lines_ref[pl.ds(pl.multiple_of(at, depth), depth), :] = ref[d, 0]

    @pl.when(pl.program_id(1) == 0)
    def _():
        place(where_ref[2], hops[0])
        for hop in range(1, len(hops) // 2 + 1):
            place(where_ref[2] - hop, hops[2 * hop - 1])
            place(where_ref[2] + hop, hops[2 * hop])

    total = None
    for i, act_ref in enumerate(acts):
        found = dot(act_ref[0, 0].reshape(-1, share), lines_ref[i * share : (i + 1) * share, :])
        total = found if total is None else total + found
    out_ref[0, 0] = total.reshape(out_ref.shape[2:])


def projected(where, mixed, hops):
    stretches, kinds, depth, cols = hops[0].shape
    _, sides, _, span, width = mixed.shape
    share = stretches * depth
    parts = width // share - 1

    def act_spec(i):
        return pl.BlockSpec((1, 1, stretches, span, share), lambda j, m, w: (j, m, 0, 0, w[2] // 2 + i))

    return pl.pallas_call(
        project_kernel,
        grid_spec=pltpu.PrefetchScalarGridSpec(
            num_scalar_prefetch=1,
            grid=(kinds, sides),
            in_specs=[act_spec(i) for i in range(parts)]
            + [pl.BlockSpec((stretches, 1, depth, cols), lambda j, m, w: (0, j, 0, 0))] * len(hops),
            out_specs=pl.BlockSpec((1, 1, stretches, span, cols), lambda j, m, w: (j, m, 0, 0, 0)),
            scratch_shapes=[pltpu.VMEM((parts * share, cols), bf16)],
        ),
        out_shape=jax.ShapeDtypeStruct((kinds, sides, stretches, span, cols), f32),
        compiler_params=vmem(60),
        cost_estimate=SMALL,
    )(where, *[mixed] * parts, *hops)


def projected_whole(where, mixed, lines):
    _, stretches, kinds, depth, cols = lines.shape
    lines = lines[:, jnp.arange(stretches) ^ where[0]]
    lines = jnp.transpose(lines, (2, 0, 1, 3, 4)).reshape(kinds, mixed.shape[-1], cols)
    return jnp.einsum("jxbtk,jkc->jxbtc", mixed, lines, preferred_element_type=f32).astype(bf16)


def decay_sums():
    place = np.arange(CHUNK)
    of, by = place[:, None], place[None, :]
    parts = []
    for level in range(1, LEVELS):
        half = 1 << level
        middle = (of // (2 * half)) * 2 * half + half - 1
        later = (of % (2 * half)) >= half
        parts.append(np.where(later, (by > middle) & (by < of), (by > of) & (by <= middle)))
    parts += [by < of, by > of, np.ones((8, CHUNK), bool)]
    sums = np.concatenate(parts).astype(np.float32)
    return np.concatenate([sums, sums], axis=1)


def pair_levels(heads):
    of, by = np.arange(CHUNK)[:, None], np.arange(CHUNK)[None, :]
    level = np.full((CHUNK, CHUNK), -1.0, np.float32)
    for bit in range(LEVELS):
        level[((of ^ by) >> bit) == 1] = bit
    return np.tile(np.where(of > by, level, -1.0).astype(np.float32), (1, heads))


def wkv_kernel(extent_ref, where_ref, *refs, prompt, parted):
    if parted:
        act_ref, *last_refs = refs[:5]
        *refs, lines_ref = refs[5:]
    proj_ref, lora_ref, right_ref, speed_ref, reward_ref, scale_ref, sums_ref, level_ref, same_ref, *refs = refs
    out_ref, memory_ref = refs
    step = pl.program_id(0)
    tokens, cols = proj_ref.shape[3:]
    heads = cols // ATTEND_DIM
    same = same_ref[...]
    same_f32 = same.astype(f32)
    level = level_ref[...]

    @pl.when(step == 0)
    def _():
        memory_ref[...] = jnp.zeros_like(memory_ref)
        if parted:
            for r, last_ref in enumerate(last_refs):

                @pl.when(where_ref[2] == r)
                def _():
                    stretches, kinds, depth, _ = last_ref.shape
                    for d in range(stretches):
                        at = pl.ds(pl.multiple_of((where_ref[0] ^ d) * depth, depth), depth)
                        for j in range(kinds):
                            lines_ref[j, at, :] = last_ref[d, j]

    def projection(j):
        if not parted:
            return proj_ref[j, 0, 0]
        return (proj_ref[j, 0, 0] + dot(act_ref[j, 0, 0], lines_ref[j])).astype(bf16)

    at = step * tokens + lax.broadcasted_iota(jnp.int32, (tokens, cols), 0)
    valid = jnp.where(at < extent_ref[prompt], 1.0, 0.0)
    r = projection(0)
    k = projection(1) * valid.astype(bf16)
    v = projection(2)
    decay = -speed_ref[...] * jnp.exp(dot(lora_ref[0, 0], right_ref[...])) * valid
    high = decay.astype(bf16)
    low = (decay - high.astype(f32)).astype(bf16)
    own = dot((r.astype(f32) * reward_ref[...] * k.astype(f32)).astype(bf16), same) * v.astype(f32)

    subs = [slice(at, at + CHUNK) for at in range(0, tokens, CHUNK)]
    both = jnp.concatenate([jnp.concatenate([part[lines] for lines in subs], axis=1) for part in (high, low)], axis=0)
    all_kept = jnp.exp(dot(sums_ref[...], both))
    memory = memory_ref[...]
    rows = []
    for sub, lines in enumerate(subs):
        r_sub, k_sub, v_sub = r[lines], k[lines], v[lines]
        kept = all_kept[:, sub * cols : (sub + 1) * cols]
        scores = jnp.zeros((CHUNK, heads * CHUNK), f32)
        for bit in range(LEVELS):
            query, lookup = r_sub, k_sub
            if bit:
                part = kept[(bit - 1) * CHUNK : bit * CHUNK].astype(bf16)
                query, lookup = query * part, lookup * part
            lookup = jnp.concatenate([lookup] * heads, axis=0) * same
            scores = jnp.where(level == bit, dot_nt(query, lookup), scores)
        v_heads = jnp.concatenate([v_sub] * heads, axis=0) * same
        after = (LEVELS - 1) * CHUNK
        from_start = r_sub * kept[after : after + CHUNK].astype(bf16)
        to_end = k_sub * kept[after + CHUNK : after + 2 * CHUNK].astype(bf16)
        whole = kept[after + 2 * CHUNK : after + 2 * CHUNK + 1]
        rows.append(dot_nt(from_start, memory.astype(bf16)) + dot(scores.astype(bf16), v_heads))
        memory = memory * whole + same_f32 * dot_tn(v_sub, to_end)
    memory_ref[...] = memory
    folded = memory[:ATTEND_DIM]
    for h in range(1, heads):
        folded += memory[h * ATTEND_DIM : (h + 1) * ATTEND_DIM]
    out_ref[0, tokens:] = folded.astype(bf16)

    y = jnp.concatenate(rows, axis=0) + own
    y_high = y.astype(bf16)
    y_low = (y - y_high.astype(f32)).astype(bf16)
    centred = y - (dot(y_high, same) + dot(y_low, same)) * (1.0 / ATTEND_DIM)
    spread = dot((centred * centred).astype(bf16), same) * (1.0 / ATTEND_DIM)
    out_ref[0, :tokens] = (centred * lax.rsqrt(spread + eps) * scale_ref[...] * valid).astype(bf16)


def recurrence(prompt, extents, where, mixed, proj, ends, lora, right, speed, reward, scale):
    kinds, _, stretches, span, cols = proj.shape
    width = mixed.shape[-1]
    inner = lora.shape[-1]
    heads = cols // ATTEND_DIM
    sums = jnp.asarray(decay_sums(), bf16)
    level = jnp.asarray(pair_levels(heads), f32)
    head = np.arange(cols) // ATTEND_DIM
    same = jnp.asarray(head[:, None] == head[None, :], bf16)

    def fixed(array):
        return pl.BlockSpec(array.shape, lambda c, e, w: (0,) * array.ndim)

    tables = (right, speed, reward, scale, sums, level, same)
    first, first_specs, scratch = (), [], [pltpu.VMEM((cols, cols), f32)]
    if ends:
        share = stretches * ends[0].shape[2]
        last = width // share - 1
        first = (mixed, *ends)
        first_specs = [
            pl.BlockSpec(
                (kinds, 1, 1, span, share),
                lambda c, e, w: (0, w[1] ^ prompt, c, 0, jnp.where(w[2] < 2, last, 0)),
            ),
            *map(fixed, ends),
        ]
        scratch.append(pltpu.VMEM((kinds, share, cols), bf16))
    return pl.pallas_call(
        functools.partial(wkv_kernel, prompt=prompt, parted=bool(ends)),
        grid_spec=pltpu.PrefetchScalarGridSpec(
            num_scalar_prefetch=2,
            grid=(stretches,),
            in_specs=first_specs
            + [
                pl.BlockSpec((kinds, 1, 1, span, cols), lambda c, e, w: (0, w[1] ^ prompt, c, 0, 0)),
                pl.BlockSpec((1, 1, span, inner), lambda c, e, w: (w[1] ^ prompt, c, 0, 0)),
            ]
            + [fixed(a) for a in tables],
            out_specs=pl.BlockSpec((1, span + ATTEND_DIM, cols), lambda c, e, w: (c, 0, 0)),
            scratch_shapes=scratch,
        ),
        out_shape=jax.ShapeDtypeStruct((stretches, span + ATTEND_DIM, cols), bf16),
        compiler_params=vmem(56),
        cost_estimate=SMALL,
    )(extents, where, *first, proj, lora, *tables)


def finish_kernel(where_ref, x_ref, own_ref, far_ref, *refs):
    weights, out_ref = refs[:5], refs[-1]
    stretches, rows, cols = own_ref.shape
    chunk = weights[0].shape[-1]
    for e in range(stretches):
        places = pl.ds(pl.multiple_of((where_ref[0] ^ e) * chunk, chunk), chunk)
        total = x_ref[:, places].astype(f32)
        for side, lines_ref in enumerate((own_ref, far_ref)):
            w_ref = weights[e].at[side, 0] if e < 3 else weights[e + side].at[0, 0]
            for d in range(stretches):
                at = pl.ds(pl.multiple_of((where_ref[0] ^ d) * cols, cols), cols)
                total += dot(lines_ref[d], w_ref[at, :])
        out_ref[0, :, places] = total.astype(bf16)


def finished(prompt, prompts, where, x, own, far, weights, earlier):
    stretches, _, cols = own.shape
    rows = x.shape[0] // prompts
    _, groups, depth, chunk = weights[0].shape
    share = groups * stretches * chunk
    if chunk % 128:
        order = jnp.arange(stretches) ^ where[0]
        total = lax.dynamic_slice(x, (prompt * rows, where[1] * share), (rows, share)).astype(f32)
        weights = [*weights[:3], jnp.concatenate(weights[3:])]
        for side, lines in enumerate((own, far)):
            w = jnp.stack([w[side] for w in weights])[order]
            w = jnp.transpose(w, (2, 1, 0, 3)).reshape(depth, share)
            lines = jnp.transpose(lines[order, :rows], (1, 0, 2)).reshape(rows, depth)
            total += dot(lines, w)
        return jnp.concatenate([*earlier, total.astype(bf16)[None]], axis=0)
    block = stretches * chunk
    lines_spec = pl.BlockSpec((stretches, rows, cols), lambda g, w: (0, 0, 0))
    return pl.pallas_call(
        finish_kernel,
        grid_spec=pltpu.PrefetchScalarGridSpec(
            num_scalar_prefetch=1,
            grid=(groups,),
            in_specs=[pl.BlockSpec((rows, block), lambda g, w: (prompt, w[1] * groups + g)), lines_spec, lines_spec]
            + [pl.BlockSpec((a.shape[0], 1, depth, chunk), lambda g, w: (0, g, 0, 0)) for a in weights]
            + [pl.BlockSpec(memory_space=pl.ANY)] * len(earlier),
            out_specs=pl.BlockSpec((1, rows, block), lambda g, w: (prompt, 0, g)),
        ),
        out_shape=jax.ShapeDtypeStruct((prompts, rows, share), bf16),
        input_output_aliases={9: 0} if earlier else {},
        compiler_params=vmem(48),
        cost_estimate=SMALL,
    )(where, x, own, far, *weights, *earlier)


def states_kernel(where_ref, blocks_ref, pick_ref, *refs):
    out_ref = refs[-1]
    stretches, _, cols = blocks_ref.shape
    heads = cols // ATTEND_DIM
    half = ATTEND_DIM // 2
    for b in range(stretches):
        lines = dot_nt(pick_ref[...], blocks_ref[where_ref[0] ^ b])
        for h in range(heads):
            at = 2 * h * half
            pairs = jnp.concatenate([lines[at : at + half], lines[at + half : at + 2 * half]], axis=1)
            head = b * heads + h
            for i in range(half):
                out_ref[0, 0, head : head + 1, 2 * i * ATTEND_DIM : 2 * (i + 1) * ATTEND_DIM] = pairs[i : i + 1]


def states_laid(prompt, prompts, where, blocks, earlier):
    stretches, lines, cols = blocks.shape
    heads = cols // ATTEND_DIM
    order = np.arange(cols).reshape(heads, ATTEND_DIM // 2, 2).transpose(0, 2, 1).reshape(-1)
    pick = jnp.asarray(order[:, None] == np.arange(cols)[None, :], bf16)
    shape = (1, 1, stretches * heads, ATTEND_DIM * ATTEND_DIM)
    return pl.pallas_call(
        states_kernel,
        grid_spec=pltpu.PrefetchScalarGridSpec(
            num_scalar_prefetch=1,
            grid=(1,),
            in_specs=[
                pl.BlockSpec((stretches, ATTEND_DIM, cols), lambda n, w: (0, lines // ATTEND_DIM - 1, 0)),
                pl.BlockSpec((cols, cols), lambda n, w: (0, 0)),
            ]
            + [pl.BlockSpec(memory_space=pl.ANY)] * len(earlier),
            out_specs=pl.BlockSpec(shape, lambda n, w: (prompt, 0, 0, 0)),
        ),
        out_shape=jax.ShapeDtypeStruct((prompts, *shape[1:]), f32),
        input_output_aliases={3: 0} if earlier else {},
        compiler_params=vmem(32),
        cost_estimate=SMALL,
    )(where, blocks, pick, *earlier)


def tied(*values):
    return lax.optimization_barrier(values)


def moved(value, axis, by):
    peers = lax.axis_size(axis)
    return lax.ppermute(value, axis, [(i, i + by) for i in range(peers) if 0 <= i + by < peers])


def local(
    incoming_activations,
    standardize_scaling,
    lagged_blending_weights,
    learner_line_permutation,
    learner_acceptor_lookup_slices,
    learner_projection_slices,
    fading_left_matrix,
    fading_right_matrix,
    feature_fading_speed,
    self_reward,
    cluster_scaling_vector,
    prompt_extents,
):
    reqs, span, width = incoming_activations.shape
    rows = reqs * span
    stretches = lax.axis_size("seq")
    cores = lax.axis_size("tensor")
    groups = lax.axis_size("req")
    assert reqs == cores == 2 and stretches == 4
    local_width = feature_fading_speed.shape[0]
    cols = local_width // stretches
    t, s = lax.axis_index("tensor"), lax.axis_index("seq")
    where = jnp.stack([s, t, lax.axis_index("req")]).astype(jnp.int32)

    x = incoming_activations.reshape(rows, width)
    own_x = lax.dynamic_slice_in_dim(x, t * span, span, 0)
    past = moved(own_x[span - PAST :], "seq", 1)
    out_half, shards = tied(learner_projection_slices.astype(bf16), learner_acceptor_lookup_slices)
    out_lines = lax.all_gather(out_half, "req", axis=0, tiled=False)
    pieces = [
        lax.dynamic_slice_in_dim(shards, (s ^ d) * cols, cols, 2).astype(bf16)
        for d in range(stretches)
    ]
    got = [swapped(pieces[d], "seq", d) for d in range(1, stretches)]

    own_x, past, *_ = tied(own_x, past, *pieces)
    coeffs = jnp.pad(lagged_blending_weights, ((0, PREFIX - 4), (0, 0)))
    act, coeffs = ordered(
        jnp.concatenate([past, own_x], axis=0),
        standardize_scaling.reshape(1, width),
        coeffs,
        learner_line_permutation.reshape(1, width),
    )
    act, perm, *got = tied(act, learner_line_permutation, *got)
    lines = jnp.stack([pieces[0], *got])
    chained = groups == 4

    def mixed_in(values, side, apart, earlier):
        return shifted(where, values, coeffs, left, side, apart, stretches, earlier)

    left = fading_left_matrix[perm]
    near, other = swapped(act, "seq", 1), swapped(act, "seq", 2)
    hops = [moved(lines, "req", 1), moved(lines, "req", -1)] if chained else [lax.all_gather(lines, "req", axis=0)]
    results = mixed_in(act, 0, 0, ())
    results = mixed_in(swapped(act, "tensor", 1), 1, 0, results)
    share = groups // cores
    def mine(array):
        return lax.dynamic_slice_in_dim(array, s * cols, cols, array.ndim - 1).reshape(-1, cols)

    tables = (fading_right_matrix, feature_fading_speed, self_reward, cluster_scaling_vector)
    out_lines, *rest = tied(out_lines, *results, *tables)
    results, tables = rest[:2], [mine(a) for a in rest[2:]]
    kept = lax.dynamic_slice_in_dim(out_lines, t * share, share, 0)
    given = lax.dynamic_slice_in_dim(out_lines, (1 - t) * share, share, 0)
    out_lines = jnp.stack([kept, swapped(given, "tensor", 1)])
    near, other, out_lines, *rest = tied(near, other, out_lines, *results, *tables, *hops)
    results, tables, hops = tuple(rest[:2]), rest[2:6], rest[6:]

    cut = (span + PAST) // 32 * 16
    across = [swapped(near[:cut], "seq", 2), swapped(other[cut:], "seq", 1)]
    if chained:
        hops += [moved(hops[0], "req", 1), moved(hops[1], "req", -1)]
    results = mixed_in(near, 0, 1, results)
    results = mixed_in(other, 0, 2, results)
    results = mixed_in(swapped(near, "tensor", 1), 1, 1, results)
    both = lax.all_gather(other, "tensor", axis=0)
    out_lines, *rest = tied(out_lines, *results, *across)
    results, across = tuple(rest[:2]), rest[2:]
    near, other = swapped(out_lines, "seq", 1), swapped(out_lines, "seq", 2)
    results = mixed_in(both, 1, 2, results)
    across = jnp.concatenate(across, axis=0)
    last = swapped(across, "tensor", 1)
    results = mixed_in(across, 0, 3, results)
    *results, = tied(*results, *hops)
    results, hops = tuple(results[:2]), results[2:]

    ends = [moved(hops[2], "req", 1), moved(hops[3], "req", -1)] if chained else []
    mixed, lora = mixed_in(last, 1, 3, results)
    if chained:
        proj = projected(where, mixed, [lines, *hops])
    else:
        proj = projected_whole(where, mixed, *hops)
    proj, near, other = tied(proj, near, other)
    across = [swapped(near[:1], "seq", 2), swapped(other[1:], "seq", 1)]
    if chained:
        ends = [ends[1], hops[3], hops[2], ends[0]]

    def one_prompt(prompt, proj):
        return recurrence(prompt, prompt_extents, where, mixed, proj, ends, lora, *tables)

    def exchanged(block):
        parts = [lax.dynamic_index_in_dim(block, s ^ d, 0, keepdims=False) for d in range(stretches)]
        return parts[:1] + [swapped(parts[d], "seq", d) for d in range(1, stretches)]

    def output(prompt, blocks, earlier):
        far_blocks = swapped(blocks, "tensor", 1)
        return finished(prompt, reqs, where, x, blocks, far_blocks, out_weights, earlier)

    block, proj = tied(one_prompt(0, proj), proj)
    first = exchanged(block)
    block, *rest = tied(one_prompt(1, proj), *first, *across)
    first, across = rest[:-2], rest[-2:]
    second = exchanged(block)
    first = jnp.stack(first)
    out_weights = [out_lines, near, other, *across]
    hidden_out = output(0, first, ())
    stretch_states = states_laid(0, reqs, where, first, ())
    hidden_out, stretch_states, *second = tied(hidden_out, stretch_states, *second)
    second = jnp.stack(second)
    hidden_out = output(1, second, (hidden_out,))
    stretch_states = states_laid(1, reqs, where, second, (stretch_states,))
    return (hidden_out, stretch_states)


def solution(mesh):
    in_specs = (
        P("req", "seq", None),
        P(),
        P(),
        P(),
        P(None, ("req", "seq"), "tensor"),
        P("tensor", ("req", "seq")),
        P(),
        P(None, "tensor"),
        P("tensor"),
        P("tensor"),
        P("tensor"),
        P("req"),
    )
    out_specs = (P("req", "seq", "tensor"), P("req", "seq", "tensor", None))
    return jax.shard_map(local, mesh=mesh, in_specs=in_specs, out_specs=out_specs, check_vma=False)
```

```python
import functools

import jax
import jax.numpy as jnp
import numpy as np
from jax import lax
from jax.experimental import pallas as pl
from jax.experimental.pallas import tpu as pltpu
from jax.sharding import PartitionSpec as P

ATTEND_DIM = 64
CHUNK = 64
LEVELS = 6
PREFIX = 8
PAST = 16

SMALL = pl.CostEstimate(flops=1024, bytes_accessed=1024, transcendentals=0)

eps = 1e-05
bf16 = jnp.bfloat16
f32 = jnp.float32


def dot(a, b):
    return jnp.dot(a, b, preferred_element_type=f32)


def dot_nt(a, b):
    return lax.dot_general(a, b, (((1,), (1,)), ((), ())), preferred_element_type=f32)


def dot_tn(a, b):
    return lax.dot_general(a, b, (((0,), (0,)), ((), ())), preferred_element_type=f32)


def swapped(value, axis, by):
    peers = lax.axis_size(axis)
    return lax.ppermute(value, axis, [(i, i ^ by) for i in range(peers)])


def vmem(mib):
    return pltpu.CompilerParams(vmem_limit_bytes=mib * 2**20)


def order_kernel(x_ref, gain_ref, coeff_ref, perm_ref, out_ref, coeff_out_ref, cur_ref):
    rows, width = x_ref.shape
    block = out_ref.shape[1]
    depth = 256

    @pl.when(pl.program_id(0) == 0)
    def _():
        x = x_ref[...].astype(f32)
        mean = jnp.mean(x, axis=-1, keepdims=True)
        centred = x - mean
        spread = jnp.mean(centred * centred, axis=-1, keepdims=True)
        cur_ref[:rows, :] = (centred * lax.rsqrt(spread + eps) * gain_ref[...]).astype(bf16)
        c = coeff_ref[...]
        high = c.astype(bf16)
        cur_ref[rows:, :] = jnp.concatenate([high, (c - high.astype(f32)).astype(bf16)], axis=0)

    perm = perm_ref[...]
    high, low = perm // depth, (perm % depth).astype(bf16)
    lines = lax.broadcasted_iota(jnp.int32, (depth, block), 0).astype(bf16)
    one, none = jnp.ones((depth, block), bf16), jnp.zeros((depth, block), bf16)
    total = jnp.zeros((rows + 2 * PREFIX, block), f32)
    for k in range(width // depth):
        mine = jnp.where(high == k, low, jnp.full_like(low, -1.0))
        total += dot(cur_ref[:, k * depth : (k + 1) * depth], jnp.where(lines == mine, one, none))
    out_ref[...] = total[:rows].astype(bf16)
    coeff_out_ref[...] = total[rows : rows + PREFIX] + total[rows + PREFIX :]


def ordered(x, gain, coeffs, perm):
    rows, width = x.shape
    block = 512
    return pl.pallas_call(
        order_kernel,
        grid=(width // block,),
        in_specs=[
            pl.BlockSpec((rows, width), lambda n: (0, 0)),
            pl.BlockSpec((1, width), lambda n: (0, 0)),
            pl.BlockSpec((PREFIX, width), lambda n: (0, 0)),
            pl.BlockSpec((1, block), lambda n: (0, n)),
        ],
        out_specs=[
            pl.BlockSpec((rows, block), lambda n: (0, n)),
            pl.BlockSpec((PREFIX, block), lambda n: (0, n)),
        ],
        out_shape=[
            jax.ShapeDtypeStruct((rows, width), bf16),
            jax.ShapeDtypeStruct((PREFIX, width), f32),
        ],
        scratch_shapes=[pltpu.VMEM((rows + 2 * PREFIX, width), bf16)],
        compiler_params=vmem(40),
        cost_estimate=SMALL,
    )(x, gain, coeffs, perm)


def mix_kernel(where_ref, act_ref, coeff_ref, left_ref, *refs):
    mixed_ref, lora_ref, inner_ref = refs[-3:]
    rows, block = mixed_ref.shape[-2:]
    width = 512
    n = pl.program_id(0)
    inner = jnp.zeros(inner_ref.shape, f32)
    for c in range(block // width):
        cols = slice(c * width, (c + 1) * width)
        cur = act_ref[PAST:, cols]
        delta = pltpu.roll(act_ref[:, cols].astype(f32), 1, 0)[PAST:].astype(bf16) - cur
        for j in range(3):
            mixed_ref[j, 0, 0, :, cols] = cur + delta * coeff_ref[j : j + 1, cols].astype(bf16)
        inner += dot(cur + delta * coeff_ref[3:4, cols].astype(bf16), left_ref[cols, :])

    @pl.when(n == 0)
    def _():
        inner_ref[...] = inner

    @pl.when(n > 0)
    def _():
        inner_ref[...] += inner

    @pl.when(n == pl.num_programs(0) - 1)
    def _():
        lora_ref[0, 0] = jnp.tanh(inner_ref[...]).astype(bf16)


def shifted(where, act, coeffs, left, side, apart, stretches, earlier):
    span, width = act.shape[-2] - PAST, act.shape[-1]
    inner = left.shape[1]
    block = 512
    act_spec = pl.BlockSpec((span + PAST, block), lambda n, w: (0, n))
    if act.ndim == 3:
        act_spec = pl.BlockSpec((None, span + PAST, block), lambda n, w: (1 - w[1], 0, n))
    kept = pl.BlockSpec(memory_space=pl.ANY)
    return pl.pallas_call(
        mix_kernel,
        grid_spec=pltpu.PrefetchScalarGridSpec(
            num_scalar_prefetch=1,
            grid=(width // block,),
            in_specs=[
                act_spec,
                pl.BlockSpec((PREFIX, block), lambda n, w: (0, n)),
                pl.BlockSpec((block, inner), lambda n, w: (n, 0)),
            ]
            + [kept] * len(earlier),
            out_specs=[
                pl.BlockSpec((3, 1, 1, span, block), lambda n, w: (0, side, w[0] ^ apart, 0, n)),
                pl.BlockSpec((1, 1, span, inner), lambda n, w: (side, w[0] ^ apart, 0, 0)),
            ],
            scratch_shapes=[pltpu.VMEM((span, inner), f32)],
        ),
        out_shape=[
            jax.ShapeDtypeStruct((3, 2, stretches, span, width), bf16),
            jax.ShapeDtypeStruct((2, stretches, span, inner), bf16),
        ],
        input_output_aliases={4: 0, 5: 1} if earlier else {},
        compiler_params=vmem(32),
        cost_estimate=SMALL,
    )(where, act, coeffs, left, *earlier)


def project_kernel(where_ref, *refs):
    *refs, out_ref, lines_ref = refs
    parts = where_ref[2] // 2
    acts, hops = refs[:3], refs[3:]
    stretches, _, depth, _ = hops[0].shape
    share = stretches * depth

    def place(r, ref):
        slot = r - parts

        @pl.when((slot >= 0) & (slot < len(acts)))
        def _():
            for d in range(stretches):
                at = slot * share + (where_ref[0] ^ d) * depth
                lines_ref[pl.ds(pl.multiple_of(at, depth), depth), :] = ref[d, 0]

    @pl.when(pl.program_id(1) == 0)
    def _():
        place(where_ref[2], hops[0])
        for hop in range(1, len(hops) // 2 + 1):
            place(where_ref[2] - hop, hops[2 * hop - 1])
            place(where_ref[2] + hop, hops[2 * hop])

    total = None
    for i, act_ref in enumerate(acts):
        found = dot(act_ref[0, 0].reshape(-1, share), lines_ref[i * share : (i + 1) * share, :])
        total = found if total is None else total + found
    out_ref[0, 0] = total.reshape(out_ref.shape[2:])


def projected(where, mixed, hops):
    stretches, kinds, depth, cols = hops[0].shape
    _, sides, _, span, width = mixed.shape
    share = stretches * depth
    parts = width // share - 1

    def act_spec(i):
        return pl.BlockSpec((1, 1, stretches, span, share), lambda j, m, w: (j, m, 0, 0, w[2] // 2 + i))

    return pl.pallas_call(
        project_kernel,
        grid_spec=pltpu.PrefetchScalarGridSpec(
            num_scalar_prefetch=1,
            grid=(kinds, sides),
            in_specs=[act_spec(i) for i in range(parts)]
            + [pl.BlockSpec((stretches, 1, depth, cols), lambda j, m, w: (0, j, 0, 0))] * len(hops),
            out_specs=pl.BlockSpec((1, 1, stretches, span, cols), lambda j, m, w: (j, m, 0, 0, 0)),
            scratch_shapes=[pltpu.VMEM((parts * share, cols), bf16)],
        ),
        out_shape=jax.ShapeDtypeStruct((kinds, sides, stretches, span, cols), f32),
        compiler_params=vmem(60),
        cost_estimate=SMALL,
    )(where, *[mixed] * parts, *hops)


def projected_whole(where, mixed, lines):
    _, stretches, kinds, depth, cols = lines.shape
    lines = lines[:, jnp.arange(stretches) ^ where[0]]
    lines = jnp.transpose(lines, (2, 0, 1, 3, 4)).reshape(kinds, mixed.shape[-1], cols)
    return jnp.einsum("jxbtk,jkc->jxbtc", mixed, lines, preferred_element_type=f32).astype(bf16)


def decay_sums():
    place = np.arange(CHUNK)
    of, by = place[:, None], place[None, :]
    parts = []
    for level in range(1, LEVELS):
        half = 1 << level
        middle = (of // (2 * half)) * 2 * half + half - 1
        later = (of % (2 * half)) >= half
        parts.append(np.where(later, (by > middle) & (by < of), (by > of) & (by <= middle)))
    parts += [by < of, by > of, np.ones((8, CHUNK), bool)]
    sums = np.concatenate(parts).astype(np.float32)
    return np.concatenate([sums, sums], axis=1)


def pair_levels(heads):
    of, by = np.arange(CHUNK)[:, None], np.arange(CHUNK)[None, :]
    level = np.full((CHUNK, CHUNK), -1.0, np.float32)
    for bit in range(LEVELS):
        level[((of ^ by) >> bit) == 1] = bit
    return np.tile(np.where(of > by, level, -1.0).astype(np.float32), (1, heads))


def wkv_kernel(extent_ref, where_ref, *refs, prompt, parted):
    if parted:
        act_ref, *last_refs = refs[:5]
        *refs, lines_ref = refs[5:]
    proj_ref, lora_ref, right_ref, speed_ref, reward_ref, scale_ref, sums_ref, level_ref, same_ref, *refs = refs
    out_ref, memory_ref = refs
    step = pl.program_id(0)
    tokens, cols = proj_ref.shape[3:]
    heads = cols // ATTEND_DIM
    same = same_ref[...]
    same_f32 = same.astype(f32)
    level = level_ref[...]

    @pl.when(step == 0)
    def _():
        memory_ref[...] = jnp.zeros_like(memory_ref)
        if parted:
            for r, last_ref in enumerate(last_refs):

                @pl.when(where_ref[2] == r)
                def _():
                    stretches, kinds, depth, _ = last_ref.shape
                    for d in range(stretches):
                        at = pl.ds(pl.multiple_of((where_ref[0] ^ d) * depth, depth), depth)
                        for j in range(kinds):
                            lines_ref[j, at, :] = last_ref[d, j]

    def projection(j):
        if not parted:
            return proj_ref[j, 0, 0]
        return (proj_ref[j, 0, 0] + dot(act_ref[j, 0, 0], lines_ref[j])).astype(bf16)

    at = step * tokens + lax.broadcasted_iota(jnp.int32, (tokens, cols), 0)
    valid = jnp.where(at < extent_ref[prompt], 1.0, 0.0)
    r = projection(0)
    k = projection(1) * valid.astype(bf16)
    v = projection(2)
    decay = -speed_ref[...] * jnp.exp(dot(lora_ref[0, 0], right_ref[...])) * valid
    high = decay.astype(bf16)
    low = (decay - high.astype(f32)).astype(bf16)
    own = dot((r.astype(f32) * reward_ref[...] * k.astype(f32)).astype(bf16), same) * v.astype(f32)

    subs = [slice(at, at + CHUNK) for at in range(0, tokens, CHUNK)]
    both = jnp.concatenate([jnp.concatenate([part[lines] for lines in subs], axis=1) for part in (high, low)], axis=0)
    all_kept = jnp.exp(dot(sums_ref[...], both))
    memory = memory_ref[...]
    rows = []
    for sub, lines in enumerate(subs):
        r_sub, k_sub, v_sub = r[lines], k[lines], v[lines]
        kept = all_kept[:, sub * cols : (sub + 1) * cols]
        scores = jnp.zeros((CHUNK, heads * CHUNK), f32)
        for bit in range(LEVELS):
            query, lookup = r_sub, k_sub
            if bit:
                part = kept[(bit - 1) * CHUNK : bit * CHUNK].astype(bf16)
                query, lookup = query * part, lookup * part
            lookup = jnp.concatenate([lookup] * heads, axis=0) * same
            scores = jnp.where(level == bit, dot_nt(query, lookup), scores)
        v_heads = jnp.concatenate([v_sub] * heads, axis=0) * same
        after = (LEVELS - 1) * CHUNK
        from_start = r_sub * kept[after : after + CHUNK].astype(bf16)
        to_end = k_sub * kept[after + CHUNK : after + 2 * CHUNK].astype(bf16)
        whole = kept[after + 2 * CHUNK : after + 2 * CHUNK + 1]
        rows.append(dot_nt(from_start, memory.astype(bf16)) + dot(scores.astype(bf16), v_heads))
        memory = memory * whole + same_f32 * dot_tn(v_sub, to_end)
    memory_ref[...] = memory
    folded = memory[:ATTEND_DIM]
    for h in range(1, heads):
        folded += memory[h * ATTEND_DIM : (h + 1) * ATTEND_DIM]
    out_ref[0, tokens:] = folded.astype(bf16)

    y = jnp.concatenate(rows, axis=0) + own
    y_high = y.astype(bf16)
    y_low = (y - y_high.astype(f32)).astype(bf16)
    centred = y - (dot(y_high, same) + dot(y_low, same)) * (1.0 / ATTEND_DIM)
    spread = dot((centred * centred).astype(bf16), same) * (1.0 / ATTEND_DIM)
    out_ref[0, :tokens] = (centred * lax.rsqrt(spread + eps) * scale_ref[...] * valid).astype(bf16)


def recurrence(prompt, extents, where, mixed, proj, ends, lora, right, speed, reward, scale):
    kinds, _, stretches, span, cols = proj.shape
    width = mixed.shape[-1]
    inner = lora.shape[-1]
    heads = cols // ATTEND_DIM
    sums = jnp.asarray(decay_sums(), bf16)
    level = jnp.asarray(pair_levels(heads), f32)
    head = np.arange(cols) // ATTEND_DIM
    same = jnp.asarray(head[:, None] == head[None, :], bf16)

    def fixed(array):
        return pl.BlockSpec(array.shape, lambda c, e, w: (0,) * array.ndim)

    tables = (right, speed, reward, scale, sums, level, same)
    first, first_specs, scratch = (), [], [pltpu.VMEM((cols, cols), f32)]
    if ends:
        share = stretches * ends[0].shape[2]
        last = width // share - 1
        first = (mixed, *ends)
        first_specs = [
            pl.BlockSpec(
                (kinds, 1, 1, span, share),
                lambda c, e, w: (0, w[1] ^ prompt, c, 0, jnp.where(w[2] < 2, last, 0)),
            ),
            *map(fixed, ends),
        ]
        scratch.append(pltpu.VMEM((kinds, share, cols), bf16))
    return pl.pallas_call(
        functools.partial(wkv_kernel, prompt=prompt, parted=bool(ends)),
        grid_spec=pltpu.PrefetchScalarGridSpec(
            num_scalar_prefetch=2,
            grid=(stretches,),
            in_specs=first_specs
            + [
                pl.BlockSpec((kinds, 1, 1, span, cols), lambda c, e, w: (0, w[1] ^ prompt, c, 0, 0)),
                pl.BlockSpec((1, 1, span, inner), lambda c, e, w: (w[1] ^ prompt, c, 0, 0)),
            ]
            + [fixed(a) for a in tables],
            out_specs=pl.BlockSpec((1, span + ATTEND_DIM, cols), lambda c, e, w: (c, 0, 0)),
            scratch_shapes=scratch,
        ),
        out_shape=jax.ShapeDtypeStruct((stretches, span + ATTEND_DIM, cols), bf16),
        compiler_params=vmem(56),
        cost_estimate=SMALL,
    )(extents, where, *first, proj, lora, *tables)


def finish_kernel(where_ref, x_ref, own_ref, far_ref, *refs):
    weights, out_ref = refs[:5], refs[-1]
    stretches, rows, cols = own_ref.shape
    chunk = weights[0].shape[-1]
    for e in range(stretches):
        places = pl.ds(pl.multiple_of((where_ref[0] ^ e) * chunk, chunk), chunk)
        total = x_ref[:, places].astype(f32)
        for side, lines_ref in enumerate((own_ref, far_ref)):
            w_ref = weights[e].at[side, 0] if e < 3 else weights[e + side].at[0, 0]
            for d in range(stretches):
                at = pl.ds(pl.multiple_of((where_ref[0] ^ d) * cols, cols), cols)
                total += dot(lines_ref[d], w_ref[at, :])
        out_ref[0, :, places] = total.astype(bf16)


def finished(prompt, prompts, where, x, own, far, weights, earlier):
    stretches, _, cols = own.shape
    rows = x.shape[0] // prompts
    _, groups, depth, chunk = weights[0].shape
    share = groups * stretches * chunk
    if chunk % 128:
        order = jnp.arange(stretches) ^ where[0]
        total = lax.dynamic_slice(x, (prompt * rows, where[1] * share), (rows, share)).astype(f32)
        weights = [*weights[:3], jnp.concatenate(weights[3:])]
        for side, lines in enumerate((own, far)):
            w = jnp.stack([w[side] for w in weights])[order]
            w = jnp.transpose(w, (2, 1, 0, 3)).reshape(depth, share)
            lines = jnp.transpose(lines[order, :rows], (1, 0, 2)).reshape(rows, depth)
            total += dot(lines, w)
        return jnp.concatenate([*earlier, total.astype(bf16)[None]], axis=0)
    block = stretches * chunk
    lines_spec = pl.BlockSpec((stretches, rows, cols), lambda g, w: (0, 0, 0))
    return pl.pallas_call(
        finish_kernel,
        grid_spec=pltpu.PrefetchScalarGridSpec(
            num_scalar_prefetch=1,
            grid=(groups,),
            in_specs=[pl.BlockSpec((rows, block), lambda g, w: (prompt, w[1] * groups + g)), lines_spec, lines_spec]
            + [pl.BlockSpec((a.shape[0], 1, depth, chunk), lambda g, w: (0, g, 0, 0)) for a in weights]
            + [pl.BlockSpec(memory_space=pl.ANY)] * len(earlier),
            out_specs=pl.BlockSpec((1, rows, block), lambda g, w: (prompt, 0, g)),
        ),
        out_shape=jax.ShapeDtypeStruct((prompts, rows, share), bf16),
        input_output_aliases={9: 0} if earlier else {},
        compiler_params=vmem(48),
        cost_estimate=SMALL,
    )(where, x, own, far, *weights, *earlier)


def states_kernel(where_ref, blocks_ref, pick_ref, *refs):
    out_ref = refs[-1]
    stretches, _, cols = blocks_ref.shape
    heads = cols // ATTEND_DIM
    half = ATTEND_DIM // 2
    for b in range(stretches):
        lines = dot_nt(pick_ref[...], blocks_ref[where_ref[0] ^ b])
        for h in range(heads):
            at = 2 * h * half
            pairs = jnp.concatenate([lines[at : at + half], lines[at + half : at + 2 * half]], axis=1)
            head = b * heads + h
            for i in range(half):
                out_ref[0, 0, head : head + 1, 2 * i * ATTEND_DIM : 2 * (i + 1) * ATTEND_DIM] = pairs[i : i + 1]


def states_laid(prompt, prompts, where, blocks, earlier):
    stretches, lines, cols = blocks.shape
    heads = cols // ATTEND_DIM
    order = np.arange(cols).reshape(heads, ATTEND_DIM // 2, 2).transpose(0, 2, 1).reshape(-1)
    pick = jnp.asarray(order[:, None] == np.arange(cols)[None, :], bf16)
    shape = (1, 1, stretches * heads, ATTEND_DIM * ATTEND_DIM)
    return pl.pallas_call(
        states_kernel,
        grid_spec=pltpu.PrefetchScalarGridSpec(
            num_scalar_prefetch=1,
            grid=(1,),
            in_specs=[
                pl.BlockSpec((stretches, ATTEND_DIM, cols), lambda n, w: (0, lines // ATTEND_DIM - 1, 0)),
                pl.BlockSpec((cols, cols), lambda n, w: (0, 0)),
            ]
            + [pl.BlockSpec(memory_space=pl.ANY)] * len(earlier),
            out_specs=pl.BlockSpec(shape, lambda n, w: (prompt, 0, 0, 0)),
        ),
        out_shape=jax.ShapeDtypeStruct((prompts, *shape[1:]), f32),
        input_output_aliases={3: 0} if earlier else {},
        compiler_params=vmem(32),
        cost_estimate=SMALL,
    )(where, blocks, pick, *earlier)


def tied(*values):
    return lax.optimization_barrier(values)


def moved(value, axis, by):
    peers = lax.axis_size(axis)
    return lax.ppermute(value, axis, [(i, i + by) for i in range(peers) if 0 <= i + by < peers])


def local(
    incoming_activations,
    standardize_scaling,
    lagged_blending_weights,
    learner_line_permutation,
    learner_acceptor_lookup_slices,
    learner_projection_slices,
    fading_left_matrix,
    fading_right_matrix,
    feature_fading_speed,
    self_reward,
    cluster_scaling_vector,
    prompt_extents,
):
    reqs, span, width = incoming_activations.shape
    rows = reqs * span
    stretches = lax.axis_size("seq")
    cores = lax.axis_size("tensor")
    groups = lax.axis_size("req")
    assert reqs == cores == 2 and stretches == 4
    local_width = feature_fading_speed.shape[0]
    cols = local_width // stretches
    t, s = lax.axis_index("tensor"), lax.axis_index("seq")
    where = jnp.stack([s, t, lax.axis_index("req")]).astype(jnp.int32)

    x = incoming_activations.reshape(rows, width)
    own_x = lax.dynamic_slice_in_dim(x, t * span, span, 0)
    past = moved(own_x[span - PAST :], "seq", 1)
    out_half, shards = tied(learner_projection_slices.astype(bf16), learner_acceptor_lookup_slices)
    out_lines = lax.all_gather(out_half, "req", axis=0, tiled=False)
    pieces = [
        lax.dynamic_slice_in_dim(shards, (s ^ d) * cols, cols, 2).astype(bf16)
        for d in range(stretches)
    ]
    got = [swapped(pieces[d], "seq", d) for d in range(1, stretches)]

    own_x, past, *_ = tied(own_x, past, *pieces)
    coeffs = jnp.pad(lagged_blending_weights, ((0, PREFIX - 4), (0, 0)))
    act, coeffs = ordered(
        jnp.concatenate([past, own_x], axis=0),
        standardize_scaling.reshape(1, width),
        coeffs,
        learner_line_permutation.reshape(1, width),
    )
    act, perm, *got = tied(act, learner_line_permutation, *got)
    lines = jnp.stack([pieces[0], *got])
    chained = groups == 4

    def mixed_in(values, side, apart, earlier):
        return shifted(where, values, coeffs, left, side, apart, stretches, earlier)

    left = fading_left_matrix[perm]
    near, other = swapped(act, "seq", 1), swapped(act, "seq", 2)
    hops = [moved(lines, "req", 1), moved(lines, "req", -1)] if chained else [lax.all_gather(lines, "req", axis=0)]
    results = mixed_in(act, 0, 0, ())
    results = mixed_in(swapped(act, "tensor", 1), 1, 0, results)
    share = groups // cores
    def mine(array):
        return lax.dynamic_slice_in_dim(array, s * cols, cols, array.ndim - 1).reshape(-1, cols)

    tables = (fading_right_matrix, feature_fading_speed, self_reward, cluster_scaling_vector)
    out_lines, *rest = tied(out_lines, *results, *tables)
    results, tables = rest[:2], [mine(a) for a in rest[2:]]
    kept = lax.dynamic_slice_in_dim(out_lines, t * share, share, 0)
    given = lax.dynamic_slice_in_dim(out_lines, (1 - t) * share, share, 0)
    out_lines = jnp.stack([kept, swapped(given, "tensor", 1)])
    near, other, out_lines, *rest = tied(near, other, out_lines, *results, *tables, *hops)
    results, tables, hops = tuple(rest[:2]), rest[2:6], rest[6:]

    cut = (span + PAST) // 32 * 16
    across = [swapped(near[:cut], "seq", 2), swapped(other[cut:], "seq", 1)]
    if chained:
        hops += [moved(hops[0], "req", 1), moved(hops[1], "req", -1)]
    results = mixed_in(near, 0, 1, results)
    results = mixed_in(other, 0, 2, results)
    results = mixed_in(swapped(near, "tensor", 1), 1, 1, results)
    both = lax.all_gather(other, "tensor", axis=0)
    out_lines, *rest = tied(out_lines, *results, *across)
    results, across = tuple(rest[:2]), rest[2:]
    near, other = swapped(out_lines, "seq", 1), swapped(out_lines, "seq", 2)
    results = mixed_in(both, 1, 2, results)
    across = jnp.concatenate(across, axis=0)
    last = swapped(across, "tensor", 1)
    results = mixed_in(across, 0, 3, results)
    *results, = tied(*results, *hops)
    results, hops = tuple(results[:2]), results[2:]

    ends = [moved(hops[2], "req", 1), moved(hops[3], "req", -1)] if chained else []
    mixed, lora = mixed_in(last, 1, 3, results)
    if chained:
        proj = projected(where, mixed, [lines, *hops])
    else:
        proj = projected_whole(where, mixed, *hops)
    proj, near, other = tied(proj, near, other)
    across = [swapped(near[:1], "seq", 2), swapped(other[1:], "seq", 1)]
    if chained:
        ends = [ends[1], hops[3], hops[2], ends[0]]

    def one_prompt(prompt, proj):
        return recurrence(prompt, prompt_extents, where, mixed, proj, ends, lora, *tables)

    def exchanged(block):
        parts = [lax.dynamic_index_in_dim(block, s ^ d, 0, keepdims=False) for d in range(stretches)]
        return parts[:1] + [swapped(parts[d], "seq", d) for d in range(1, stretches)]

    def output(prompt, blocks, earlier):
        far_blocks = swapped(blocks, "tensor", 1)
        return finished(prompt, reqs, where, x, blocks, far_blocks, out_weights, earlier)

    block, proj = tied(one_prompt(0, proj), proj)
    first = exchanged(block)
    block, *rest = tied(one_prompt(1, proj), *first, *across)
    first, across = rest[:-2], rest[-2:]
    second = exchanged(block)
    first = jnp.stack(first)
    out_weights = [out_lines, near, other, *across]
    hidden_out = output(0, first, ())
    stretch_states = states_laid(0, reqs, where, first, ())
    hidden_out, stretch_states, *second = tied(hidden_out, stretch_states, *second)
    second = jnp.stack(second)
    hidden_out = output(1, second, (hidden_out,))
    stretch_states = states_laid(1, reqs, where, second, (stretch_states,))
    return (hidden_out, stretch_states)


def solution(mesh):
    in_specs = (
        P("req", "seq", None),
        P(),
        P(),
        P(),
        P(None, ("req", "seq"), "tensor"),
        P("tensor", ("req", "seq")),
        P(),
        P(None, "tensor"),
        P("tensor"),
        P("tensor"),
        P("tensor"),
        P("req"),
    )
    out_specs = (P("req", "seq", "tensor"), P("req", "seq", "tensor", None))
    return jax.shard_map(local, mesh=mesh, in_specs=in_specs, out_specs=out_specs, check_vma=False)
```
